32 devices in a mesh: dp: 8 (over z, y), heads: 4 (over x, core).
Axes of the slice: x: 2, y: 2, z: 4, core: 2. Of those that a mesh axis runs over, the one named last changes fastest.
Arguments:
- inputs: bfloat16 [8, 4096, 768], P('dp', 'heads'), may hold values from -6 to 6
- doc_lengths: int32 [8], P('dp'), may hold values from 3073 to 4096, as said below
- random_blocks: int32 [8, 64, 3], P('dp'), may hold values from 0 to 63
- qkv_weight: bfloat16 [768, 2304], replicated, may hold values from -0.21875 to 0.21875
- query_bias: bfloat16 [768], replicated, may hold values from -3 to 3
- value_bias: bfloat16 [768], replicated, may hold values from -0.1796875 to 0.1796875
- proj_weight: bfloat16 [768, 768], replicated, may hold values from -2.5 to 2.5
- proj_bias: bfloat16 [768], replicated, may hold values from -3 to 3
- first_gain: bfloat16 [768], replicated, may hold values from 0.099609375 to 1.8984375
- first_shift: bfloat16 [768], replicated, may hold values from -3 to 3
- expand_weight: bfloat16 [768, 3072], replicated, may hold values from -0.21875 to 0.21875
- expand_bias: bfloat16 [3072], replicated, may hold values from -3 to 3
- shrink_weight: bfloat16 [3072, 768], replicated, may hold values from -0.109375 to 0.109375
- shrink_bias: bfloat16 [768], replicated, may hold values from -3 to 3
- second_gain: bfloat16 [768], replicated, may hold values from 0.099609375 to 1.8984375
- second_shift: bfloat16 [768], replicated, may hold values from -3 to 3
- cotangent: bfloat16 [8, 4096, 768], P('dp', 'heads'), may hold values from -6 to 6
Outputs:
- output: bfloat16 [8, 4096, 768], P('dp', 'heads')
- input_grad: float32 [8, 4096, 768], P('dp', 'heads')
- grad_qkv_weight: float32 [768, 2304], replicated
- grad_query_bias: float32 [768], replicated
- grad_value_bias: float32 [768], replicated
- grad_proj_weight: float32 [768, 768], replicated
- grad_proj_bias: float32 [768], replicated
- grad_first_gain: float32 [768], replicated
- grad_first_shift: float32 [768], replicated
- grad_expand_weight: float32 [768, 3072], replicated
- grad_expand_bias: float32 [3072], replicated
- grad_shrink_weight: float32 [3072, 768], replicated
- grad_shrink_bias: float32 [768], replicated
- grad_second_gain: float32 [768], replicated
- grad_second_shift: float32 [768], replicated
The draws below stay inside these ranges and needn't reach their ends.
Inputs may be any that keep to these rules, and one draw needn't show every extreme that they name: `doc_lengths`: one document fills all 4096 slots and one has exactly the least length.
All inputs are finite; a program needn't handle non-finite values.
Results may differ from the reference program's by a relative error of at most 0.015.
Values may be sent and summed in bfloat16 or wider, within the bound.
No kernel may reach another device: no remote copies, remote signals or barrier semaphores. Data moves between devices by JAX's collectives and lax.ppermute only.
A program may use at most 320 MiB of HBM per device.

```python
import jax
import jax.numpy as jnp
from jax import lax

D = 768
HEADS = 12
HEAD_DIM = 64
FF = 3072
BLOCK = 64
LEN = 4096
DOCS = 8
NB = 64
N_HEADS = 4


def draw_doc_lengths(key, part):
    least = LEN - LEN // N_HEADS + 1
    lengths = jax.random.randint(key, (DOCS,), least, LEN + 1, dtype=jnp.int32)
    lengths = lengths.at[0].set(LEN)
    return lengths.at[1].set(least)


def plant(array, stream_key, low, high):
    shape = array.shape
    index_at = [jax.random.randint(jax.random.fold_in(stream_key, axis), (), 0, shape[axis]) for axis in range(len(shape))]
    array = array.at[tuple(index_at)].set(low)
    longest = shape.index(max(shape))
    index_at[longest] = (index_at[longest] + 1) % shape[longest]
    return array.at[tuple(index_at)].set(high)


def block_levels(key, dims, cuts, smallest, largest):
    factor_of, own = 1.0, jax.random.fold_in(key, 6)
    for dim, parts in cuts:
        draws = jnp.exp(jax.random.uniform(jax.random.fold_in(own, dim), (parts,), jnp.float32, smallest / len(cuts), largest / len(cuts)))
        factor_of = factor_of * jnp.repeat(draws, dims[dim] // parts).reshape([-1 if axis == dim else 1 for axis in range(len(dims))])
    return factor_of


def bell_draw(stream_key, shape, deviation, bound, cuts=(), held_as=jnp.bfloat16):
    drawn = jax.random.normal(stream_key, shape, jnp.float32) * deviation
    if len(cuts) > 0:
        drawn = block_levels(stream_key, shape, cuts, -0.22, 0.18) * drawn
    return jnp.clip(drawn, min=-bound, max=bound).astype(held_as)


def setup_inputs(seed: int = 0) -> dict:
    arg_keys = jax.random.split(jax.random.key(seed), 18)
    return {
        "inputs": bell_draw(arg_keys[0], (DOCS, LEN, D), 1.0, 6.0, ((0, 8), (1, 4))),
        "doc_lengths": draw_doc_lengths(jax.random.fold_in(arg_keys[17], 71), 0),
        "random_blocks": plant(jax.random.randint(arg_keys[2], (DOCS, NB, 3), 0, NB), jax.random.fold_in(arg_keys[2], 1), 0, NB - 1).astype(jnp.int32),
        "qkv_weight": bell_draw(arg_keys[3], (D, 3 * D), D ** -0.5, 0.21875),
        "query_bias": bell_draw(arg_keys[4], (D,), 0.5, 3.0),
        "value_bias": bell_draw(arg_keys[5], (D,), 0.03, 0.1796875),
        "proj_weight": bell_draw(arg_keys[6], (D, D), (max(D // 128, 1)) ** -0.5, 2.5),
        "proj_bias": bell_draw(arg_keys[7], (D,), 0.5, 3.0),
        "first_gain": jnp.clip(1.0 + 0.18 * jax.random.normal(arg_keys[8], (D,), jnp.float32), 0.099609375, 1.8984375).astype(jnp.bfloat16),
        "first_shift": bell_draw(arg_keys[9], (D,), 0.5, 3.0),
        "expand_weight": bell_draw(arg_keys[10], (D, FF), D ** -0.5, 0.21875),
        "expand_bias": bell_draw(arg_keys[11], (FF,), 0.5, 3.0),
        "shrink_weight": bell_draw(arg_keys[12], (FF, D), FF ** -0.5, 0.109375),
        "shrink_bias": bell_draw(arg_keys[13], (D,), 0.5, 3.0),
        "second_gain": jnp.clip(1.0 + 0.18 * jax.random.normal(arg_keys[14], (D,), jnp.float32), 0.099609375, 1.8984375).astype(jnp.bfloat16),
        "second_shift": bell_draw(arg_keys[15], (D,), 0.5, 3.0),
        "cotangent": bell_draw(arg_keys[16], (DOCS, LEN, D), 1.0, 6.0, ((0, 8), (1, 4))),
    }


@jax.custom_vjp
def low(v):
    return lax.optimization_barrier(v.astype(jnp.bfloat16)).astype(jnp.float32)

@jax.custom_vjp
def low_back(v):
    return v

def low_keep(v):
    return (low(v), None)

def low_pass(kept, grad):
    return (grad,)

def back_keep(v):
    return (v, None)

def back_low(kept, grad):
    return (low(grad),)
low.defvjp(low_keep, low_pass)
low_back.defvjp(back_keep, back_low)
norm_epsilon = 1e-12
masked_score = -1e+30

def layer_norm(values, scaling, offset):
    center = values - lax.optimization_barrier(jnp.mean(values, axis=-1, keepdims=True))
    spread = lax.optimization_barrier(jnp.mean(center * center, axis=-1, keepdims=True))
    return center * lax.rsqrt(spread + norm_epsilon) * scaling + offset

def token_mask(length, randoms):
    blocks = LEN // BLOCK
    block_count = (length + BLOCK - 1) // BLOCK
    places = jnp.arange(blocks, dtype=jnp.int32)
    row_block = places[:, None]
    col_block = places[None, :]
    allowed = jnp.abs(row_block - col_block) <= 1
    allowed = allowed | (row_block == 0) | (row_block == block_count - 1)
    allowed = allowed | (col_block == 0) | (col_block == block_count - 1)
    allowed = allowed | jnp.any(randoms[:, :, None] == places[None, None, :], axis=1)
    expanded = jnp.repeat(jnp.repeat(allowed, BLOCK, axis=0), BLOCK, axis=1)
    return expanded & (jnp.arange(LEN, dtype=jnp.int32) < length)[None, :]

def reference(inputs, doc_lengths, random_blocks, qkv_weight, query_bias, value_bias, proj_weight, proj_bias, first_gain, first_shift, expand_weight, expand_bias, shrink_weight, shrink_bias, second_gain, second_shift, cotangent):
    doc_count = doc_lengths.shape[0]
    highest = lax.Precision.HIGHEST

    def attend(items):
        queries, keys, values, length, randoms = items
        allowed = token_mask(length, randoms)

        def one_head(head_items):
            query_head, key_head, value_head = head_items
            raw = jnp.dot(query_head, key_head.T, precision=highest) * HEAD_DIM ** (-0.5)
            scores = jnp.where(allowed, low_back(raw), masked_score)
            shares = jax.nn.softmax(scores, axis=-1)
            return jnp.dot(low(shares), value_head, precision=highest)
        per_head = lax.map(jax.checkpoint(one_head), (queries.transpose(1, 0, 2), keys.transpose(1, 0, 2), values.transpose(1, 0, 2)))
        return per_head.transpose(1, 0, 2)

    def forward(source, w_joined, bias_query, bias_value, w_proj, bias_proj, gain_first, offset_first, w_expand, bias_expand, w_shrink, bias_shrink, gain_second, offset_second):
        rows = source.reshape(-1, D)
        joined = jnp.dot(rows, w_joined, precision=highest)
        queries = low_back(low(joined[:, :D] + bias_query))
        keys = low_back(low(joined[:, D:2 * D]))
        values = low_back(low(joined[:, 2 * D:] + bias_value))
        shape_four = (doc_count, LEN, HEADS, HEAD_DIM)
        context = lax.map(jax.checkpoint(attend), (queries.reshape(shape_four), keys.reshape(shape_four), values.reshape(shape_four), doc_lengths, random_blocks))
        context = low_back(low(context.reshape(-1, D)))
        branch = low_back(jnp.dot(context, w_proj, precision=highest) + bias_proj)
        hidden = layer_norm(rows + branch, gain_first, offset_first)
        inner = low_back(jnp.dot(low(hidden), w_expand, precision=highest) + bias_expand)
        active = low(jax.nn.gelu(inner, approximate=False))
        branch_two = low_back(jnp.dot(active, w_shrink, precision=highest) + bias_shrink)
        result = layer_norm(hidden + branch_two, gain_second, offset_second)
        return result.reshape(doc_count, LEN, D)
    floats = [member.astype(jnp.float32) for member in (inputs, qkv_weight, query_bias, value_bias, proj_weight, proj_bias, first_gain, first_shift, expand_weight, expand_bias, shrink_weight, shrink_bias, second_gain, second_shift)]
    output, pull_back = jax.vjp(forward, *floats)
    grads = pull_back(cotangent.astype(jnp.float32))
    return (output.astype(jnp.bfloat16), grads[0], grads[1], grads[2], grads[3], grads[4], grads[5], grads[6], grads[7], grads[8], grads[9], grads[10], grads[11], grads[12], grads[13])
```

```python
from functools import partial

import jax
import jax.numpy as jnp
from jax import lax
from jax.experimental import pallas as pl
from jax.experimental.pallas import tpu as pltpu
from jax.sharding import Mesh
from jax.sharding import PartitionSpec as P

D = 768
HEADS = 12
HEAD_DIM = 64
BLOCK = 64
SLOTS = 8
norm_epsilon = 1e-12
masked_score = -1e30
f32 = jnp.float32
bf16 = jnp.bfloat16


def dot_nn(left, right):
    return lax.dot_general(left, right, (((1,), (0,)), ((), ())), preferred_element_type=f32)


def dot_nt(left, right):
    return lax.dot_general(left, right, (((1,), (1,)), ((), ())), preferred_element_type=f32)


def dot_tn(left, right):
    return lax.dot_general(left, right, (((0,), (0,)), ((), ())), preferred_element_type=f32)


def layer_norm(values, scaling, offset):
    center = values - jnp.mean(values, axis=-1, keepdims=True)
    spread = jnp.mean(center * center, axis=-1, keepdims=True)
    return center * lax.rsqrt(spread + norm_epsilon) * scaling + offset


def block_plan(length, randoms, flip, query_blocks):
    blocks = randoms.shape[0]
    last = (length + BLOCK - 1) // BLOCK - 1
    places = jnp.arange(query_blocks, dtype=jnp.int32) ^ flip
    own_randoms = jnp.take_along_axis(randoms, places[:, None], axis=0)
    zero = jnp.zeros((query_blocks,), jnp.int32)
    candidates = jnp.concatenate(
        [
            jnp.stack([places - 1, places, places + 1, zero, zero + last], axis=1),
            own_randoms,
        ],
        axis=1,
    )
    usable = (candidates >= 0) & (candidates < blocks)
    same = candidates[:, :, None] == candidates[:, None, :]
    before = jnp.arange(SLOTS)[:, None] > jnp.arange(SLOTS)[None, :]
    usable = usable & ~jnp.any(same & before[None], axis=2)
    is_global = (places == 0) | (places == last)
    usable = usable & ~is_global[:, None]
    names = jnp.clip(candidates, 0, blocks - 1) ^ flip
    global_name = jnp.where((flip ^ last) < query_blocks, flip ^ last, flip)
    every = jnp.arange(blocks, dtype=jnp.int32).reshape(blocks // SLOTS, SLOTS)
    query_names = jnp.concatenate(
        [
            jnp.arange(query_blocks, dtype=jnp.int32),
            jnp.zeros((blocks // SLOTS,), jnp.int32) + global_name,
        ]
    )
    key_names = jnp.concatenate([names, every])
    bias_names = jnp.concatenate([jnp.where(usable, names, blocks), every])
    return query_names, key_names, bias_names, global_name.reshape(1)


def halves(pair):
    lane = lax.broadcasted_iota(jnp.int32, pair.shape, 1)
    zero = jnp.zeros_like(pair)
    return jnp.concatenate(
        [jnp.where(lane < HEAD_DIM, pair, zero), jnp.where(lane < HEAD_DIM, zero, pair)], axis=0
    )


def join_halves(stacked):
    lane = lax.broadcasted_iota(jnp.int32, (BLOCK, 2 * HEAD_DIM), 1)
    return jnp.where(lane < HEAD_DIM, stacked[:BLOCK], stacked[BLOCK:])


def block_rows(name):
    return pl.ds(pl.multiple_of(name * BLOCK, BLOCK), BLOCK)


def gather_blocks(ref, names):
    return jnp.concatenate([ref[block_rows(name), :] for name in names], axis=0)


def fill_length_bias(bias_scratch, length, flip):
    rows = bias_scratch.shape[0] - BLOCK
    place = lax.broadcasted_iota(jnp.int32, bias_scratch.shape, 0)
    token = (((place // BLOCK) ^ flip) * BLOCK) + place % BLOCK
    live = (token < length) & (place < rows)
    bias_scratch[...] = jnp.where(live, 0.0, masked_score)


def forward_kernel(
    key_names, bias_names, global_name, lengths, flips,
    q_ref, k_ref, v_ref, context_ref, logsum_ref, bias_scratch, score_scratch, *, unroll, query_blocks,
):
    @pl.when(pl.program_id(0) == 0)
    def _():
        fill_length_bias(bias_scratch, lengths[0], flips[0])

    def put(block, context, largest, total):
        context_ref[block_rows(block), :] = join_halves(context).astype(bf16)
        logsum_ref[0, pl.ds(block, 1), :] = largest + jnp.log(total)

    def one(block):
        queries = halves(q_ref[block_rows(block), :])
        names = [key_names[block, slot] for slot in range(SLOTS)]
        biases = [bias_names[block, slot] for slot in range(SLOTS)]
        scores = dot_nt(gather_blocks(k_ref, names), queries) + gather_blocks(bias_scratch, biases)
        largest = jnp.max(scores, axis=0, keepdims=True)
        weights = jnp.exp(scores - largest)
        total = jnp.sum(weights, axis=0, keepdims=True)
        shares = (weights * (1.0 / total)).astype(bf16)
        put(block, dot_tn(shares, gather_blocks(v_ref, names)), largest, total)

    def body(step, carry):
        for within in range(unroll):
            one(step * unroll + within)
        return carry

    lax.fori_loop(0, query_blocks // unroll, body, 0)
    block = global_name[0]
    queries = halves(q_ref[block_rows(block), :])
    tokens = k_ref.shape[0]
    chunk = SLOTS * BLOCK
    together = 4

    def score_chunk(step, largest):
        for within in range(together):
            rows = pl.ds(pl.multiple_of((step * together + within) * chunk, chunk), chunk)
            scores = dot_nt(k_ref[rows, :], queries) + bias_scratch[rows, :]
            score_scratch[rows, :] = scores
            largest = jnp.maximum(largest, jnp.max(scores, axis=0, keepdims=True))
        return largest

    steps = tokens // chunk // together
    lanes = 2 * BLOCK
    largest = lax.fori_loop(0, steps, score_chunk, jnp.full((1, lanes), masked_score, f32))

    def value_chunk(step, carry):
        total, context = carry
        for within in range(together):
            rows = pl.ds(pl.multiple_of((step * together + within) * chunk, chunk), chunk)
            weights = jnp.exp(score_scratch[rows, :] - largest)
            total = total + jnp.sum(weights, axis=0, keepdims=True)
            context = context + dot_tn(weights.astype(bf16), v_ref[rows, :])
        return total, context

    total, context = lax.fori_loop(
        0, steps, value_chunk, (jnp.zeros((1, lanes), f32), jnp.zeros((lanes, lanes), f32))
    )
    context = context * jnp.transpose(jnp.broadcast_to(1.0 / total, (lanes, lanes)))
    put(block, context, largest, total)


def attend(plan, length, flip, q, k, v):
    query_names, key_names, bias_names, global_name = plan
    query_rows, width = q.shape
    tokens = k.shape[0]
    pairs = width // 128
    query_blocks = query_rows // BLOCK
    q_spec = pl.BlockSpec((query_rows, 128), lambda pair, *_: (0, pair))
    k_spec = pl.BlockSpec((tokens, 128), lambda pair, *_: (0, pair))
    return pl.pallas_call(
        partial(forward_kernel, unroll=8, query_blocks=query_blocks),
        grid_spec=pltpu.PrefetchScalarGridSpec(
            num_scalar_prefetch=5,
            grid=(pairs,),
            in_specs=[q_spec, k_spec, k_spec],
            out_specs=[q_spec, pl.BlockSpec((1, query_blocks, 128), lambda pair, *_: (pair, 0, 0))],
            scratch_shapes=[
                pltpu.VMEM((tokens + BLOCK, 128), f32),
                pltpu.VMEM((tokens, 128), f32),
            ],
        ),
        out_shape=[
            jax.ShapeDtypeStruct(q.shape, bf16),
            jax.ShapeDtypeStruct((pairs, query_blocks, 128), f32),
        ],
        compiler_params=pltpu.CompilerParams(vmem_limit_bytes=48 << 20),
        cost_estimate=pl.CostEstimate(flops=40 * 10**9, bytes_accessed=10**7, transcendentals=10**7),
        name="attend_forward",
    )(key_names, bias_names, global_name, length, flip, q, k, v)


def backward_kernel(
    query_names, key_names, bias_names, lengths, flips,
    q_ref, k_ref, v_ref, back_ref, context_ref, logsum_ref,
    back_q_ref, back_k_ref, back_v_ref, bias_scratch, q_scratch, k_scratch, v_scratch, *, unroll, items,
):
    @pl.when(pl.program_id(0) == 0)
    def _():
        fill_length_bias(bias_scratch, lengths[0], flips[0])

    q_scratch[...] = jnp.zeros_like(q_scratch)
    k_scratch[...] = jnp.zeros_like(k_scratch)
    v_scratch[...] = jnp.zeros_like(v_scratch)
    ones = jnp.ones((16, 128), bf16)

    def one(item):
        block = query_names[item]
        rows = block_rows(block)
        queries = halves(q_ref[rows, :])
        back = back_ref[rows, :]
        backs = halves(back)
        product = (back.astype(f32) * context_ref[rows, :].astype(f32)).astype(bf16)
        inner = dot_nt(ones, halves(product))[0:1]
        logsum = logsum_ref[0, pl.ds(block, 1), :]
        names = [key_names[item, slot] for slot in range(SLOTS)]
        biases = [bias_names[item, slot] for slot in range(SLOTS)]
        keys = gather_blocks(k_ref, names)
        scores = dot_nt(keys, queries) + gather_blocks(bias_scratch, biases)
        shares = jnp.exp(scores - logsum)
        back_shares = dot_nt(gather_blocks(v_ref, names), backs)
        back_values = dot_nn(shares.astype(bf16), backs)
        back_scores = (shares * (back_shares - inner)).astype(bf16)
        back_keys = dot_nn(back_scores, queries)
        q_scratch[rows, :] += join_halves(dot_tn(back_scores, keys))
        for slot in range(SLOTS):
            part = slice(slot * BLOCK, (slot + 1) * BLOCK)
            v_scratch[block_rows(names[slot]), :] += back_values[part]
            k_scratch[block_rows(names[slot]), :] += back_keys[part]

    def body(step, carry):
        for within in range(unroll):
            one(step * unroll + within)
        return carry

    lax.fori_loop(0, items // unroll, body, 0)
    back_q_ref[...] = (q_scratch[...] * HEAD_DIM ** (-0.5)).astype(bf16)
    back_k_ref[...] = k_scratch[...].astype(bf16)
    back_v_ref[...] = v_scratch[...].astype(bf16)


def attend_back(plan, length, flip, q, k, v, back, context, logsum):
    query_names, key_names, bias_names, _ = plan
    query_rows, width = q.shape
    tokens = k.shape[0]
    pairs = width // 128
    query_blocks = query_rows // BLOCK
    q_spec = pl.BlockSpec((query_rows, 128), lambda pair, *_: (0, pair))
    k_spec = pl.BlockSpec((tokens, 128), lambda pair, *_: (0, pair))
    return pl.pallas_call(
        partial(backward_kernel, unroll=8, items=query_names.shape[0]),
        grid_spec=pltpu.PrefetchScalarGridSpec(
            num_scalar_prefetch=5,
            grid=(pairs,),
            in_specs=[
                q_spec, k_spec, k_spec, q_spec, q_spec,
                pl.BlockSpec((1, query_blocks, 128), lambda pair, *_: (pair, 0, 0)),
            ],
            out_specs=[q_spec, k_spec, k_spec],
            scratch_shapes=[
                pltpu.VMEM((tokens + BLOCK, 128), f32),
                pltpu.VMEM((query_rows, 128), f32),
                pltpu.VMEM((tokens, 128), f32),
                pltpu.VMEM((tokens, 128), f32),
            ],
        ),
        out_shape=[
            jax.ShapeDtypeStruct(q.shape, bf16),
            jax.ShapeDtypeStruct(k.shape, bf16),
            jax.ShapeDtypeStruct(k.shape, bf16),
        ],
        compiler_params=pltpu.CompilerParams(vmem_limit_bytes=56 << 20),
        cost_estimate=pl.CostEstimate(flops=60 * 10**9, bytes_accessed=10**7, transcendentals=10**7),
        name="attend_backward",
    )(query_names, key_names, bias_names, length, flip, q, k, v, back, context, logsum)


def swap(value, axis, bit=1):
    size = lax.axis_size(axis)
    return lax.ppermute(value, axis, [(place, place ^ bit) for place in range(size)])


def exchange_steps():
    steps = []
    bit = 1
    while bit < lax.axis_size("dp"):
        steps.append(("dp", bit))
        bit *= 2
    return steps


def sum_everywhere(value, steps):
    for axis, bit in steps:
        half = value.shape[0] // 2
        upper = (lax.axis_index(axis) & bit) // bit
        keep = lax.dynamic_slice_in_dim(value, upper * half, half, 0)
        send = lax.dynamic_slice_in_dim(value, (1 - upper) * half, half, 0)
        value = (keep.astype(f32) + swap(send, axis, bit).astype(f32)).astype(bf16)
    for axis, bit in reversed(steps):
        upper = (lax.axis_index(axis) & bit) // bit
        other = swap(value, axis, bit)
        value = jnp.where(
            upper == 0,
            jnp.concatenate([value, other], axis=0),
            jnp.concatenate([other, value], axis=0),
        )
    return value


def per_device(
    inputs, doc_lengths, random_blocks, qkv_weight, query_bias, value_bias, proj_weight, proj_bias,
    first_gain, first_shift, expand_weight, expand_bias, shrink_weight, shrink_bias,
    second_gain, second_shift, cotangent,
):
    hx = lax.axis_index("hx")
    hc = lax.axis_index("hc")
    docs, rows, _ = inputs.shape
    assert docs == 1 and lax.axis_size("hx") == 2 and lax.axis_size("hc") == 2
    half = D // 2
    x = inputs.reshape(rows, D)
    row_blocks = rows // BLOCK
    flip = (hx * 2 + hc).astype(jnp.int32) * row_blocks
    plan = block_plan(doc_lengths[0], random_blocks[0], flip, 2 * row_blocks)
    flip = flip.reshape(1)
    x_far = swap(x, "hx")
    x_near = swap(x, "hc")
    x_all = jnp.concatenate([x, x_near, x_far, swap(x_far, "hc")], axis=0)
    x_chip = x_all[: 2 * rows]

    def own_columns(array, start):
        return lax.dynamic_slice_in_dim(array, start + hc * half, half, array.ndim - 1)

    w_q = own_columns(qkv_weight, 0)
    w_k = own_columns(qkv_weight, D)
    w_v = own_columns(qkv_weight, 2 * D)
    w_proj = jnp.concatenate(
        [
            lax.dynamic_slice_in_dim(proj_weight, hc * half, half, 0),
            lax.dynamic_slice_in_dim(proj_weight, (1 - hc) * half, half, 0),
        ],
        axis=0,
    )
    q = (dot_nn(x_chip, w_q) + own_columns(query_bias, 0).astype(f32)).astype(bf16)
    q = q * jnp.asarray(HEAD_DIM ** (-0.5), bf16)
    k = dot_nn(x_all, w_k).astype(bf16)
    v = (dot_nn(x_all, w_v) + own_columns(value_bias, 0).astype(f32)).astype(bf16)
    context_chip, logsum = attend(plan, doc_lengths, flip, q, k, v)
    context = jnp.concatenate([context_chip[:rows], swap(context_chip[rows:], "hc")], axis=1)

    branch = dot_nn(context, w_proj) + proj_bias.astype(f32)
    resid_one = x.astype(f32) + branch
    hidden, first_pull = jax.vjp(
        layer_norm, resid_one, first_gain.astype(f32), first_shift.astype(f32)
    )
    hidden_low = hidden.astype(bf16)
    inner = dot_nn(hidden_low, expand_weight) + expand_bias.astype(f32)
    active, gelu_pull = jax.vjp(partial(jax.nn.gelu, approximate=False), inner)
    active_low = active.astype(bf16)
    resid_two = hidden + dot_nn(active_low, shrink_weight) + shrink_bias.astype(f32)
    output, second_pull = jax.vjp(
        layer_norm, resid_two, second_gain.astype(f32), second_shift.astype(f32)
    )
    back_two, grad_second_gain, grad_second_shift = second_pull(
        cotangent.reshape(rows, D).astype(f32)
    )
    back_ffn = back_two.astype(bf16)
    grad_shrink = dot_tn(active_low, back_ffn).astype(bf16)
    grad_shrink_bias = jnp.sum(back_ffn.astype(f32), axis=0)
    back_inner = gelu_pull(dot_nt(back_ffn, shrink_weight))[0].astype(bf16)
    grad_expand = dot_tn(hidden_low, back_inner).astype(bf16)
    grad_expand_bias = jnp.sum(back_inner.astype(f32), axis=0)
    back_hidden = back_two + dot_nt(back_inner, expand_weight)
    back_one, grad_first_gain, grad_first_shift = first_pull(back_hidden)
    back_branch = back_one.astype(bf16)
    grad_proj = dot_tn(context, back_branch).astype(bf16)
    grad_proj_bias = jnp.sum(back_branch.astype(f32), axis=0)
    back_context = dot_nt(back_branch, w_proj).astype(bf16)
    back_chip = jnp.concatenate([back_context[:, :half], swap(back_context[:, half:], "hc")], axis=0)

    back_q, back_k, back_v = attend_back(
        plan, doc_lengths, flip, q, k, v, back_chip, context_chip, logsum
    )
    steps = exchange_steps()
    all_steps = [("hc", 1)] + steps + [("hx", 1)]
    chip_steps = steps + [("hx", 1)]
    grad_shrink = sum_everywhere(grad_shrink, all_steps).astype(f32)
    grad_expand = sum_everywhere(grad_expand, all_steps).astype(f32)
    swapped = jnp.concatenate([grad_proj[half:], grad_proj[:half]], axis=0)
    grad_proj = jnp.where(hc == 0, grad_proj, swapped)
    grad_proj = sum_everywhere(grad_proj, all_steps).astype(f32)

    far = slice(2 * rows, 4 * rows)
    back_far = dot_nt(back_k[far], w_k) + dot_nt(back_v[far], w_v)
    back_near = (
        dot_nt(back_k[: 2 * rows], w_k)
        + dot_nt(back_v[: 2 * rows], w_v)
        + dot_nt(back_q, w_q)
    )
    far_own = back_far[:rows] + swap(back_far[rows:].astype(bf16), "hc").astype(f32)
    from_far = swap(far_own.astype(bf16), "hx")
    near_own = back_near[:rows] + swap(back_near[rows:].astype(bf16), "hc").astype(f32)
    input_grad = back_one + near_own + from_far.astype(f32)

    grad_joined = jnp.concatenate(
        [dot_tn(x_chip, back_q), dot_tn(x_all, back_k), dot_tn(x_all, back_v)], axis=1
    ).astype(bf16)
    grad_joined = sum_everywhere(grad_joined, chip_steps)
    other = swap(grad_joined, "hc")
    first = jnp.where(hc == 0, grad_joined, other).reshape(D, 3, half)
    second = jnp.where(hc == 0, other, grad_joined).reshape(D, 3, half)
    grad_qkv = jnp.concatenate([first, second], axis=2).reshape(D, 3 * D).astype(f32)

    sum_q = jnp.sum(back_q.astype(f32), axis=0)
    sum_v = jnp.sum(back_v.astype(f32), axis=0)
    empty = jnp.zeros_like(sum_q)
    vectors = [
        jnp.where(hc == 0, jnp.concatenate([sum_q, empty]), jnp.concatenate([empty, sum_q])),
        jnp.where(hc == 0, jnp.concatenate([sum_v, empty]), jnp.concatenate([empty, sum_v])),
        grad_proj_bias, grad_first_gain, grad_first_shift, grad_expand_bias,
        grad_shrink_bias, grad_second_gain, grad_second_shift,
    ]
    sizes = [member.shape[0] for member in vectors]
    summed = lax.psum(jnp.concatenate(vectors), ("dp", "hx", "hc"))
    parts = []
    at = 0
    for size in sizes:
        parts.append(summed[at : at + size])
        at += size
    return (
        output.astype(bf16).reshape(docs, rows, D),
        input_grad.reshape(docs, rows, D),
        grad_qkv, parts[0], parts[1], grad_proj, parts[2], parts[3], parts[4],
        grad_expand, parts[5], grad_shrink, parts[6], parts[7], parts[8],
    )


def solution(mesh):
    dp = mesh.shape["dp"]
    heads = mesh.shape["heads"]
    split = Mesh(mesh.devices.reshape(dp, heads // 2, 2), ("dp", "hx", "hc"))
    rows = P("dp", ("hx", "hc"), None)
    in_specs = (rows, P("dp"), P("dp", None, None)) + (P(),) * 13 + (rows,)
    out_specs = (rows, rows) + (P(),) * 13
    return jax.shard_map(
        per_device, mesh=split, in_specs=in_specs, out_specs=out_specs, check_vma=False
    )
```

```python
from functools import partial

import jax
import jax.numpy as jnp
from jax import lax
from jax.experimental import pallas as pl
from jax.experimental.pallas import tpu as pltpu
from jax.sharding import Mesh
from jax.sharding import PartitionSpec as P

D = 768
HEADS = 12
HEAD_DIM = 64
BLOCK = 64
SLOTS = 8
norm_epsilon = 1e-12
masked_score = -1e30
f32 = jnp.float32
bf16 = jnp.bfloat16


def dot_nn(left, right):
    return lax.dot_general(left, right, (((1,), (0,)), ((), ())), preferred_element_type=f32)


def dot_nt(left, right):
    return lax.dot_general(left, right, (((1,), (1,)), ((), ())), preferred_element_type=f32)


def dot_tn(left, right):
    return lax.dot_general(left, right, (((0,), (0,)), ((), ())), preferred_element_type=f32)


def layer_norm(values, scaling, offset):
    center = values - jnp.mean(values, axis=-1, keepdims=True)
    spread = jnp.mean(center * center, axis=-1, keepdims=True)
    return center * lax.rsqrt(spread + norm_epsilon) * scaling + offset


def block_plan(length, randoms, flip, query_blocks):
    blocks = randoms.shape[0]
    last = (length + BLOCK - 1) // BLOCK - 1
    places = jnp.arange(query_blocks, dtype=jnp.int32) ^ flip
    own_randoms = jnp.take_along_axis(randoms, places[:, None], axis=0)
    zero = jnp.zeros((query_blocks,), jnp.int32)
    candidates = jnp.concatenate(
        [
            jnp.stack([places - 1, places, places + 1, zero, zero + last], axis=1),
            own_randoms,
        ],
        axis=1,
    )
    usable = (candidates >= 0) & (candidates < blocks)
    same = candidates[:, :, None] == candidates[:, None, :]
    before = jnp.arange(SLOTS)[:, None] > jnp.arange(SLOTS)[None, :]
    usable = usable & ~jnp.any(same & before[None], axis=2)
    is_global = (places == 0) | (places == last)
    usable = usable & ~is_global[:, None]
    names = jnp.clip(candidates, 0, blocks - 1) ^ flip
    global_name = jnp.where((flip ^ last) < query_blocks, flip ^ last, flip)
    every = jnp.arange(blocks, dtype=jnp.int32).reshape(blocks // SLOTS, SLOTS)
    query_names = jnp.concatenate(
        [
            jnp.arange(query_blocks, dtype=jnp.int32),
            jnp.zeros((blocks // SLOTS,), jnp.int32) + global_name,
        ]
    )
    key_names = jnp.concatenate([names, every])
    bias_names = jnp.concatenate([jnp.where(usable, names, blocks), every])
    return query_names, key_names, bias_names, global_name.reshape(1)


def halves(pair):
    lane = lax.broadcasted_iota(jnp.int32, pair.shape, 1)
    zero = jnp.zeros_like(pair)
    return jnp.concatenate(
        [jnp.where(lane < HEAD_DIM, pair, zero), jnp.where(lane < HEAD_DIM, zero, pair)], axis=0
    )


def join_halves(stacked):
    lane = lax.broadcasted_iota(jnp.int32, (BLOCK, 2 * HEAD_DIM), 1)
    return jnp.where(lane < HEAD_DIM, stacked[:BLOCK], stacked[BLOCK:])


def block_rows(name):
    return pl.ds(pl.multiple_of(name * BLOCK, BLOCK), BLOCK)


def gather_blocks(ref, names):
    return jnp.concatenate([ref[block_rows(name), :] for name in names], axis=0)


def fill_length_bias(bias_scratch, length, flip):
    rows = bias_scratch.shape[0] - BLOCK
    place = lax.broadcasted_iota(jnp.int32, bias_scratch.shape, 0)
    token = (((place // BLOCK) ^ flip) * BLOCK) + place % BLOCK
    live = (token < length) & (place < rows)
    bias_scratch[...] = jnp.where(live, 0.0, masked_score)


def forward_kernel(
    key_names, bias_names, global_name, lengths, flips,
    q_ref, k_ref, v_ref, context_ref, logsum_ref, bias_scratch, score_scratch, *, unroll, query_blocks,
):
    @pl.when(pl.program_id(0) == 0)
    def _():
        fill_length_bias(bias_scratch, lengths[0], flips[0])

    def put(block, context, largest, total):
        context_ref[block_rows(block), :] = join_halves(context).astype(bf16)
        logsum_ref[0, pl.ds(block, 1), :] = largest + jnp.log(total)

    def one(block):
        queries = halves(q_ref[block_rows(block), :])
        names = [key_names[block, slot] for slot in range(SLOTS)]
        biases = [bias_names[block, slot] for slot in range(SLOTS)]
        scores = dot_nt(gather_blocks(k_ref, names), queries) + gather_blocks(bias_scratch, biases)
        largest = jnp.max(scores, axis=0, keepdims=True)
        weights = jnp.exp(scores - largest)
        total = jnp.sum(weights, axis=0, keepdims=True)
        shares = (weights * (1.0 / total)).astype(bf16)
        put(block, dot_tn(shares, gather_blocks(v_ref, names)), largest, total)

    def body(step, carry):
        for within in range(unroll):
            one(step * unroll + within)
        return carry

    lax.fori_loop(0, query_blocks // unroll, body, 0)
    block = global_name[0]
    queries = halves(q_ref[block_rows(block), :])
    tokens = k_ref.shape[0]
    chunk = SLOTS * BLOCK
    together = 4

    def score_chunk(step, largest):
        for within in range(together):
            rows = pl.ds(pl.multiple_of((step * together + within) * chunk, chunk), chunk)
            scores = dot_nt(k_ref[rows, :], queries) + bias_scratch[rows, :]
            score_scratch[rows, :] = scores
            largest = jnp.maximum(largest, jnp.max(scores, axis=0, keepdims=True))
        return largest

    steps = tokens // chunk // together
    lanes = 2 * BLOCK
    largest = lax.fori_loop(0, steps, score_chunk, jnp.full((1, lanes), masked_score, f32))

    def value_chunk(step, carry):
        total, context = carry
        for within in range(together):
            rows = pl.ds(pl.multiple_of((step * together + within) * chunk, chunk), chunk)
            weights = jnp.exp(score_scratch[rows, :] - largest)
            total = total + jnp.sum(weights, axis=0, keepdims=True)
            context = context + dot_tn(weights.astype(bf16), v_ref[rows, :])
        return total, context

    total, context = lax.fori_loop(
        0, steps, value_chunk, (jnp.zeros((1, lanes), f32), jnp.zeros((lanes, lanes), f32))
    )
    context = context * jnp.transpose(jnp.broadcast_to(1.0 / total, (lanes, lanes)))
    put(block, context, largest, total)


def attend(plan, length, flip, q, k, v):
    query_names, key_names, bias_names, global_name = plan
    query_rows, width = q.shape
    tokens = k.shape[0]
    pairs = width // 128
    query_blocks = query_rows // BLOCK
    q_spec = pl.BlockSpec((query_rows, 128), lambda pair, *_: (0, pair))
    k_spec = pl.BlockSpec((tokens, 128), lambda pair, *_: (0, pair))
    return pl.pallas_call(
        partial(forward_kernel, unroll=8, query_blocks=query_blocks),
        grid_spec=pltpu.PrefetchScalarGridSpec(
            num_scalar_prefetch=5,
            grid=(pairs,),
            in_specs=[q_spec, k_spec, k_spec],
            out_specs=[q_spec, pl.BlockSpec((1, query_blocks, 128), lambda pair, *_: (pair, 0, 0))],
            scratch_shapes=[
                pltpu.VMEM((tokens + BLOCK, 128), f32),
                pltpu.VMEM((tokens, 128), f32),
            ],
        ),
        out_shape=[
            jax.ShapeDtypeStruct(q.shape, bf16),
            jax.ShapeDtypeStruct((pairs, query_blocks, 128), f32),
        ],
        compiler_params=pltpu.CompilerParams(vmem_limit_bytes=48 << 20),
        cost_estimate=pl.CostEstimate(flops=40 * 10**9, bytes_accessed=10**7, transcendentals=10**7),
        name="attend_forward",
    )(key_names, bias_names, global_name, length, flip, q, k, v)


def backward_kernel(
    query_names, key_names, bias_names, lengths, flips,
    q_ref, k_ref, v_ref, back_ref, context_ref, logsum_ref,
    back_q_ref, back_k_ref, back_v_ref, bias_scratch, q_scratch, k_scratch, v_scratch, *, unroll, items,
):
    @pl.when(pl.program_id(0) == 0)
    def _():
        fill_length_bias(bias_scratch, lengths[0], flips[0])

    q_scratch[...] = jnp.zeros_like(q_scratch)
    k_scratch[...] = jnp.zeros_like(k_scratch)
    v_scratch[...] = jnp.zeros_like(v_scratch)
    ones = jnp.ones((16, 128), bf16)

    def one(item):
        block = query_names[item]
        rows = block_rows(block)
        queries = halves(q_ref[rows, :])
        back = back_ref[rows, :]
        backs = halves(back)
        product = (back.astype(f32) * context_ref[rows, :].astype(f32)).astype(bf16)
        inner = dot_nt(ones, halves(product))[0:1]
        logsum = logsum_ref[0, pl.ds(block, 1), :]
        names = [key_names[item, slot] for slot in range(SLOTS)]
        biases = [bias_names[item, slot] for slot in range(SLOTS)]
        keys = gather_blocks(k_ref, names)
        scores = dot_nt(keys, queries) + gather_blocks(bias_scratch, biases)
        shares = jnp.exp(scores - logsum)
        back_shares = dot_nt(gather_blocks(v_ref, names), backs)
        back_values = dot_nn(shares.astype(bf16), backs)
        back_scores = (shares * (back_shares - inner)).astype(bf16)
        back_keys = dot_nn(back_scores, queries)
        q_scratch[rows, :] += join_halves(dot_tn(back_scores, keys))
        for slot in range(SLOTS):
            part = slice(slot * BLOCK, (slot + 1) * BLOCK)
            v_scratch[block_rows(names[slot]), :] += back_values[part]
            k_scratch[block_rows(names[slot]), :] += back_keys[part]

    def body(step, carry):
        for within in range(unroll):
            one(step * unroll + within)
        return carry

    lax.fori_loop(0, items // unroll, body, 0)
    back_q_ref[...] = (q_scratch[...] * HEAD_DIM ** (-0.5)).astype(bf16)
    back_k_ref[...] = k_scratch[...].astype(bf16)
    back_v_ref[...] = v_scratch[...].astype(bf16)


def attend_back(plan, length, flip, pair, q, k, v, back, context, logsum):
    query_names, key_names, bias_names, _ = plan
    query_rows = q.shape[0]
    tokens = k.shape[0]
    query_blocks = query_rows // BLOCK
    q_in = pl.BlockSpec((query_rows, 128), lambda step, *_: (0, pair))
    k_in = pl.BlockSpec((tokens, 128), lambda step, *_: (0, pair))
    q_out = pl.BlockSpec((query_rows, 128), lambda step, *_: (0, 0))
    k_out = pl.BlockSpec((tokens, 128), lambda step, *_: (0, 0))
    return pl.pallas_call(
        partial(backward_kernel, unroll=8, items=query_names.shape[0]),
        grid_spec=pltpu.PrefetchScalarGridSpec(
            num_scalar_prefetch=5,
            grid=(1,),
            in_specs=[
                q_in, k_in, k_in, q_in, q_in,
                pl.BlockSpec((1, query_blocks, 128), lambda step, *_: (pair, 0, 0)),
            ],
            out_specs=[q_out, k_out, k_out],
            scratch_shapes=[
                pltpu.VMEM((tokens + BLOCK, 128), f32),
                pltpu.VMEM((query_rows, 128), f32),
                pltpu.VMEM((tokens, 128), f32),
                pltpu.VMEM((tokens, 128), f32),
            ],
        ),
        out_shape=[
            jax.ShapeDtypeStruct((query_rows, 128), bf16),
            jax.ShapeDtypeStruct((tokens, 128), bf16),
            jax.ShapeDtypeStruct((tokens, 128), bf16),
        ],
        compiler_params=pltpu.CompilerParams(vmem_limit_bytes=40 << 20),
        cost_estimate=pl.CostEstimate(flops=16 * 10**9, bytes_accessed=10**6, transcendentals=10**6),
        name="attend_backward",
    )(query_names, key_names, bias_names, length, flip, q, k, v, back, context, logsum)


def project_kernel(core, x_ref, x_near_ref, w_q, w_k, w_v, b_q, b_v, q_ref, k_ref, v_ref):
    step = pl.program_id(0)

    def project(tile):
        q = (dot_nn(tile, w_q[...]) + b_q[...]).astype(bf16)
        q_ref[...] = q * jnp.asarray(HEAD_DIM ** (-0.5), bf16)
        k_ref[...] = dot_nn(tile, w_k[...]).astype(bf16)
        v_ref[...] = (dot_nn(tile, w_v[...]) + b_v[...]).astype(bf16)

    @pl.when(step < pl.num_programs(0) // 2)
    def _():
        project(x_ref[...])

    @pl.when(step >= pl.num_programs(0) // 2)
    def _():
        project(x_near_ref[...])


def project_far_kernel(core, x_ref, x_near_ref, w_k, w_v, b_v, k_old, v_old, k_ref, v_ref):
    step = pl.program_id(0)

    def project(tile):
        k_ref[...] = dot_nn(tile, w_k[...]).astype(bf16)
        v_ref[...] = (dot_nn(tile, w_v[...]) + b_v[...]).astype(bf16)

    @pl.when(step < pl.num_programs(0) // 2)
    def _():
        project(x_ref[...])

    @pl.when(step >= pl.num_programs(0) // 2)
    def _():
        project(x_near_ref[...])


TILE = 512


def piece_spec(piece, per, width):
    return pl.BlockSpec((TILE, width), lambda step, *_: (jnp.clip(step - piece * per, 0, per - 1), 0))


def own_weight(which):
    return pl.BlockSpec((D, D // 2), lambda step, core, *_: (0, 2 * which + core[0]))


def own_bias():
    return pl.BlockSpec((1, D // 2), lambda step, core, *_: (0, core[0]))


def project_chip(core, x, x_near, qkv_weight, query_bias, value_bias):
    rows = x.shape[0]
    half = D // 2
    per = rows // TILE
    out = pl.BlockSpec((TILE, half), lambda step, *_: (step, 0))
    return pl.pallas_call(
        project_kernel,
        grid_spec=pltpu.PrefetchScalarGridSpec(
            num_scalar_prefetch=1,
            grid=(2 * per,),
            in_specs=[piece_spec(0, per, D), piece_spec(1, per, D)]
            + [own_weight(0), own_weight(1), own_weight(2), own_bias(), own_bias()],
            out_specs=[out, out, out],
        ),
        out_shape=[
            jax.ShapeDtypeStruct((2 * rows, half), bf16),
            jax.ShapeDtypeStruct((4 * rows, half), bf16),
            jax.ShapeDtypeStruct((4 * rows, half), bf16),
        ],
        compiler_params=pltpu.CompilerParams(vmem_limit_bytes=32 << 20),
        cost_estimate=pl.CostEstimate(flops=4 * 10**9, bytes_accessed=10**7, transcendentals=0),
        name="project_chip",
    )(core, x, x_near, qkv_weight, qkv_weight, qkv_weight, query_bias, value_bias)


def project_far(core, x_far, x_far_near, qkv_weight, value_bias, k, v):
    rows = x_far.shape[0]
    half = D // 2
    per = rows // TILE
    out = pl.BlockSpec((TILE, half), lambda step, *_: (2 * per + step, 0))
    kept = pl.BlockSpec(memory_space=pl.ANY)
    return pl.pallas_call(
        project_far_kernel,
        grid_spec=pltpu.PrefetchScalarGridSpec(
            num_scalar_prefetch=1,
            grid=(2 * per,),
            in_specs=[piece_spec(0, per, D), piece_spec(1, per, D)]
            + [own_weight(1), own_weight(2), own_bias(), kept, kept],
            out_specs=[out, out],
        ),
        out_shape=[jax.ShapeDtypeStruct(k.shape, bf16), jax.ShapeDtypeStruct(v.shape, bf16)],
        input_output_aliases={6: 0, 7: 1},
        compiler_params=pltpu.CompilerParams(vmem_limit_bytes=32 << 20),
        cost_estimate=pl.CostEstimate(flops=3 * 10**9, bytes_accessed=10**7, transcendentals=0),
        name="project_far",
    )(core, x_far, x_far_near, qkv_weight, qkv_weight, value_bias, k, v)


def gelu_pair(x):
    t = 1.0 / (1.0 + (0.3275911 * 0.5**0.5) * jnp.abs(x))
    bell = jnp.exp(-0.5 * x * x)
    poly = 0.7107068705 + t * (-0.7265760135 + t * 0.5307027145)
    tail = t * (0.127414796 + t * (-0.142248368 + t * poly)) * bell
    cdf = jnp.where(x < 0, tail, 1.0 - tail)
    return x * cdf, cdf + x * bell * 0.3989422804014327


def norm_parts(value):
    center = value - jnp.mean(value, axis=-1, keepdims=True)
    spread = jnp.mean(center * center, axis=-1, keepdims=True)
    scale = lax.rsqrt(spread + norm_epsilon)
    return center * scale, scale


def norm_back(slope, normed, scale):
    along = jnp.mean(slope * normed, axis=-1, keepdims=True)
    return scale * (slope - jnp.mean(slope, axis=-1, keepdims=True) - normed * along)


def column_sum(value):
    return jnp.sum(value, axis=0, keepdims=True)


PIECES = 32
STAGES = 8
VECTOR_ROWS = 256


def middle_kernel(
    places, core,
    own_ref, other_ref, x_ref, cot_ref, vector_ref, expand_bias_ref, proj_hbm, expand_hbm, shrink_hbm,
    output_ref, back_one_ref, back_own_ref, back_other_ref, keep_ref, send_ref,
    proj_w, expand_w, shrink_w, active_s, slope_s, shrink_g, expand_g, proj_g, vector_g, bias_g, stage,
    weight_sems, sems, *, chunk,
):
    step = pl.program_id(0)
    half = D // 2
    ff = expand_w.shape[1]
    chunks = ff // chunk
    hc = core[0]
    loads = [
        pltpu.make_async_copy(proj_hbm.at[pl.ds(hc * half, half)], proj_w.at[pl.ds(0, half)], weight_sems.at[0]),
        pltpu.make_async_copy(
            proj_hbm.at[pl.ds((1 - hc) * half, half)], proj_w.at[pl.ds(half, half)], weight_sems.at[1]
        ),
        pltpu.make_async_copy(expand_hbm, expand_w, weight_sems.at[2]),
        pltpu.make_async_copy(shrink_hbm, shrink_w, weight_sems.at[3]),
    ]

    @pl.when(step == 0)
    def _():
        for load in loads:
            load.start()
        for total in (shrink_g, expand_g, proj_g, vector_g, bias_g):
            total[...] = jnp.zeros_like(total)
        loads[0].wait()
        loads[1].wait()

    def vector(row):
        return vector_ref[pl.ds(row, 1), :]

    context = jnp.concatenate([own_ref[...], other_ref[...]], axis=1)
    resid = x_ref[...].astype(f32) + dot_nn(context, proj_w[...]) + vector(0)
    normed_one, scale_one = norm_parts(resid)
    hidden = normed_one * vector(1) + vector(2)
    low = hidden.astype(bf16)
    resid_two = hidden + vector(3)

    @pl.when(step == 0)
    def _():
        loads[2].wait()
        loads[3].wait()

    for part in range(chunks):
        cols = slice(part * chunk, (part + 1) * chunk)
        inner = dot_nn(low, expand_w[:, cols]) + expand_bias_ref[:, cols]
        active, slope = gelu_pair(inner)
        active = active.astype(bf16)
        active_s[:, cols] = active
        slope_s[:, cols] = slope.astype(bf16)
        resid_two = resid_two + dot_nn(active, shrink_w[cols, :])
    normed_two, scale_two = norm_parts(resid_two)
    output_ref[...] = (normed_two * vector(4) + vector(5)).astype(bf16)
    cot = cot_ref[...].astype(f32)
    back_two = norm_back(vector(4) * cot, normed_two, scale_two)
    low_two = back_two.astype(bf16)
    vector_g[3:4, :] += column_sum(low_two.astype(f32))
    vector_g[4:5, :] += column_sum(cot * normed_two)
    vector_g[5:6, :] += column_sum(cot)
    back = back_two
    for part in range(chunks):
        cols = slice(part * chunk, (part + 1) * chunk)
        back_inner = (dot_nt(low_two, shrink_w[cols, :]) * slope_s[:, cols].astype(f32)).astype(bf16)
        bias_g[:, cols] += column_sum(back_inner.astype(f32))
        back = back + dot_nt(back_inner, expand_w[:, cols])
        shrink_g[cols, :] += dot_tn(active_s[:, cols], low_two)
        expand_g[:, cols] += dot_tn(low, back_inner)
    vector_g[1:2, :] += column_sum(back * normed_one)
    vector_g[2:3, :] += column_sum(back)
    back_one = norm_back(vector(1) * back, normed_one, scale_one)
    back_one_ref[...] = back_one
    low_one = back_one.astype(bf16)
    vector_g[0:1, :] += column_sum(low_one.astype(f32))
    proj_g[:D, :] += dot_tn(context, low_one)
    back_context = dot_nt(low_one, proj_w[...]).astype(bf16)
    back_own_ref[...] = back_context[:, :half]
    back_other_ref[...] = back_context[:, half:]

    @pl.when(step == pl.num_programs(0) - 1)
    def _():
        proj_g[D:, :] = jnp.zeros((proj_g.shape[0] - D, D), f32)
        proj_g[D : D + 8, :] = vector_g[...]
        for part in range(ff // D):
            proj_g[D + 8 + part : D + 9 + part, :] = bias_g[:, part * D : (part + 1) * D]
        kept = PIECES // 2
        rows = ff // PIECES
        extra = proj_g.shape[0] // (2 * PIECES)
        wide = ff // D
        half_chunks = half // extra

        def wait(color, slot):
            pltpu.make_async_copy(stage.at[color, slot], keep_ref.at[0], sems.at[color, slot]).wait()

        def put(piece, carry):
            slot = lax.rem(piece, STAGES)

            @pl.when(piece >= STAGES)
            def _():
                wait(0, slot)
                wait(1, slot)

            first = piece ^ places[0]
            second = piece ^ places[1]

            def extra_rows(place):
                turned = lax.rem(place + half_chunks * hc, 2 * half_chunks)
                place = jnp.where(place < 2 * half_chunks, turned, place)
                return proj_g[pl.ds(pl.multiple_of(place * extra, extra), extra), :].astype(bf16)

            stage[0, slot, :rows, :] = shrink_g[pl.ds(pl.multiple_of(first * rows, rows), rows), :].astype(bf16)
            stage[0, slot, rows:, :] = extra_rows(first)
            down = pl.ds(pl.multiple_of((second // wide) * rows, rows), rows)
            across = pl.ds(pl.multiple_of((second % wide) * D, D), D)
            stage[1, slot, :rows, :] = expand_g[down, across].astype(bf16)
            stage[1, slot, rows:, :] = extra_rows(PIECES + second)
            place = lax.rem(piece, kept)
            for color in range(2):
                source = stage.at[color, slot]

                @pl.when(piece < kept)
                def _():
                    pltpu.make_async_copy(source, keep_ref.at[color * kept + place], sems.at[color, slot]).start()

                @pl.when(piece >= kept)
                def _():
                    pltpu.make_async_copy(source, send_ref.at[color * kept + place], sems.at[color, slot]).start()

            return carry

        lax.fori_loop(0, PIECES, put, 0)
        for slot in range(STAGES):
            wait(0, slot)
            wait(1, slot)


def middle(places, core, own, other, x, cot, vectors, expand_bias, proj_weight, expand_weight, shrink_weight):
    rows = x.shape[0]
    ff = expand_weight.shape[1]
    half = D // 2
    tile = 256
    piece_rows = ff // PIECES + (D + VECTOR_ROWS) // (2 * PIECES)

    def row(width):
        return pl.BlockSpec((tile, width), lambda step, *_: (step, 0))

    def whole(array):
        return pl.BlockSpec(array.shape, lambda step, *_: (0, 0))

    kept = pl.BlockSpec(memory_space=pl.ANY)
    packed = jax.ShapeDtypeStruct((PIECES, piece_rows, D), bf16)
    return pl.pallas_call(
        partial(middle_kernel, chunk=D),
        grid_spec=pltpu.PrefetchScalarGridSpec(
            num_scalar_prefetch=2,
            grid=(rows // tile,),
            in_specs=[row(half), row(half), row(D), row(D), whole(vectors), whole(expand_bias), kept, kept, kept],
            out_specs=[row(D), row(D), row(half), row(half), kept, kept],
            scratch_shapes=[
                pltpu.VMEM((D, D), bf16),
                pltpu.VMEM((D, ff), bf16),
                pltpu.VMEM((ff, D), bf16),
                pltpu.VMEM((tile, ff), bf16),
                pltpu.VMEM((tile, ff), bf16),
                pltpu.VMEM((ff, D), f32),
                pltpu.VMEM((D, ff), f32),
                pltpu.VMEM((D + VECTOR_ROWS, D), f32),
                pltpu.VMEM((8, D), f32),
                pltpu.VMEM((1, ff), f32),
                pltpu.VMEM((2, STAGES, piece_rows, D), bf16),
                pltpu.SemaphoreType.DMA((4,)),
                pltpu.SemaphoreType.DMA((2, STAGES)),
            ],
        ),
        out_shape=[
            jax.ShapeDtypeStruct((rows, D), bf16),
            jax.ShapeDtypeStruct((rows, D), f32),
            jax.ShapeDtypeStruct((rows, half), bf16),
            jax.ShapeDtypeStruct((rows, half), bf16),
            packed,
            packed,
        ],
        compiler_params=pltpu.CompilerParams(vmem_limit_bytes=60 << 20),
        cost_estimate=pl.CostEstimate(flops=60 * 10**9, bytes_accessed=10**7, transcendentals=10**7),
        name="middle",
    )(places, core, own, other, x, cot, vectors, expand_bias, proj_weight, expand_weight, shrink_weight)


def input_far_kernel(core, *refs):
    w_k, w_v, out = refs[0], refs[1], refs[-1]
    arrays = refs[2:-1]
    pairs = len(arrays) // 2
    back_k = jnp.concatenate([ref[...] for ref in arrays[:pairs]], axis=1)
    back_v = jnp.concatenate([ref[...] for ref in arrays[pairs:]], axis=1)
    out[...] = (dot_nt(back_k, w_k[...]) + dot_nt(back_v, w_v[...])).astype(bf16)


def input_far(core, qkv_weight, back_ks, back_vs, rows):
    first = 2 * rows // TILE
    token = pl.BlockSpec((TILE, 128), lambda step, *_: (first + step, 0))
    arrays = list(back_ks) + list(back_vs)
    return pl.pallas_call(
        input_far_kernel,
        grid_spec=pltpu.PrefetchScalarGridSpec(
            num_scalar_prefetch=1,
            grid=(2 * rows // TILE,),
            in_specs=[own_weight(1), own_weight(2)] + [token] * len(arrays),
            out_specs=pl.BlockSpec((TILE, D), lambda step, *_: (step, 0)),
        ),
        out_shape=jax.ShapeDtypeStruct((2 * rows, D), bf16),
        compiler_params=pltpu.CompilerParams(vmem_limit_bytes=32 << 20),
        cost_estimate=pl.CostEstimate(flops=3 * 10**9, bytes_accessed=10**7, transcendentals=0),
        name="input_far",
    )(core, qkv_weight, qkv_weight, *arrays)


QKV_PIECES = 16


def joined_kernel(places, core, *refs, tiles, pairs):
    w_q, w_k, w_v = refs[:3]
    x_refs = refs[3:7]
    arrays = refs[7 : 7 + 3 * pairs]
    near_ref, first_ref, second_ref = refs[7 + 3 * pairs : 10 + 3 * pairs]
    q_g, k_g, v_g, b_g = refs[10 + 3 * pairs :]
    step = pl.program_id(0)
    half = D // 2
    per = tiles // 4

    @pl.when(step == 0)
    def _():
        for total in (q_g, k_g, v_g, b_g):
            total[...] = jnp.zeros_like(total)

    def joined(which):
        return jnp.concatenate([ref[...] for ref in arrays[which * pairs : (which + 1) * pairs]], axis=1)

    ones = jnp.ones((TILE, 128), bf16)
    for piece in range(4):

        @pl.when((step >= piece * per) & (step < (piece + 1) * per))
        def _():
            x = x_refs[piece][...]
            back_k = joined(1)
            back_v = joined(2)
            k_g[...] += dot_tn(x, back_k)
            v_g[...] += dot_tn(x, back_v)
            b_g[half:, :] += dot_tn(back_v, ones)
            if piece < 2:
                back_q = joined(0)
                q_g[...] += dot_tn(x, back_q)
                b_g[:half, :] += dot_tn(back_q, ones)
                near_ref[...] = (
                    dot_nt(back_q, w_q[...]) + dot_nt(back_k, w_k[...]) + dot_nt(back_v, w_v[...])
                ).astype(bf16)

    @pl.when(step == tiles - 1)
    def _():
        rows = D // QKV_PIECES
        for piece in range(QKV_PIECES):
            part = pl.ds(pl.multiple_of((piece ^ places[0]) * rows, rows), rows)
            first_ref[piece, :, :half] = q_g[part, :].astype(bf16)
            first_ref[piece, :, half:] = k_g[part, :256].astype(bf16)
            part = pl.ds(pl.multiple_of((piece ^ places[1]) * rows, rows), rows)
            second_ref[piece, :, :128] = k_g[part, 256:].astype(bf16)
            second_ref[piece, :, 128 : 128 + half] = v_g[part, :].astype(bf16)
            second_ref[piece, :, 128 + half :] = b_g[part, :].astype(bf16)


def joined_grads(places, core, qkv_weight, xs, back_qs, back_ks, back_vs):
    rows = xs[0].shape[0]
    pairs = len(back_qs)
    per = rows // TILE
    tiles = 4 * per
    half = D // 2
    width = half + 256
    token = pl.BlockSpec((TILE, 128), lambda step, *_: (step, 0))
    query = pl.BlockSpec((TILE, 128), lambda step, *_: (jnp.minimum(step, 2 * per - 1), 0))
    weights = [
        pl.BlockSpec((D, half), lambda step, places, core, which=which: (0, 2 * which + core[0]))
        for which in range(3)
    ]
    packed = pl.BlockSpec((QKV_PIECES, D // QKV_PIECES, width), lambda step, *_: (0, 0, 0))
    packed_shape = jax.ShapeDtypeStruct((QKV_PIECES, D // QKV_PIECES, width), bf16)
    return pl.pallas_call(
        partial(joined_kernel, tiles=tiles, pairs=pairs),
        grid_spec=pltpu.PrefetchScalarGridSpec(
            num_scalar_prefetch=2,
            grid=(tiles,),
            in_specs=weights
            + [piece_spec(piece, per, D) for piece in range(4)]
            + [query] * pairs
            + [token] * (2 * pairs),
            out_specs=[
                pl.BlockSpec((TILE, D), lambda step, *_: (jnp.minimum(step, 2 * per - 1), 0)),
                packed,
                packed,
            ],
            scratch_shapes=[pltpu.VMEM((D, half), f32)] * 3 + [pltpu.VMEM((D, 128), f32)],
        ),
        out_shape=[jax.ShapeDtypeStruct((2 * rows, D), bf16), packed_shape, packed_shape],
        compiler_params=pltpu.CompilerParams(vmem_limit_bytes=48 << 20),
        cost_estimate=pl.CostEstimate(flops=10 * 10**9, bytes_accessed=10**7, transcendentals=0),
        name="joined_grads",
    )(places, core, qkv_weight, qkv_weight, qkv_weight, *xs, *back_qs, *back_ks, *back_vs)


def unpack_kernel(places, first_own, first_other, second_own, second_other, shrink_ref, expand_ref, low_ref, high_ref, *, rows):
    step = pl.program_id(0)
    kept = PIECES // 2

    def put(first, second):
        shrink_ref[...] = first[0, :rows, :].astype(f32)
        expand_ref[...] = second[0, :rows, :].astype(f32)
        low_ref[...] = first[0, rows:, :].astype(f32)
        high_ref[...] = second[0, rows:, :].astype(f32)

    @pl.when(step < kept)
    def _():
        put(first_own, second_own)

    @pl.when(step >= kept)
    def _():
        put(first_other, second_other)


def unpack(places, first_own, first_other, second_own, second_other, ff):
    kept, piece_rows, _ = first_own.shape
    rows = ff // PIECES
    extra = piece_rows - rows
    wide = ff // D
    own = pl.BlockSpec((1, piece_rows, D), lambda step, *_: (jnp.minimum(step, kept - 1), 0, 0))
    other = pl.BlockSpec((1, piece_rows, D), lambda step, *_: (jnp.maximum(step - kept, 0), 0, 0))
    return pl.pallas_call(
        partial(unpack_kernel, rows=rows),
        grid_spec=pltpu.PrefetchScalarGridSpec(
            num_scalar_prefetch=1,
            grid=(PIECES,),
            in_specs=[own, other, own, other],
            out_specs=[
                pl.BlockSpec((rows, D), lambda step, places: (step ^ places[0], 0)),
                pl.BlockSpec((rows, D), lambda step, places: ((step ^ places[1]) // wide, (step ^ places[1]) % wide)),
                pl.BlockSpec((extra, D), lambda step, places: (step ^ places[0], 0)),
                pl.BlockSpec((extra, D), lambda step, places: (step ^ places[1], 0)),
            ],
        ),
        out_shape=[
            jax.ShapeDtypeStruct((ff, D), f32),
            jax.ShapeDtypeStruct((D, ff), f32),
            jax.ShapeDtypeStruct((extra * PIECES, D), f32),
            jax.ShapeDtypeStruct((extra * PIECES, D), f32),
        ],
        compiler_params=pltpu.CompilerParams(vmem_limit_bytes=32 << 20),
        cost_estimate=pl.CostEstimate(flops=10**6, bytes_accessed=42 * 10**6, transcendentals=0),
        name="unpack",
    )(places, first_own, first_other, second_own, second_other)


def unpack_joined_kernel(places, core, first_own, second_own, first_other, second_other, out_ref, bias_ref):
    half = D // 2

    def put(first, second, place):
        def at(which):
            return slice(which * D + place * half, which * D + (place + 1) * half)

        out_ref[:, at(0)] = first[0, :, :half].astype(f32)
        out_ref[:, at(1)] = jnp.concatenate([first[0, :, half:], second[0, :, :128]], axis=1).astype(f32)
        out_ref[:, at(2)] = second[0, :, 128 : 128 + half].astype(f32)
        bias_ref[:, place * 128 : (place + 1) * 128] = second[0, :, 128 + half :].astype(f32)

    @pl.when(core[0] == 0)
    def _():
        put(first_own, second_own, 0)
        put(first_other, second_other, 1)

    @pl.when(core[0] != 0)
    def _():
        put(first_own, second_own, 1)
        put(first_other, second_other, 0)


def unpack_joined(places, core, first_own, second_own, first_other, second_other):
    count, rows, width = first_own.shape
    first = pl.BlockSpec((1, rows, width), lambda step, places, core: (step ^ places[0], 0, 0))
    second = pl.BlockSpec((1, rows, width), lambda step, places, core: (step ^ places[1], 0, 0))
    return pl.pallas_call(
        unpack_joined_kernel,
        grid_spec=pltpu.PrefetchScalarGridSpec(
            num_scalar_prefetch=2,
            grid=(count,),
            in_specs=[first, second, first, second],
            out_specs=[
                pl.BlockSpec((rows, 3 * D), lambda step, *_: (step, 0)),
                pl.BlockSpec((rows, 256), lambda step, *_: (step, 0)),
            ],
        ),
        out_shape=[jax.ShapeDtypeStruct((D, 3 * D), f32), jax.ShapeDtypeStruct((D, 256), f32)],
        compiler_params=pltpu.CompilerParams(vmem_limit_bytes=32 << 20),
        cost_estimate=pl.CostEstimate(flops=10**6, bytes_accessed=10**7, transcendentals=0),
        name="unpack_joined",
    )(places, core, first_own, second_own, first_other, second_other)


def swap(value, axis, bit=1):
    size = lax.axis_size(axis)
    return lax.ppermute(value, axis, [(place, place ^ bit) for place in range(size)])


def place_of(order):
    number = jnp.zeros((), jnp.int32)
    for axis, bit in order:
        number = 2 * number + ((lax.axis_index(axis) & bit) // bit).astype(jnp.int32)
    return number


def add_low(left, right):
    return (left.astype(f32) + right.astype(f32)).astype(bf16)


def scatter_sum(keep, arrived, order):
    for axis, bit in order:
        half = keep.shape[0] // 2
        if arrived is None:
            send, keep = keep[half:], keep[:half]
        else:
            send, keep = add_low(keep[half:], arrived[half:]), add_low(keep[:half], arrived[:half])
        arrived = swap(send, axis, bit)
    total = add_low(keep, arrived)
    bit = 8
    while bit < lax.axis_size("dp"):
        total = add_low(total, swap(total, "dp", bit))
        bit *= 2
    return total


def gather_sum(piece, order):
    for axis, bit in reversed(order):
        piece = jnp.concatenate([piece, swap(piece, axis, bit)], axis=0)
    return piece


def per_device(
    inputs, doc_lengths, random_blocks, qkv_weight, query_bias, value_bias, proj_weight, proj_bias,
    first_gain, first_shift, expand_weight, expand_bias, shrink_weight, shrink_bias,
    second_gain, second_shift, cotangent,
):
    hx = lax.axis_index("hx")
    hc = lax.axis_index("hc")
    docs, rows, _ = inputs.shape
    assert docs == 1 and lax.axis_size("hx") == 2 and lax.axis_size("hc") == 2
    half = D // 2
    ff = expand_weight.shape[1]
    pairs = half // 128
    x = inputs.reshape(rows, D)
    x_far = swap(x, "hx")
    x_near = swap(x, "hc")
    row_blocks = rows // BLOCK
    flip = (hx * 2 + hc).astype(jnp.int32) * row_blocks
    plan = block_plan(doc_lengths[0], random_blocks[0], flip, 2 * row_blocks)
    flip = flip.reshape(1)
    core = hc.astype(jnp.int32).reshape(1)
    first_order = [("dp", 1), ("dp", 2), ("dp", 4), ("hx", 1)]
    second_order = [("hx", 1), ("dp", 1), ("dp", 2), ("dp", 4)]
    core_order = [("hc", 1)]
    places = jnp.stack([place_of(core_order + first_order), place_of(core_order + second_order)])
    chip_places = jnp.stack([place_of(first_order), place_of(second_order)])

    bias_q = query_bias.astype(f32).reshape(1, D)
    bias_v = value_bias.astype(f32).reshape(1, D)
    q, k, v = project_chip(core, x, x_near, qkv_weight, bias_q, bias_v)
    x_far_near = swap(x_far, "hc")
    k, v = project_far(core, x_far, x_far_near, qkv_weight, bias_v, k, v)
    context, logsum = attend(plan, doc_lengths, flip, q, k, v)
    other_context = swap(context[rows:], "hc")
    empty = jnp.zeros((D,), bf16)
    vectors = jnp.stack(
        [proj_bias, first_gain, first_shift, shrink_bias, second_gain, second_shift, empty, empty]
    ).astype(f32)
    output, back_one, back_own, back_other, grads_keep, grads_send = middle(
        places, core, context, other_context, x, cotangent.reshape(rows, D), vectors,
        expand_bias.astype(f32).reshape(1, ff), proj_weight, expand_weight, shrink_weight,
    )
    back = jnp.concatenate([back_own, swap(back_other, "hc")], axis=0)
    grads_arrived = swap(grads_send, "hc")
    back_qs, back_ks, back_vs = zip(
        *[attend_back(plan, doc_lengths, flip, pair, q, k, v, back, context, logsum) for pair in range(pairs)]
    )
    kept = PIECES // 2
    first = scatter_sum(grads_keep[:kept], grads_arrived[:kept], first_order)
    second = scatter_sum(grads_keep[kept:], grads_arrived[kept:], second_order)

    far = input_far(core, qkv_weight, back_ks, back_vs, rows)
    far_own = add_low(far[:rows], swap(far[rows:], "hc"))
    from_far = swap(far_own, "hx")
    near, joined_first, joined_second = joined_grads(
        chip_places, core, qkv_weight, (x, x_near, x_far, x_far_near), back_qs, back_ks, back_vs
    )
    from_near = swap(near[rows:], "hc")
    joined_first = gather_sum(scatter_sum(joined_first, None, first_order), first_order)
    joined_second = gather_sum(scatter_sum(joined_second, None, second_order), second_order)
    first = gather_sum(first, first_order)
    second = gather_sum(second, second_order)
    input_grad = back_one + near[:rows].astype(f32) + from_near.astype(f32) + from_far.astype(f32)

    grad_shrink, grad_expand, low, high = unpack(
        places, first, swap(first, "hc"), second, swap(second, "hc"), ff
    )
    grad_qkv, bias = unpack_joined(
        chip_places, core, joined_first, joined_second, swap(joined_first, "hc"), swap(joined_second, "hc")
    )
    low_rows = low.shape[0]
    grad_proj = jnp.concatenate([low, high[: D - low_rows]], axis=0)
    vector = high[D - low_rows :]
    grad_query_bias = jnp.concatenate([bias[:half, 0], bias[:half, 128]])
    grad_value_bias = jnp.concatenate([bias[half:, 0], bias[half:, 128]])
    grad_expand_bias = vector[8 : 8 + ff // D].reshape(ff)
    return (
        output.reshape(docs, rows, D),
        input_grad.reshape(docs, rows, D),
        grad_qkv, grad_query_bias, grad_value_bias, grad_proj, vector[0], vector[1], vector[2],
        grad_expand, grad_expand_bias, grad_shrink, vector[3], vector[4], vector[5],
    )


def solution(mesh):
    dp = mesh.shape["dp"]
    heads = mesh.shape["heads"]
    split = Mesh(mesh.devices.reshape(dp, heads // 2, 2), ("dp", "hx", "hc"))
    rows = P("dp", ("hx", "hc"), None)
    in_specs = (rows, P("dp"), P("dp", None, None)) + (P(),) * 13 + (rows,)
    out_specs = (rows, rows) + (P(),) * 13
    return jax.shard_map(
        per_device, mesh=split, in_specs=in_specs, out_specs=out_specs, check_vma=False
    )
```

```python
from functools import partial

import jax
import jax.numpy as jnp
from jax import lax
from jax.experimental import pallas as pl
from jax.experimental.pallas import tpu as pltpu
from jax.sharding import Mesh
from jax.sharding import PartitionSpec as P

D = 768
HEADS = 12
HEAD_DIM = 64
BLOCK = 64
SLOTS = 8
norm_epsilon = 1e-12
masked_score = -1e30
f32 = jnp.float32
bf16 = jnp.bfloat16


def dot_nn(left, right):
    return lax.dot_general(left, right, (((1,), (0,)), ((), ())), preferred_element_type=f32)


def dot_nt(left, right):
    return lax.dot_general(left, right, (((1,), (1,)), ((), ())), preferred_element_type=f32)


def dot_tn(left, right):
    return lax.dot_general(left, right, (((0,), (0,)), ((), ())), preferred_element_type=f32)


def layer_norm(values, scaling, offset):
    center = values - jnp.mean(values, axis=-1, keepdims=True)
    spread = jnp.mean(center * center, axis=-1, keepdims=True)
    return center * lax.rsqrt(spread + norm_epsilon) * scaling + offset


def block_plan(length, randoms, flip, query_blocks):
    blocks = randoms.shape[0]
    last = (length + BLOCK - 1) // BLOCK - 1
    places = jnp.arange(query_blocks, dtype=jnp.int32) ^ flip
    own_randoms = jnp.take_along_axis(randoms, places[:, None], axis=0)
    zero = jnp.zeros((query_blocks,), jnp.int32)
    candidates = jnp.concatenate(
        [
            jnp.stack([places - 1, places, places + 1, zero, zero + last], axis=1),
            own_randoms,
        ],
        axis=1,
    )
    usable = (candidates >= 0) & (candidates < blocks)
    same = candidates[:, :, None] == candidates[:, None, :]
    before = jnp.arange(SLOTS)[:, None] > jnp.arange(SLOTS)[None, :]
    usable = usable & ~jnp.any(same & before[None], axis=2)
    is_global = (places == 0) | (places == last)
    usable = usable & ~is_global[:, None]
    names = jnp.clip(candidates, 0, blocks - 1) ^ flip
    global_name = jnp.where((flip ^ last) < query_blocks, flip ^ last, flip)
    every = jnp.arange(blocks, dtype=jnp.int32).reshape(blocks // SLOTS, SLOTS)
    query_names = jnp.concatenate(
        [
            jnp.arange(query_blocks, dtype=jnp.int32),
            jnp.zeros((blocks // SLOTS,), jnp.int32) + global_name,
        ]
    )
    key_names = jnp.concatenate([names, every])
    bias_names = jnp.concatenate([jnp.where(usable, names, blocks), every])
    return query_names, key_names, bias_names, global_name.reshape(1)


def halves(pair):
    lane = lax.broadcasted_iota(jnp.int32, pair.shape, 1)
    zero = jnp.zeros_like(pair)
    return jnp.concatenate(
        [jnp.where(lane < HEAD_DIM, pair, zero), jnp.where(lane < HEAD_DIM, zero, pair)], axis=0
    )


def join_halves(stacked):
    lane = lax.broadcasted_iota(jnp.int32, (BLOCK, 2 * HEAD_DIM), 1)
    return jnp.where(lane < HEAD_DIM, stacked[:BLOCK], stacked[BLOCK:])


def block_rows(name):
    return pl.ds(pl.multiple_of(name * BLOCK, BLOCK), BLOCK)


def gather_blocks(ref, names):
    return jnp.concatenate([ref[block_rows(name), :] for name in names], axis=0)


def fill_length_bias(bias_scratch, length, flip):
    rows = bias_scratch.shape[0] - BLOCK
    place = lax.broadcasted_iota(jnp.int32, bias_scratch.shape, 0)
    token = (((place // BLOCK) ^ flip) * BLOCK) + place % BLOCK
    live = (token < length) & (place < rows)
    bias_scratch[...] = jnp.where(live, 0.0, masked_score)


def forward_kernel(
    key_names, bias_names, global_name, lengths, flips,
    q_ref, k_ref, v_ref, context_ref, logsum_ref, bias_scratch, score_scratch, *, unroll, query_blocks,
):
    @pl.when(pl.program_id(0) == 0)
    def _():
        fill_length_bias(bias_scratch, lengths[0], flips[0])

    def put(block, context, largest, total):
        context_ref[block_rows(block), :] = join_halves(context).astype(bf16)
        logsum_ref[0, pl.ds(block, 1), :] = largest + jnp.log(total)

    def one(block):
        queries = halves(q_ref[block_rows(block), :])
        names = [key_names[block, slot] for slot in range(SLOTS)]
        biases = [bias_names[block, slot] for slot in range(SLOTS)]
        scores = dot_nt(gather_blocks(k_ref, names), queries) + gather_blocks(bias_scratch, biases)
        largest = jnp.max(scores, axis=0, keepdims=True)
        weights = jnp.exp(scores - largest)
        total = jnp.sum(weights, axis=0, keepdims=True)
        shares = (weights * (1.0 / total)).astype(bf16)
        put(block, dot_tn(shares, gather_blocks(v_ref, names)), largest, total)

    def body(step, carry):
        for within in range(unroll):
            one(step * unroll + within)
        return carry

    lax.fori_loop(0, query_blocks // unroll, body, 0)
    block = global_name[0]
    queries = halves(q_ref[block_rows(block), :])
    tokens = k_ref.shape[0]
    chunk = SLOTS * BLOCK
    together = 4

    def score_chunk(step, largest):
        for within in range(together):
            rows = pl.ds(pl.multiple_of((step * together + within) * chunk, chunk), chunk)
            scores = dot_nt(k_ref[rows, :], queries) + bias_scratch[rows, :]
            score_scratch[rows, :] = scores
            largest = jnp.maximum(largest, jnp.max(scores, axis=0, keepdims=True))
        return largest

    steps = tokens // chunk // together
    lanes = 2 * BLOCK
    largest = lax.fori_loop(0, steps, score_chunk, jnp.full((1, lanes), masked_score, f32))

    def value_chunk(step, carry):
        total, context = carry
        for within in range(together):
            rows = pl.ds(pl.multiple_of((step * together + within) * chunk, chunk), chunk)
            weights = jnp.exp(score_scratch[rows, :] - largest)
            total = total + jnp.sum(weights, axis=0, keepdims=True)
            context = context + dot_tn(weights.astype(bf16), v_ref[rows, :])
        return total, context

    total, context = lax.fori_loop(
        0, steps, value_chunk, (jnp.zeros((1, lanes), f32), jnp.zeros((lanes, lanes), f32))
    )
    context = context * jnp.transpose(jnp.broadcast_to(1.0 / total, (lanes, lanes)))
    put(block, context, largest, total)


def attend(plan, length, flip, q, k, v):
    query_names, key_names, bias_names, global_name = plan
    query_rows, width = q.shape
    tokens = k.shape[0]
    pairs = width // 128
    query_blocks = query_rows // BLOCK
    q_spec = pl.BlockSpec((query_rows, 128), lambda pair, *_: (0, pair))
    k_spec = pl.BlockSpec((tokens, 128), lambda pair, *_: (0, pair))
    return pl.pallas_call(
        partial(forward_kernel, unroll=8, query_blocks=query_blocks),
        grid_spec=pltpu.PrefetchScalarGridSpec(
            num_scalar_prefetch=5,
            grid=(pairs,),
            in_specs=[q_spec, k_spec, k_spec],
            out_specs=[q_spec, pl.BlockSpec((1, query_blocks, 128), lambda pair, *_: (pair, 0, 0))],
            scratch_shapes=[
                pltpu.VMEM((tokens + BLOCK, 128), f32),
                pltpu.VMEM((tokens, 128), f32),
            ],
        ),
        out_shape=[
            jax.ShapeDtypeStruct(q.shape, bf16),
            jax.ShapeDtypeStruct((pairs, query_blocks, 128), f32),
        ],
        compiler_params=pltpu.CompilerParams(vmem_limit_bytes=48 << 20),
        cost_estimate=pl.CostEstimate(flops=40 * 10**9, bytes_accessed=10**7, transcendentals=10**7),
        name="attend_forward",
    )(key_names, bias_names, global_name, length, flip, q, k, v)


def backward_kernel(
    query_names, key_names, bias_names, lengths, flips,
    q_ref, k_ref, v_ref, back_ref, context_ref, logsum_ref,
    back_q_ref, back_k_ref, back_v_ref, bias_scratch, q_scratch, k_scratch, v_scratch, *, unroll, items,
):
    @pl.when(pl.program_id(0) == 0)
    def _():
        fill_length_bias(bias_scratch, lengths[0], flips[0])

    q_scratch[...] = jnp.zeros_like(q_scratch)
    k_scratch[...] = jnp.zeros_like(k_scratch)
    v_scratch[...] = jnp.zeros_like(v_scratch)
    ones = jnp.ones((16, 128), bf16)

    def one(item):
        block = query_names[item]
        rows = block_rows(block)
        queries = halves(q_ref[rows, :])
        back = back_ref[rows, :]
        backs = halves(back)
        product = (back.astype(f32) * context_ref[rows, :].astype(f32)).astype(bf16)
        inner = dot_nt(ones, halves(product))[0:1]
        logsum = logsum_ref[0, pl.ds(block, 1), :]
        names = [key_names[item, slot] for slot in range(SLOTS)]
        biases = [bias_names[item, slot] for slot in range(SLOTS)]
        keys = gather_blocks(k_ref, names)
        scores = dot_nt(keys, queries) + gather_blocks(bias_scratch, biases)
        shares = jnp.exp(scores - logsum)
        back_shares = dot_nt(gather_blocks(v_ref, names), backs)
        back_values = dot_nn(shares.astype(bf16), backs)
        back_scores = (shares * (back_shares - inner)).astype(bf16)
        back_keys = dot_nn(back_scores, queries)
        q_scratch[rows, :] += join_halves(dot_tn(back_scores, keys))
        for slot in range(SLOTS):
            part = slice(slot * BLOCK, (slot + 1) * BLOCK)
            v_scratch[block_rows(names[slot]), :] += back_values[part]
            k_scratch[block_rows(names[slot]), :] += back_keys[part]

    def body(step, carry):
        for within in range(unroll):
            one(step * unroll + within)
        return carry

    lax.fori_loop(0, items // unroll, body, 0)
    back_q_ref[...] = (q_scratch[...] * HEAD_DIM ** (-0.5)).astype(bf16)
    back_k_ref[...] = k_scratch[...].astype(bf16)
    back_v_ref[...] = v_scratch[...].astype(bf16)


def attend_back(plan, length, flip, pair, q, k, v, back, context, logsum):
    query_names, key_names, bias_names, _ = plan
    query_rows = q.shape[0]
    tokens = k.shape[0]
    query_blocks = query_rows // BLOCK
    q_in = pl.BlockSpec((query_rows, 128), lambda step, *_: (0, pair))
    k_in = pl.BlockSpec((tokens, 128), lambda step, *_: (0, pair))
    q_out = pl.BlockSpec((query_rows, 128), lambda step, *_: (0, 0))
    k_out = pl.BlockSpec((tokens, 128), lambda step, *_: (0, 0))
    return pl.pallas_call(
        partial(backward_kernel, unroll=8, items=query_names.shape[0]),
        grid_spec=pltpu.PrefetchScalarGridSpec(
            num_scalar_prefetch=5,
            grid=(1,),
            in_specs=[
                q_in, k_in, k_in, q_in, q_in,
                pl.BlockSpec((1, query_blocks, 128), lambda step, *_: (pair, 0, 0)),
            ],
            out_specs=[q_out, k_out, k_out],
            scratch_shapes=[
                pltpu.VMEM((tokens + BLOCK, 128), f32),
                pltpu.VMEM((query_rows, 128), f32),
                pltpu.VMEM((tokens, 128), f32),
                pltpu.VMEM((tokens, 128), f32),
            ],
        ),
        out_shape=[
            jax.ShapeDtypeStruct((query_rows, 128), bf16),
            jax.ShapeDtypeStruct((tokens, 128), bf16),
            jax.ShapeDtypeStruct((tokens, 128), bf16),
        ],
        compiler_params=pltpu.CompilerParams(vmem_limit_bytes=40 << 20),
        cost_estimate=pl.CostEstimate(flops=10**9, bytes_accessed=10**6, transcendentals=10**5),
        name="attend_backward",
    )(query_names, key_names, bias_names, length, flip, q, k, v, back, context, logsum)


def project_kernel(core, x_ref, x_near_ref, w_q, w_k, w_v, b_q, b_v, q_ref, k_ref, v_ref):
    step = pl.program_id(0)

    def project(tile):
        q = (dot_nn(tile, w_q[...]) + b_q[...]).astype(bf16)
        q_ref[...] = q * jnp.asarray(HEAD_DIM ** (-0.5), bf16)
        k_ref[...] = dot_nn(tile, w_k[...]).astype(bf16)
        v_ref[...] = (dot_nn(tile, w_v[...]) + b_v[...]).astype(bf16)

    @pl.when(step < pl.num_programs(0) // 2)
    def _():
        project(x_ref[...])

    @pl.when(step >= pl.num_programs(0) // 2)
    def _():
        project(x_near_ref[...])


def project_far_kernel(core, x_ref, x_near_ref, w_k, w_v, b_v, k_old, v_old, k_ref, v_ref):
    step = pl.program_id(0)

    def project(tile):
        k_ref[...] = dot_nn(tile, w_k[...]).astype(bf16)
        v_ref[...] = (dot_nn(tile, w_v[...]) + b_v[...]).astype(bf16)

    @pl.when(step < pl.num_programs(0) // 2)
    def _():
        project(x_ref[...])

    @pl.when(step >= pl.num_programs(0) // 2)
    def _():
        project(x_near_ref[...])


TILE = 512


def piece_spec(piece, per, width):
    return pl.BlockSpec((TILE, width), lambda step, *_: (jnp.clip(step - piece * per, 0, per - 1), 0))


def own_weight(which):
    return pl.BlockSpec((D, D // 2), lambda step, core, *_: (0, 2 * which + core[0]))


def own_bias():
    return pl.BlockSpec((1, D // 2), lambda step, core, *_: (0, core[0]))


def project_chip(core, x, x_near, qkv_weight, query_bias, value_bias):
    rows = x.shape[0]
    half = D // 2
    per = rows // TILE
    out = pl.BlockSpec((TILE, half), lambda step, *_: (step, 0))
    return pl.pallas_call(
        project_kernel,
        grid_spec=pltpu.PrefetchScalarGridSpec(
            num_scalar_prefetch=1,
            grid=(2 * per,),
            in_specs=[piece_spec(0, per, D), piece_spec(1, per, D)]
            + [own_weight(0), own_weight(1), own_weight(2), own_bias(), own_bias()],
            out_specs=[out, out, out],
        ),
        out_shape=[
            jax.ShapeDtypeStruct((2 * rows, half), bf16),
            jax.ShapeDtypeStruct((4 * rows, half), bf16),
            jax.ShapeDtypeStruct((4 * rows, half), bf16),
        ],
        compiler_params=pltpu.CompilerParams(vmem_limit_bytes=32 << 20),
        cost_estimate=pl.CostEstimate(flops=4 * 10**9, bytes_accessed=10**7, transcendentals=0),
        name="project_chip",
    )(core, x, x_near, qkv_weight, qkv_weight, qkv_weight, query_bias, value_bias)


def project_far(core, x_far, x_far_near, qkv_weight, value_bias, k, v):
    rows = x_far.shape[0]
    half = D // 2
    per = rows // TILE
    out = pl.BlockSpec((TILE, half), lambda step, *_: (2 * per + step, 0))
    kept = pl.BlockSpec(memory_space=pl.ANY)
    return pl.pallas_call(
        project_far_kernel,
        grid_spec=pltpu.PrefetchScalarGridSpec(
            num_scalar_prefetch=1,
            grid=(2 * per,),
            in_specs=[piece_spec(0, per, D), piece_spec(1, per, D)]
            + [own_weight(1), own_weight(2), own_bias(), kept, kept],
            out_specs=[out, out],
        ),
        out_shape=[jax.ShapeDtypeStruct(k.shape, bf16), jax.ShapeDtypeStruct(v.shape, bf16)],
        input_output_aliases={6: 0, 7: 1},
        compiler_params=pltpu.CompilerParams(vmem_limit_bytes=32 << 20),
        cost_estimate=pl.CostEstimate(flops=3 * 10**9, bytes_accessed=10**7, transcendentals=0),
        name="project_far",
    )(core, x_far, x_far_near, qkv_weight, qkv_weight, value_bias, k, v)


def gelu_pair(x):
    t = 1.0 / (1.0 + (0.3275911 * 0.5**0.5) * jnp.abs(x))
    bell = jnp.exp(-0.5 * x * x)
    poly = 0.7107068705 + t * (-0.7265760135 + t * 0.5307027145)
    tail = t * (0.127414796 + t * (-0.142248368 + t * poly)) * bell
    cdf = jnp.where(x < 0, tail, 1.0 - tail)
    return x * cdf, cdf + x * bell * 0.3989422804014327


def norm_parts(value):
    center = value - jnp.mean(value, axis=-1, keepdims=True)
    spread = jnp.mean(center * center, axis=-1, keepdims=True)
    scale = lax.rsqrt(spread + norm_epsilon)
    return center * scale, scale


def norm_back(slope, normed, scale):
    along = jnp.mean(slope * normed, axis=-1, keepdims=True)
    return scale * (slope - jnp.mean(slope, axis=-1, keepdims=True) - normed * along)


def column_sum(value):
    return jnp.sum(value, axis=0, keepdims=True)


PIECES = 32
STAGES = 8
VECTOR_ROWS = 256


class Packer:
    def __init__(self, places, stage, sems, keep, send, first_row, rows, pieces):
        self.places, self.stage, self.sems = places, stage, sems
        self.keep, self.send = keep, send
        self.first_row, self.rows, self.pieces = first_row, rows, pieces

    def target(self, array, place):
        return array.at[place, pl.ds(self.first_row, self.rows)]

    def wait(self, slot):
        pltpu.make_async_copy(self.stage.at[slot], self.target(self.keep, 0), self.sems.at[slot]).wait()

    def put(self, number, color, piece, value):
        slot = lax.rem(number, STAGES)

        @pl.when(number >= STAGES)
        def _():
            self.wait(slot)

        self.stage[slot] = value.astype(bf16)
        kept = self.pieces // 2
        relative = piece ^ self.places[color]
        place = color * kept + lax.rem(relative, kept)

        @pl.when(relative < kept)
        def _():
            pltpu.make_async_copy(self.stage.at[slot], self.target(self.keep, place), self.sems.at[slot]).start()

        @pl.when(relative >= kept)
        def _():
            pltpu.make_async_copy(self.stage.at[slot], self.target(self.send, place), self.sems.at[slot]).start()

    def finish(self):
        for slot in range(STAGES):
            self.wait(slot)


def proj_loads(proj_hbm, proj_w, core, sems):
    half = D // 2
    hc = core[0]
    return [
        pltpu.make_async_copy(proj_hbm.at[pl.ds(hc * half, half)], proj_w.at[pl.ds(0, half)], sems.at[0]),
        pltpu.make_async_copy(proj_hbm.at[pl.ds((1 - hc) * half, half)], proj_w.at[pl.ds(half, half)], sems.at[1]),
    ]


def middle_forward_kernel(
    places, core,
    own_ref, other_ref, x_ref, cot_ref, vector_ref, expand_bias_ref, proj_hbm, expand_hbm, shrink_hbm,
    output_ref, back_two_ref, normed_ref, scale_ref, slope_ref, vector_g, keep_ref, send_ref,
    proj_w, expand_w, shrink_w, active_s, shrink_g, stage, weight_sems, sems, *, chunk,
):
    step = pl.program_id(0)
    ff = expand_w.shape[1]
    chunks = ff // chunk
    loads = proj_loads(proj_hbm, proj_w, core, weight_sems) + [
        pltpu.make_async_copy(expand_hbm, expand_w, weight_sems.at[2]),
        pltpu.make_async_copy(shrink_hbm, shrink_w, weight_sems.at[3]),
    ]

    @pl.when(step == 0)
    def _():
        for load in loads:
            load.start()
        shrink_g[...] = jnp.zeros_like(shrink_g)
        vector_g[...] = jnp.zeros_like(vector_g)
        loads[0].wait()
        loads[1].wait()

    def vector(row):
        return vector_ref[pl.ds(row, 1), :]

    context = jnp.concatenate([own_ref[...], other_ref[...]], axis=1)
    resid = x_ref[...].astype(f32) + dot_nn(context, proj_w[...]) + vector(0)
    normed_one, scale_one = norm_parts(resid)
    normed_ref[...] = normed_one
    scale_ref[...] = jnp.broadcast_to(scale_one, scale_ref.shape)
    hidden = normed_one * vector(1) + vector(2)
    low = hidden.astype(bf16)
    resid_two = hidden + vector(3)

    @pl.when(step == 0)
    def _():
        loads[2].wait()
        loads[3].wait()

    for part in range(chunks):
        cols = slice(part * chunk, (part + 1) * chunk)
        inner = dot_nn(low, expand_w[:, cols]) + expand_bias_ref[:, cols]
        active, slope = gelu_pair(inner)
        active = active.astype(bf16)
        active_s[:, cols] = active
        slope_ref[:, cols] = slope.astype(bf16)
        resid_two = resid_two + dot_nn(active, shrink_w[cols, :])
    normed_two, scale_two = norm_parts(resid_two)
    output_ref[...] = (normed_two * vector(4) + vector(5)).astype(bf16)
    cot = cot_ref[...].astype(f32)
    back_two = norm_back(vector(4) * cot, normed_two, scale_two)
    back_two_ref[...] = back_two
    low_two = back_two.astype(bf16)
    vector_g[3:4, :] += column_sum(low_two.astype(f32))
    vector_g[4:5, :] += column_sum(cot * normed_two)
    vector_g[5:6, :] += column_sum(cot)
    rows = ff // (2 * PIECES)
    packer = Packer(places, stage, sems, keep_ref, send_ref, 0, rows, PIECES)
    per = chunk // rows
    for part in range(chunks):
        cols = slice(part * chunk, (part + 1) * chunk)
        shrink_g[cols, :] += dot_tn(active_s[:, cols], low_two)

        @pl.when(step == pl.num_programs(0) - 1)
        def _():
            def put(within, carry):
                number = part * per + within
                value = shrink_g[pl.ds(pl.multiple_of(number * rows, rows), rows), :]
                packer.put(number, (part * per) // PIECES, lax.rem(number, PIECES), value)
                return carry

            lax.fori_loop(0, per, put, 0)

    @pl.when(step == pl.num_programs(0) - 1)
    def _():
        packer.finish()


def row_spec(tile, width):
    return pl.BlockSpec((tile, width), lambda step, *_: (step, 0))


def whole_spec(shape):
    return pl.BlockSpec(shape, lambda step, *_: (0, 0))


def middle_forward(places, core, own, other, x, cot, vectors, expand_bias, proj_weight, expand_weight, shrink_weight):
    rows = x.shape[0]
    ff = expand_weight.shape[1]
    half = D // 2
    tile = 256
    piece_rows = ff // (2 * PIECES)
    kept = pl.BlockSpec(memory_space=pl.ANY)
    packed = jax.ShapeDtypeStruct((PIECES, piece_rows, D), bf16)
    return pl.pallas_call(
        partial(middle_forward_kernel, chunk=D),
        grid_spec=pltpu.PrefetchScalarGridSpec(
            num_scalar_prefetch=2,
            grid=(rows // tile,),
            in_specs=[row_spec(tile, half)] * 2
            + [row_spec(tile, D)] * 2
            + [whole_spec(vectors.shape), whole_spec(expand_bias.shape), kept, kept, kept],
            out_specs=[row_spec(tile, D)] * 3
            + [row_spec(tile, 128), row_spec(tile, ff), whole_spec((8, D)), kept, kept],
            scratch_shapes=[
                pltpu.VMEM((D, D), bf16),
                pltpu.VMEM((D, ff), bf16),
                pltpu.VMEM((ff, D), bf16),
                pltpu.VMEM((tile, ff), bf16),
                pltpu.VMEM((ff, D), f32),
                pltpu.VMEM((STAGES, piece_rows, D), bf16),
                pltpu.SemaphoreType.DMA((4,)),
                pltpu.SemaphoreType.DMA((STAGES,)),
            ],
        ),
        out_shape=[
            jax.ShapeDtypeStruct((rows, D), bf16),
            jax.ShapeDtypeStruct((rows, D), f32),
            jax.ShapeDtypeStruct((rows, D), f32),
            jax.ShapeDtypeStruct((rows, 128), f32),
            jax.ShapeDtypeStruct((rows, ff), bf16),
            jax.ShapeDtypeStruct((8, D), f32),
            packed,
            packed,
        ],
        compiler_params=pltpu.CompilerParams(vmem_limit_bytes=60 << 20),
        cost_estimate=pl.CostEstimate(flops=10**9, bytes_accessed=10**7, transcendentals=10**6),
        name="middle_forward",
    )(places, core, own, other, x, cot, vectors, expand_bias, proj_weight, expand_weight, shrink_weight)


def middle_back_kernel(
    places, core,
    own_ref, other_ref, back_two_ref, normed_ref, scale_ref, slope_ref, vector_ref, sums_ref,
    proj_hbm, expand_hbm, shrink_hbm,
    back_one_ref, back_own_ref, back_other_ref, keep_ref, send_ref,
    proj_w, expand_w, shrink_w, expand_g, proj_g, vector_g, bias_g, stage, extra_stage, weight_sems, sems, extra_sems,
    *, chunk,
):
    step = pl.program_id(0)
    last = step == pl.num_programs(0) - 1
    half = D // 2
    ff = expand_w.shape[1]
    chunks = ff // chunk
    loads = proj_loads(proj_hbm, proj_w, core, weight_sems) + [
        pltpu.make_async_copy(expand_hbm, expand_w, weight_sems.at[2]),
        pltpu.make_async_copy(shrink_hbm, shrink_w, weight_sems.at[3]),
    ]

    @pl.when(step == 0)
    def _():
        for load in reversed(loads):
            load.start()
        for total in (expand_g, proj_g, bias_g):
            total[...] = jnp.zeros_like(total)
        vector_g[...] = sums_ref[...]
        for load in reversed(loads):
            load.wait()

    def vector(row):
        return vector_ref[pl.ds(row, 1), :]

    context = jnp.concatenate([own_ref[...], other_ref[...]], axis=1)
    normed_one = normed_ref[...]
    low = (normed_one * vector(1) + vector(2)).astype(bf16)
    back = back_two_ref[...]
    low_two = back.astype(bf16)
    rows = ff // (2 * PIECES)
    packer = Packer(places, stage, sems, keep_ref, send_ref, 0, rows, PIECES)
    per = D // rows
    wide = ff // chunk
    for part in range(chunks):
        cols = slice(part * chunk, (part + 1) * chunk)
        back_inner = (dot_nt(low_two, shrink_w[cols, :]) * slope_ref[:, cols].astype(f32)).astype(bf16)
        bias_g[:, cols] += column_sum(back_inner.astype(f32))
        expand_g[:, cols] += dot_tn(low, back_inner)
        back = back + dot_nt(back_inner, expand_w[:, cols])

        @pl.when(last)
        def _():
            def put(down, carry):
                number = down * wide + part
                value = expand_g[pl.ds(pl.multiple_of(down * rows, rows), rows), cols]
                packer.put(part * per + down, number // PIECES, lax.rem(number, PIECES), value)
                return carry

            lax.fori_loop(0, per, put, 0)

    vector_g[1:2, :] += column_sum(back * normed_one)
    vector_g[2:3, :] += column_sum(back)
    back_one = norm_back(vector(1) * back, normed_one, scale_ref[:, 0:1])
    back_one_ref[...] = back_one
    low_one = back_one.astype(bf16)
    vector_g[0:1, :] += column_sum(low_one.astype(f32))
    proj_g[:D, :] += dot_tn(context, low_one)
    back_context = dot_nt(low_one, proj_w[...]).astype(bf16)
    back_own_ref[...] = back_context[:, :half]
    back_other_ref[...] = back_context[:, half:]

    @pl.when(last)
    def _():
        proj_g[D:, :] = jnp.zeros((proj_g.shape[0] - D, D), f32)
        proj_g[D : D + 8, :] = vector_g[...]
        for part in range(ff // D):
            proj_g[D + 8 + part : D + 9 + part, :] = bias_g[:, part * D : (part + 1) * D]
        extra = proj_g.shape[0] // (2 * PIECES)
        half_chunks = half // extra
        extra_packer = Packer(places, extra_stage, extra_sems, keep_ref, send_ref, rows, extra, PIECES)

        def put(number, carry):
            turned = lax.rem(number + half_chunks * core[0], 2 * half_chunks)
            source = jnp.where(number < 2 * half_chunks, turned, number)
            value = proj_g[pl.ds(pl.multiple_of(source * extra, extra), extra), :]
            extra_packer.put(number, number // PIECES, lax.rem(number, PIECES), value)
            return carry

        lax.fori_loop(0, 2 * PIECES, put, 0)
        packer.finish()
        extra_packer.finish()


def middle_back(
    places, core, own, other, back_two, normed, scale, slope, vectors, sums, proj_weight, expand_weight, shrink_weight
):
    rows = own.shape[0] // 2
    ff = expand_weight.shape[1]
    half = D // 2
    tile = 256
    piece_rows = ff // (2 * PIECES)
    extra_rows = (D + VECTOR_ROWS) // (2 * PIECES)
    kept = pl.BlockSpec(memory_space=pl.ANY)
    packed = jax.ShapeDtypeStruct((PIECES, piece_rows + extra_rows, D), bf16)
    return pl.pallas_call(
        partial(middle_back_kernel, chunk=D),
        grid_spec=pltpu.PrefetchScalarGridSpec(
            num_scalar_prefetch=2,
            grid=(rows // tile,),
            in_specs=[row_spec(tile, half)] * 2
            + [row_spec(tile, D)] * 2
            + [row_spec(tile, 128), row_spec(tile, ff), whole_spec(vectors.shape), whole_spec((8, D)), kept, kept, kept],
            out_specs=[row_spec(tile, D), row_spec(tile, half), row_spec(tile, half), kept, kept],
            scratch_shapes=[
                pltpu.VMEM((D, D), bf16),
                pltpu.VMEM((D, ff), bf16),
                pltpu.VMEM((ff, D), bf16),
                pltpu.VMEM((D, ff), f32),
                pltpu.VMEM((D + VECTOR_ROWS, D), f32),
                pltpu.VMEM((8, D), f32),
                pltpu.VMEM((1, ff), f32),
                pltpu.VMEM((STAGES, piece_rows, D), bf16),
                pltpu.VMEM((STAGES, extra_rows, D), bf16),
                pltpu.SemaphoreType.DMA((4,)),
                pltpu.SemaphoreType.DMA((STAGES,)),
                pltpu.SemaphoreType.DMA((STAGES,)),
            ],
        ),
        out_shape=[
            jax.ShapeDtypeStruct((rows, D), f32),
            jax.ShapeDtypeStruct((rows, half), bf16),
            jax.ShapeDtypeStruct((rows, half), bf16),
            packed,
            packed,
        ],
        compiler_params=pltpu.CompilerParams(vmem_limit_bytes=60 << 20),
        cost_estimate=pl.CostEstimate(flops=10**9, bytes_accessed=10**7, transcendentals=0),
        name="middle_back",
    )(places, core, own, other, back_two, normed, scale, slope, vectors, sums, proj_weight, expand_weight, shrink_weight)


def input_far_kernel(core, *refs):
    w_k, w_v, out = refs[0], refs[1], refs[-1]
    arrays = refs[2:-1]
    pairs = len(arrays) // 2
    back_k = jnp.concatenate([ref[...] for ref in arrays[:pairs]], axis=1)
    back_v = jnp.concatenate([ref[...] for ref in arrays[pairs:]], axis=1)
    out[...] = (dot_nt(back_k, w_k[...]) + dot_nt(back_v, w_v[...])).astype(bf16)


def input_far(core, qkv_weight, back_ks, back_vs, rows):
    first = 2 * rows // TILE
    token = pl.BlockSpec((TILE, 128), lambda step, *_: (first + step, 0))
    arrays = list(back_ks) + list(back_vs)
    return pl.pallas_call(
        input_far_kernel,
        grid_spec=pltpu.PrefetchScalarGridSpec(
            num_scalar_prefetch=1,
            grid=(2 * rows // TILE,),
            in_specs=[own_weight(1), own_weight(2)] + [token] * len(arrays),
            out_specs=pl.BlockSpec((TILE, D), lambda step, *_: (step, 0)),
        ),
        out_shape=jax.ShapeDtypeStruct((2 * rows, D), bf16),
        compiler_params=pltpu.CompilerParams(vmem_limit_bytes=32 << 20),
        cost_estimate=pl.CostEstimate(flops=3 * 10**9, bytes_accessed=10**7, transcendentals=0),
        name="input_far",
    )(core, qkv_weight, qkv_weight, *arrays)


QKV_PIECES = 16


def joined_kernel(places, core, *refs, tiles, pairs):
    x_refs = refs[:4]
    arrays = refs[4 : 4 + 3 * pairs]
    first_ref, second_ref = refs[4 + 3 * pairs : 6 + 3 * pairs]
    total, sums = refs[6 + 3 * pairs :]
    step = pl.program_id(0)
    half = D // 2
    per = tiles // 4

    @pl.when(step == 0)
    def _():
        total[...] = jnp.zeros_like(total)
        sums[...] = jnp.zeros_like(sums)

    def joined(first, last):
        return jnp.concatenate([ref[...] for ref in arrays[first * pairs : last * pairs]], axis=1)

    for piece in range(4):

        @pl.when((step >= piece * per) & (step < (piece + 1) * per))
        def _():
            first = 0 if piece < 2 else 1
            back = joined(first, 3)
            total[:, first * half : 3 * half] += dot_tn(x_refs[piece][...], back)
            sums[0:1, first * half :] += column_sum(back.astype(f32))

    @pl.when(step == tiles - 1)
    def _():
        rows = D // QKV_PIECES
        q_sums = jnp.transpose(jnp.broadcast_to(sums[0:1, :half], (128, half)))
        v_sums = jnp.transpose(jnp.broadcast_to(sums[0:1, 2 * half :], (128, half)))
        total[:half, 3 * half :] = q_sums
        total[half:, 3 * half :] = v_sums
        width = first_ref.shape[2]
        for piece in range(QKV_PIECES):
            part = pl.ds(pl.multiple_of((piece ^ places[0]) * rows, rows), rows)
            first_ref[piece] = total[part, :width].astype(bf16)
            part = pl.ds(pl.multiple_of((piece ^ places[1]) * rows, rows), rows)
            second_ref[piece] = total[part, width:].astype(bf16)


def joined_grads(places, core, xs, back_qs, back_ks, back_vs):
    rows = xs[0].shape[0]
    pairs = len(back_qs)
    per = rows // TILE
    tiles = 4 * per
    width = D // 2 + 256
    token = pl.BlockSpec((TILE, 128), lambda step, *_: (step, 0))
    query = pl.BlockSpec((TILE, 128), lambda step, *_: (jnp.minimum(step, 2 * per - 1), 0))
    packed = pl.BlockSpec((QKV_PIECES, D // QKV_PIECES, width), lambda step, *_: (0, 0, 0))
    packed_shape = jax.ShapeDtypeStruct((QKV_PIECES, D // QKV_PIECES, width), bf16)
    return pl.pallas_call(
        partial(joined_kernel, tiles=tiles, pairs=pairs),
        grid_spec=pltpu.PrefetchScalarGridSpec(
            num_scalar_prefetch=2,
            grid=(tiles,),
            in_specs=[piece_spec(piece, per, D) for piece in range(4)] + [query] * pairs + [token] * (2 * pairs),
            out_specs=[packed, packed],
            scratch_shapes=[pltpu.VMEM((D, 2 * width), f32), pltpu.VMEM((8, 3 * D // 2), f32)],
        ),
        out_shape=[packed_shape, packed_shape],
        compiler_params=pltpu.CompilerParams(vmem_limit_bytes=48 << 20),
        cost_estimate=pl.CostEstimate(flops=10**9, bytes_accessed=10**7, transcendentals=0),
        name="joined_grads",
    )(places, core, *xs, *back_qs, *back_ks, *back_vs)


def input_near_kernel(core, *refs):
    w_q, w_k, w_v, out = refs[0], refs[1], refs[2], refs[-1]
    arrays = refs[3:-1]
    pairs = len(arrays) // 3

    def joined(which):
        return jnp.concatenate([ref[...] for ref in arrays[which * pairs : (which + 1) * pairs]], axis=1)

    out[...] = (dot_nt(joined(0), w_q[...]) + dot_nt(joined(1), w_k[...]) + dot_nt(joined(2), w_v[...])).astype(bf16)


def input_near(core, qkv_weight, back_qs, back_ks, back_vs):
    rows = back_qs[0].shape[0]
    token = pl.BlockSpec((TILE, 128), lambda step, *_: (step, 0))
    arrays = list(back_qs) + list(back_ks) + list(back_vs)
    return pl.pallas_call(
        input_near_kernel,
        grid_spec=pltpu.PrefetchScalarGridSpec(
            num_scalar_prefetch=1,
            grid=(rows // TILE,),
            in_specs=[own_weight(0), own_weight(1), own_weight(2)] + [token] * len(arrays),
            out_specs=pl.BlockSpec((TILE, D), lambda step, *_: (step, 0)),
        ),
        out_shape=jax.ShapeDtypeStruct((rows, D), bf16),
        compiler_params=pltpu.CompilerParams(vmem_limit_bytes=32 << 20),
        cost_estimate=pl.CostEstimate(flops=10**9, bytes_accessed=10**7, transcendentals=0),
        name="input_near",
    )(core, qkv_weight, qkv_weight, qkv_weight, *arrays)


def unpack_shrink_body(places, first_own, first_other, second_own, second_other, out):
    step = pl.program_id(0)
    within = lax.rem(step, PIECES)
    for color, (own, other) in enumerate(((first_own, first_other), (second_own, second_other))):

        @pl.when((step // PIECES == color) & (within < PIECES // 2))
        def _():
            out[...] = own[0].astype(f32)

        @pl.when((step // PIECES == color) & (within >= PIECES // 2))
        def _():
            out[...] = other[0].astype(f32)


def colored(color, part, rows):
    kept = PIECES // 2

    def index(step, *_):
        return (jnp.clip(step - color * PIECES - part * kept, 0, kept - 1), 0, 0)

    return pl.BlockSpec((1, rows, D), index)


def piece_number(step, places):
    color = step // PIECES
    return color * PIECES + (lax.rem(step, PIECES) ^ places[color])


def unpack_shrink(places, first_own, first_other, second_own, second_other):
    rows = first_own.shape[1]
    return pl.pallas_call(
        unpack_shrink_body,
        grid_spec=pltpu.PrefetchScalarGridSpec(
            num_scalar_prefetch=1,
            grid=(2 * PIECES,),
            in_specs=[colored(color, part, rows) for color in range(2) for part in range(2)],
            out_specs=pl.BlockSpec((rows, D), lambda step, places: (piece_number(step, places), 0)),
        ),
        out_shape=jax.ShapeDtypeStruct((2 * PIECES * rows, D), f32),
        compiler_params=pltpu.CompilerParams(vmem_limit_bytes=32 << 20),
        cost_estimate=pl.CostEstimate(flops=10**6, bytes_accessed=10**6, transcendentals=0),
        name="unpack_shrink",
    )(places, first_own, first_other, second_own, second_other)


def unpack_expand_body(places, first_own, first_other, second_own, second_other, expand_ref, proj_ref, *, rows):
    step = pl.program_id(0)
    within = lax.rem(step, PIECES)

    def put(source):
        expand_ref[...] = source[0, :rows, :].astype(f32)
        proj_ref[...] = source[0, rows:, :].astype(f32)

    for color, (own, other) in enumerate(((first_own, first_other), (second_own, second_other))):

        @pl.when((step // PIECES == color) & (within < PIECES // 2))
        def _():
            put(own)

        @pl.when((step // PIECES == color) & (within >= PIECES // 2))
        def _():
            put(other)


def unpack_expand(places, first_own, first_other, second_own, second_other, ff):
    piece_rows = first_own.shape[1]
    rows = ff // (2 * PIECES)
    extra = piece_rows - rows
    wide = ff // D

    def place(step, places):
        number = piece_number(step, places)
        return (number // wide, lax.rem(number, wide))

    return pl.pallas_call(
        partial(unpack_expand_body, rows=rows),
        grid_spec=pltpu.PrefetchScalarGridSpec(
            num_scalar_prefetch=1,
            grid=(2 * PIECES,),
            in_specs=[colored(color, part, piece_rows) for color in range(2) for part in range(2)],
            out_specs=[
                pl.BlockSpec((rows, D), place),
                pl.BlockSpec((extra, D), lambda step, places: (piece_number(step, places), 0)),
            ],
        ),
        out_shape=[
            jax.ShapeDtypeStruct((D, ff), f32),
            jax.ShapeDtypeStruct((2 * PIECES * extra, D), f32),
        ],
        compiler_params=pltpu.CompilerParams(vmem_limit_bytes=32 << 20),
        cost_estimate=pl.CostEstimate(flops=10**6, bytes_accessed=10**6, transcendentals=0),
        name="unpack_expand",
    )(places, first_own, first_other, second_own, second_other)


def unpack_joined_kernel(places, core, first_own, second_own, first_other, second_other, out_ref, bias_ref):
    half = D // 2

    def put(first, second, place):
        def at(which):
            return slice(which * D + place * half, which * D + (place + 1) * half)

        out_ref[:, at(0)] = first[0, :, :half].astype(f32)
        out_ref[:, at(1)] = jnp.concatenate([first[0, :, half:], second[0, :, :128]], axis=1).astype(f32)
        out_ref[:, at(2)] = second[0, :, 128 : 128 + half].astype(f32)
        bias_ref[:, place * 128 : (place + 1) * 128] = second[0, :, 128 + half :].astype(f32)

    @pl.when(core[0] == 0)
    def _():
        put(first_own, second_own, 0)
        put(first_other, second_other, 1)

    @pl.when(core[0] != 0)
    def _():
        put(first_own, second_own, 1)
        put(first_other, second_other, 0)


def unpack_joined(places, core, first_own, second_own, first_other, second_other):
    count, rows, width = first_own.shape
    first = pl.BlockSpec((1, rows, width), lambda step, places, core: (step ^ places[0], 0, 0))
    second = pl.BlockSpec((1, rows, width), lambda step, places, core: (step ^ places[1], 0, 0))
    return pl.pallas_call(
        unpack_joined_kernel,
        grid_spec=pltpu.PrefetchScalarGridSpec(
            num_scalar_prefetch=2,
            grid=(count,),
            in_specs=[first, second, first, second],
            out_specs=[
                pl.BlockSpec((rows, 3 * D), lambda step, *_: (step, 0)),
                pl.BlockSpec((rows, 256), lambda step, *_: (step, 0)),
            ],
        ),
        out_shape=[jax.ShapeDtypeStruct((D, 3 * D), f32), jax.ShapeDtypeStruct((D, 256), f32)],
        compiler_params=pltpu.CompilerParams(vmem_limit_bytes=32 << 20),
        cost_estimate=pl.CostEstimate(flops=10**6, bytes_accessed=10**7, transcendentals=0),
        name="unpack_joined",
    )(places, core, first_own, second_own, first_other, second_other)


def swap(value, axis, bit=1):
    size = lax.axis_size(axis)
    return lax.ppermute(value, axis, [(place, place ^ bit) for place in range(size)])


def place_of(order):
    number = jnp.zeros((), jnp.int32)
    for axis, bit in order:
        number = 2 * number + ((lax.axis_index(axis) & bit) // bit).astype(jnp.int32)
    return number


def add_low(left, right):
    return (left.astype(f32) + right.astype(f32)).astype(bf16)


class Chain:
    def __init__(self, order, keep, arrived=None):
        self.order, self.keep, self.arrived = order, keep, arrived
        self.at = 0
        self.gathered = None

    def send(self):
        steps = len(self.order)
        if self.at < steps:
            half = self.keep.shape[0] // 2
            low, high = self.keep[:half], self.keep[half:]
            if self.arrived is not None:
                low = add_low(low, self.arrived[:half])
                high = add_low(high, self.arrived[half:])
            self.keep = low
            return high
        if self.at == steps:
            total = add_low(self.keep, self.arrived)
            bit = 8
            while bit < lax.axis_size("dp"):
                total = add_low(total, swap(total, "dp", bit))
                bit *= 2
            self.gathered = total
        else:
            self.gathered = jnp.concatenate([self.gathered, self.arrived], axis=0)
        return self.gathered

    def move(self, value):
        steps = len(self.order)
        if self.at >= steps:
            self.gathered = value
        if self.at < 2 * steps:
            axis, bit = self.order[self.at if self.at < steps else 2 * steps - 1 - self.at]
        else:
            axis, bit = "hc", 1
        self.arrived = swap(value, axis, bit)
        self.at += 1


def advance(chains, tied=()):
    sends = [chain.send() for chain in chains]
    *sends, = lax.optimization_barrier(tuple(sends) + tuple(tied))
    for chain, value in zip(chains, sends):
        chain.move(value)
    return sends[len(chains) :]


def ready(*values):
    return lax.optimization_barrier(values)


def per_device(
    inputs, doc_lengths, random_blocks, qkv_weight, query_bias, value_bias, proj_weight, proj_bias,
    first_gain, first_shift, expand_weight, expand_bias, shrink_weight, shrink_bias,
    second_gain, second_shift, cotangent,
):
    hx = lax.axis_index("hx")
    hc = lax.axis_index("hc")
    docs, rows, _ = inputs.shape
    assert docs == 1 and lax.axis_size("hx") == 2 and lax.axis_size("hc") == 2
    half = D // 2
    ff = expand_weight.shape[1]
    pairs = half // 128
    x = inputs.reshape(rows, D)
    x_far = swap(x, "hx")
    x_near = swap(x, "hc")
    row_blocks = rows // BLOCK
    flip = (hx * 2 + hc).astype(jnp.int32) * row_blocks
    plan = block_plan(doc_lengths[0], random_blocks[0], flip, 2 * row_blocks)
    flip = flip.reshape(1)
    core = hc.astype(jnp.int32).reshape(1)
    first_order = [("dp", 1), ("dp", 2), ("dp", 4), ("hx", 1)]
    second_order = [("hx", 1), ("dp", 1), ("dp", 2), ("dp", 4)]
    core_order = [("hc", 1)]
    places = jnp.stack([place_of(core_order + first_order), place_of(core_order + second_order)])
    chip_places = jnp.stack([place_of(first_order), place_of(second_order)])
    empty = jnp.zeros((D,), bf16)
    vectors = jnp.stack(
        [proj_bias, first_gain, first_shift, shrink_bias, second_gain, second_shift, empty, empty]
    ).astype(f32)
    bias_q = query_bias.astype(f32).reshape(1, D)
    bias_v = value_bias.astype(f32).reshape(1, D)
    kept = PIECES // 2

    def two_chains(keep, arrived):
        return [
            Chain(first_order, keep[:kept], arrived[:kept]),
            Chain(second_order, keep[kept:], arrived[kept:]),
        ]

    q, k, v = project_chip(core, x, x_near, qkv_weight, bias_q, bias_v)
    x_far, q = ready(x_far, q)
    x_far_near = swap(x_far, "hc")
    k, v = project_far(core, x_far, x_far_near, qkv_weight, bias_v, k, v)
    context, logsum = attend(plan, doc_lengths, flip, q, k, v)
    other_context = swap(context[rows:], "hc")
    output, back_two, normed, scale, slope, sums, shrink_keep, shrink_send = middle_forward(
        places, core, context, other_context, x, cotangent.reshape(rows, D), vectors,
        expand_bias.astype(f32).reshape(1, ff), proj_weight, expand_weight, shrink_weight,
    )
    shrink = two_chains(shrink_keep, swap(shrink_send, "hc"))
    (back_two,) = advance(shrink, (back_two,))
    back_one, back_own, back_other, expand_keep, expand_send = middle_back(
        places, core, context, other_context, back_two, normed, scale, slope, vectors, sums,
        proj_weight, expand_weight, shrink_weight,
    )
    back = jnp.concatenate([back_own, swap(back_other, "hc")], axis=0)
    back, expand_send = advance(shrink, (back, expand_send))
    expand_arrived = swap(expand_send, "hc")
    grads = []

    def attend_pair(pair, back):
        grads.append(attend_back(plan, doc_lengths, flip, pair, q, k, v, back, context, logsum))

    attend_pair(0, back)
    back, expand_keep, expand_arrived, _ = ready(back, expand_keep, expand_arrived, grads[0][0])
    expand = two_chains(expand_keep, expand_arrived)
    (back,) = advance(shrink + expand, (back,))
    attend_pair(1, back)
    back, _ = ready(back, grads[1][0])
    (back,) = advance(shrink + expand, (back,))
    attend_pair(2, back)
    (last,) = advance(shrink + expand, (grads[2][0],))
    grads[2] = (last,) + tuple(grads[2][1:])
    back_qs, back_ks, back_vs = zip(*grads)

    joined_first, joined_second = joined_grads(
        chip_places, core, (x, x_near, x_far, x_far_near), back_qs, back_ks, back_vs
    )
    joined = [Chain(first_order, joined_first), Chain(second_order, joined_second)]
    (last,) = advance(joined + shrink + expand, (back_ks[0],))
    back_ks = (last,) + tuple(back_ks[1:])
    far = input_far(core, qkv_weight, back_ks, back_vs, rows)
    far_own = add_low(far[:rows], swap(far[rows:], "hc"))
    (far_own,) = advance(joined + shrink + expand, (far_own,))
    from_far = swap(far_own, "hx")
    far_own, last = ready(far_own, back_qs[0])
    near = input_near(core, qkv_weight, (last,) + tuple(back_qs[1:]), back_ks, back_vs)
    from_near = swap(near[rows:], "hc")

    def left(chain):
        return 2 * len(chain.order) + 1 - chain.at

    while any(left(chain) > 0 for chain in joined + shrink + expand):
        advance([chain for chain in joined + shrink + expand if left(chain) > 0])
    input_grad = back_one + near[:rows].astype(f32) + from_near.astype(f32) + from_far.astype(f32)

    def both(chains):
        return [value for chain in chains for value in (chain.gathered, chain.arrived)]

    grad_shrink = unpack_shrink(places, *both(shrink))
    grad_expand, proj_rows = unpack_expand(places, *both(expand), ff)
    first_own, first_other, second_own, second_other = both(joined)
    grad_qkv, bias = unpack_joined(chip_places, core, first_own, second_own, first_other, second_other)
    grad_proj = proj_rows[:D]
    vector = proj_rows[D:]
    grad_query_bias = jnp.concatenate([bias[:half, 0], bias[:half, 128]])
    grad_value_bias = jnp.concatenate([bias[half:, 0], bias[half:, 128]])
    grad_expand_bias = vector[8 : 8 + ff // D].reshape(ff)
    return (
        output.reshape(docs, rows, D),
        input_grad.reshape(docs, rows, D),
        grad_qkv, grad_query_bias, grad_value_bias, grad_proj, vector[0], vector[1], vector[2],
        grad_expand, grad_expand_bias, grad_shrink, vector[3], vector[4], vector[5],
    )


def solution(mesh):
    dp = mesh.shape["dp"]
    heads = mesh.shape["heads"]
    split = Mesh(mesh.devices.reshape(dp, heads // 2, 2), ("dp", "hx", "hc"))
    rows = P("dp", ("hx", "hc"), None)
    in_specs = (rows, P("dp"), P("dp", None, None)) + (P(),) * 13 + (rows,)
    out_specs = (rows, rows) + (P(),) * 13
    return jax.shard_map(
        per_device, mesh=split, in_specs=in_specs, out_specs=out_specs, check_vma=False
    )
```

```python
from functools import partial

import jax
import jax.numpy as jnp
from jax import lax
from jax.experimental import pallas as pl
from jax.experimental.pallas import tpu as pltpu
from jax.sharding import Mesh
from jax.sharding import PartitionSpec as P

D = 768
HEADS = 12
HEAD_DIM = 64
BLOCK = 64
SLOTS = 8
norm_epsilon = 1e-12
masked_score = -1e30
f32 = jnp.float32
bf16 = jnp.bfloat16


def dot_nn(left, right):
    return lax.dot_general(left, right, (((1,), (0,)), ((), ())), preferred_element_type=f32)


def dot_nt(left, right):
    return lax.dot_general(left, right, (((1,), (1,)), ((), ())), preferred_element_type=f32)


def dot_tn(left, right):
    return lax.dot_general(left, right, (((0,), (0,)), ((), ())), preferred_element_type=f32)


def layer_norm(values, scaling, offset):
    center = values - jnp.mean(values, axis=-1, keepdims=True)
    spread = jnp.mean(center * center, axis=-1, keepdims=True)
    return center * lax.rsqrt(spread + norm_epsilon) * scaling + offset


def block_plan(length, randoms, flip, query_blocks):
    blocks = randoms.shape[0]
    last = (length + BLOCK - 1) // BLOCK - 1
    places = jnp.arange(query_blocks, dtype=jnp.int32) ^ flip
    own_randoms = jnp.take_along_axis(randoms, places[:, None], axis=0)
    zero = jnp.zeros((query_blocks,), jnp.int32)
    candidates = jnp.concatenate(
        [
            jnp.stack([places - 1, places, places + 1, zero, zero + last], axis=1),
            own_randoms,
        ],
        axis=1,
    )
    usable = (candidates >= 0) & (candidates < blocks)
    same = candidates[:, :, None] == candidates[:, None, :]
    before = jnp.arange(SLOTS)[:, None] > jnp.arange(SLOTS)[None, :]
    usable = usable & ~jnp.any(same & before[None], axis=2)
    is_global = (places == 0) | (places == last)
    usable = usable & ~is_global[:, None]
    names = jnp.clip(candidates, 0, blocks - 1) ^ flip
    global_name = jnp.where((flip ^ last) < query_blocks, flip ^ last, flip)
    every = jnp.arange(blocks, dtype=jnp.int32).reshape(blocks // SLOTS, SLOTS)
    query_names = jnp.concatenate(
        [
            jnp.arange(query_blocks, dtype=jnp.int32),
            jnp.zeros((blocks // SLOTS,), jnp.int32) + global_name,
        ]
    )
    key_names = jnp.concatenate([names, every])
    bias_names = jnp.concatenate([jnp.where(usable, names, blocks), every])
    return query_names, key_names, bias_names, global_name.reshape(1)


def halves(pair):
    lane = lax.broadcasted_iota(jnp.int32, pair.shape, 1)
    zero = jnp.zeros_like(pair)
    return jnp.concatenate(
        [jnp.where(lane < HEAD_DIM, pair, zero), jnp.where(lane < HEAD_DIM, zero, pair)], axis=0
    )


def join_halves(stacked):
    lane = lax.broadcasted_iota(jnp.int32, (BLOCK, 2 * HEAD_DIM), 1)
    return jnp.where(lane < HEAD_DIM, stacked[:BLOCK], stacked[BLOCK:])


def block_rows(name):
    return pl.ds(pl.multiple_of(name * BLOCK, BLOCK), BLOCK)


def gather_blocks(ref, names):
    return jnp.concatenate([ref[block_rows(name), :] for name in names], axis=0)


def fill_length_bias(bias_scratch, length, flip):
    rows = bias_scratch.shape[0] - BLOCK
    place = lax.broadcasted_iota(jnp.int32, bias_scratch.shape, 0)
    token = (((place // BLOCK) ^ flip) * BLOCK) + place % BLOCK
    live = (token < length) & (place < rows)
    bias_scratch[...] = jnp.where(live, 0.0, masked_score)


def forward_kernel(
    key_names, bias_names, global_name, lengths, flips,
    q_ref, k_ref, v_ref, context_ref, logsum_ref, bias_scratch, score_scratch, *, unroll, query_blocks,
):
    @pl.when(pl.program_id(0) == 0)
    def _():
        fill_length_bias(bias_scratch, lengths[0], flips[0])

    def put(block, context, largest, total):
        context_ref[block_rows(block), :] = join_halves(context).astype(bf16)
        logsum_ref[0, pl.ds(block, 1), :] = largest + jnp.log(total)

    def one(block):
        queries = halves(q_ref[block_rows(block), :])
        names = [key_names[block, slot] for slot in range(SLOTS)]
        biases = [bias_names[block, slot] for slot in range(SLOTS)]
        scores = dot_nt(gather_blocks(k_ref, names), queries) + gather_blocks(bias_scratch, biases)
        largest = jnp.max(scores, axis=0, keepdims=True)
        weights = jnp.exp(scores - largest)
        total = jnp.sum(weights, axis=0, keepdims=True)
        shares = (weights * (1.0 / total)).astype(bf16)
        put(block, dot_tn(shares, gather_blocks(v_ref, names)), largest, total)

    def body(step, carry):
        for within in range(unroll):
            one(step * unroll + within)
        return carry

    lax.fori_loop(0, query_blocks // unroll, body, 0)
    block = global_name[0]
    queries = halves(q_ref[block_rows(block), :])
    tokens = k_ref.shape[0]
    chunk = SLOTS * BLOCK
    together = 4

    def score_chunk(step, largest):
        for within in range(together):
            rows = pl.ds(pl.multiple_of((step * together + within) * chunk, chunk), chunk)
            scores = dot_nt(k_ref[rows, :], queries) + bias_scratch[rows, :]
            score_scratch[rows, :] = scores
            largest = jnp.maximum(largest, jnp.max(scores, axis=0, keepdims=True))
        return largest

    steps = tokens // chunk // together
    lanes = 2 * BLOCK
    largest = lax.fori_loop(0, steps, score_chunk, jnp.full((1, lanes), masked_score, f32))

    def value_chunk(step, carry):
        total, context = carry
        for within in range(together):
            rows = pl.ds(pl.multiple_of((step * together + within) * chunk, chunk), chunk)
            weights = jnp.exp(score_scratch[rows, :] - largest)
            total = total + jnp.sum(weights, axis=0, keepdims=True)
            context = context + dot_tn(weights.astype(bf16), v_ref[rows, :])
        return total, context

    total, context = lax.fori_loop(
        0, steps, value_chunk, (jnp.zeros((1, lanes), f32), jnp.zeros((lanes, lanes), f32))
    )
    context = context * jnp.transpose(jnp.broadcast_to(1.0 / total, (lanes, lanes)))
    put(block, context, largest, total)


def attend(plan, length, flip, q, k, v):
    query_names, key_names, bias_names, global_name = plan
    query_rows, width = q.shape
    tokens = k.shape[0]
    pairs = width // 128
    query_blocks = query_rows // BLOCK
    q_spec = pl.BlockSpec((query_rows, 128), lambda pair, *_: (0, pair))
    k_spec = pl.BlockSpec((tokens, 128), lambda pair, *_: (0, pair))
    return pl.pallas_call(
        partial(forward_kernel, unroll=query_blocks, query_blocks=query_blocks),
        grid_spec=pltpu.PrefetchScalarGridSpec(
            num_scalar_prefetch=5,
            grid=(pairs,),
            in_specs=[q_spec, k_spec, k_spec],
            out_specs=[q_spec, pl.BlockSpec((1, query_blocks, 128), lambda pair, *_: (pair, 0, 0))],
            scratch_shapes=[
                pltpu.VMEM((tokens + BLOCK, 128), f32),
                pltpu.VMEM((tokens, 128), f32),
            ],
        ),
        out_shape=[
            jax.ShapeDtypeStruct(q.shape, bf16),
            jax.ShapeDtypeStruct((pairs, query_blocks, 128), f32),
        ],
        compiler_params=pltpu.CompilerParams(vmem_limit_bytes=60 << 20),
        cost_estimate=pl.CostEstimate(flops=40 * 10**9, bytes_accessed=10**7, transcendentals=10**7),
        name="attend_forward",
    )(key_names, bias_names, global_name, length, flip, q, k, v)


def backward_kernel(
    query_names, key_names, bias_names, lengths, flips,
    q_ref, k_ref, v_ref, back_ref, context_ref, logsum_ref,
    back_q_ref, back_k_ref, back_v_ref, bias_scratch, q_scratch, k_scratch, v_scratch, *, unroll, items,
):
    @pl.when(pl.program_id(0) == 0)
    def _():
        fill_length_bias(bias_scratch, lengths[0], flips[0])

    q_scratch[...] = jnp.zeros_like(q_scratch)
    k_scratch[...] = jnp.zeros_like(k_scratch)
    v_scratch[...] = jnp.zeros_like(v_scratch)
    ones = jnp.ones((16, 128), bf16)

    def one(item):
        block = query_names[item]
        rows = block_rows(block)
        queries = halves(q_ref[rows, :])
        back = back_ref[rows, :]
        backs = halves(back)
        product = (back.astype(f32) * context_ref[rows, :].astype(f32)).astype(bf16)
        inner = dot_nt(ones, halves(product))[0:1]
        logsum = logsum_ref[0, pl.ds(block, 1), :]
        names = [key_names[item, slot] for slot in range(SLOTS)]
        biases = [bias_names[item, slot] for slot in range(SLOTS)]
        keys = gather_blocks(k_ref, names)
        scores = dot_nt(keys, queries) + gather_blocks(bias_scratch, biases)
        shares = jnp.exp(scores - logsum)
        back_shares = dot_nt(gather_blocks(v_ref, names), backs)
        back_values = dot_nn(shares.astype(bf16), backs)
        back_scores = (shares * (back_shares - inner)).astype(bf16)
        back_keys = dot_nn(back_scores, queries)
        q_scratch[rows, :] += join_halves(dot_tn(back_scores, keys))
        for slot in range(SLOTS):
            part = slice(slot * BLOCK, (slot + 1) * BLOCK)
            v_scratch[block_rows(names[slot]), :] += back_values[part]
            k_scratch[block_rows(names[slot]), :] += back_keys[part]

    def body(step, carry):
        for within in range(unroll):
            one(step * unroll + within)
        return carry

    lax.fori_loop(0, items // unroll, body, 0)
    back_q_ref[...] = (q_scratch[...] * HEAD_DIM ** (-0.5)).astype(bf16)
    back_k_ref[...] = k_scratch[...].astype(bf16)
    back_v_ref[...] = v_scratch[...].astype(bf16)


def attend_back(plan, length, flip, pair, q, k, v, back, context, logsum):
    query_names, key_names, bias_names, _ = plan
    query_rows = q.shape[0]
    tokens = k.shape[0]
    query_blocks = query_rows // BLOCK
    q_in = pl.BlockSpec((query_rows, 128), lambda step, *_: (0, pair))
    k_in = pl.BlockSpec((tokens, 128), lambda step, *_: (0, pair))
    q_out = pl.BlockSpec((query_rows, 128), lambda step, *_: (0, 0))
    k_out = pl.BlockSpec((tokens, 128), lambda step, *_: (0, 0))
    return pl.pallas_call(
        partial(backward_kernel, unroll=8, items=query_names.shape[0]),
        grid_spec=pltpu.PrefetchScalarGridSpec(
            num_scalar_prefetch=5,
            grid=(1,),
            in_specs=[
                q_in, k_in, k_in, q_in, q_in,
                pl.BlockSpec((1, query_blocks, 128), lambda step, *_: (pair, 0, 0)),
            ],
            out_specs=[q_out, k_out, k_out],
            scratch_shapes=[
                pltpu.VMEM((tokens + BLOCK, 128), f32),
                pltpu.VMEM((query_rows, 128), f32),
                pltpu.VMEM((tokens, 128), f32),
                pltpu.VMEM((tokens, 128), f32),
            ],
        ),
        out_shape=[
            jax.ShapeDtypeStruct((query_rows, 128), bf16),
            jax.ShapeDtypeStruct((tokens, 128), bf16),
            jax.ShapeDtypeStruct((tokens, 128), bf16),
        ],
        compiler_params=pltpu.CompilerParams(vmem_limit_bytes=60 << 20),
        cost_estimate=pl.CostEstimate(flops=10**9, bytes_accessed=10**6, transcendentals=10**5),
        name="attend_backward",
    )(query_names, key_names, bias_names, length, flip, q, k, v, back, context, logsum)


def project_kernel(core, x_ref, x_near_ref, w_q, w_k, w_v, b_q, b_v, q_ref, k_ref, v_ref):
    step = pl.program_id(0)

    def project(tile):
        q = (dot_nn(tile, w_q[...]) + b_q[...]).astype(bf16)
        q_ref[...] = q * jnp.asarray(HEAD_DIM ** (-0.5), bf16)
        k_ref[...] = dot_nn(tile, w_k[...]).astype(bf16)
        v_ref[...] = (dot_nn(tile, w_v[...]) + b_v[...]).astype(bf16)

    @pl.when(step < pl.num_programs(0) // 2)
    def _():
        project(x_ref[...])

    @pl.when(step >= pl.num_programs(0) // 2)
    def _():
        project(x_near_ref[...])


def project_far_kernel(core, x_ref, x_near_ref, w_k, w_v, b_v, k_old, v_old, k_ref, v_ref):
    step = pl.program_id(0)

    def project(tile):
        k_ref[...] = dot_nn(tile, w_k[...]).astype(bf16)
        v_ref[...] = (dot_nn(tile, w_v[...]) + b_v[...]).astype(bf16)

    @pl.when(step < pl.num_programs(0) // 2)
    def _():
        project(x_ref[...])

    @pl.when(step >= pl.num_programs(0) // 2)
    def _():
        project(x_near_ref[...])


TILE = 512


def piece_spec(piece, per, width):
    return pl.BlockSpec((TILE, width), lambda step, *_: (jnp.clip(step - piece * per, 0, per - 1), 0))


def own_weight(which):
    return pl.BlockSpec((D, D // 2), lambda step, core, *_: (0, 2 * which + core[0]))


def own_bias():
    return pl.BlockSpec((1, D // 2), lambda step, core, *_: (0, core[0]))


def project_chip(core, x, x_near, qkv_weight, query_bias, value_bias):
    rows = x.shape[0]
    half = D // 2
    per = rows // TILE
    out = pl.BlockSpec((TILE, half), lambda step, *_: (step, 0))
    return pl.pallas_call(
        project_kernel,
        grid_spec=pltpu.PrefetchScalarGridSpec(
            num_scalar_prefetch=1,
            grid=(2 * per,),
            in_specs=[piece_spec(0, per, D), piece_spec(1, per, D)]
            + [own_weight(0), own_weight(1), own_weight(2), own_bias(), own_bias()],
            out_specs=[out, out, out],
        ),
        out_shape=[
            jax.ShapeDtypeStruct((2 * rows, half), bf16),
            jax.ShapeDtypeStruct((4 * rows, half), bf16),
            jax.ShapeDtypeStruct((4 * rows, half), bf16),
        ],
        compiler_params=pltpu.CompilerParams(vmem_limit_bytes=60 << 20),
        cost_estimate=pl.CostEstimate(flops=4 * 10**9, bytes_accessed=10**7, transcendentals=0),
        name="project_chip",
    )(core, x, x_near, qkv_weight, qkv_weight, qkv_weight, query_bias, value_bias)


def project_far(core, x_far, x_far_near, qkv_weight, value_bias, k, v):
    rows = x_far.shape[0]
    half = D // 2
    per = rows // TILE
    out = pl.BlockSpec((TILE, half), lambda step, *_: (2 * per + step, 0))
    kept = pl.BlockSpec(memory_space=pl.ANY)
    return pl.pallas_call(
        project_far_kernel,
        grid_spec=pltpu.PrefetchScalarGridSpec(
            num_scalar_prefetch=1,
            grid=(2 * per,),
            in_specs=[piece_spec(0, per, D), piece_spec(1, per, D)]
            + [own_weight(1), own_weight(2), own_bias(), kept, kept],
            out_specs=[out, out],
        ),
        out_shape=[jax.ShapeDtypeStruct(k.shape, bf16), jax.ShapeDtypeStruct(v.shape, bf16)],
        input_output_aliases={6: 0, 7: 1},
        compiler_params=pltpu.CompilerParams(vmem_limit_bytes=60 << 20),
        cost_estimate=pl.CostEstimate(flops=3 * 10**9, bytes_accessed=10**7, transcendentals=0),
        name="project_far",
    )(core, x_far, x_far_near, qkv_weight, qkv_weight, value_bias, k, v)


def gelu_pair(x):
    t = 1.0 / (1.0 + (0.3275911 * 0.5**0.5) * jnp.abs(x))
    bell = jnp.exp(-0.5 * x * x)
    poly = 0.7107068705 + t * (-0.7265760135 + t * 0.5307027145)
    tail = t * (0.127414796 + t * (-0.142248368 + t * poly)) * bell
    cdf = jnp.where(x < 0, tail, 1.0 - tail)
    return x * cdf, cdf + x * bell * 0.3989422804014327


def norm_parts(value):
    center = value - jnp.mean(value, axis=-1, keepdims=True)
    spread = jnp.mean(center * center, axis=-1, keepdims=True)
    scale = lax.rsqrt(spread + norm_epsilon)
    return center * scale, scale


def norm_back(slope, normed, scale):
    along = jnp.mean(slope * normed, axis=-1, keepdims=True)
    return scale * (slope - jnp.mean(slope, axis=-1, keepdims=True) - normed * along)


def column_sum(value):
    return jnp.sum(value, axis=0, keepdims=True)


PIECES = 16
VECTOR_ROWS = 128


def row_spec(tile, width):
    return pl.BlockSpec((tile, width), lambda step, *_: (step, 0))


def stack_spec(count, tile, width):
    return pl.BlockSpec((count, tile, width), lambda step, *_: (0, step, 0))


def whole_spec(shape):
    return pl.BlockSpec(shape, lambda step, *_: (0,) * len(shape))


def middle_kernel(
    core,
    own_ref, other_ref, x_ref, cot_ref, vector_ref, expand_bias_ref, proj_hbm, expand_hbm, shrink_hbm,
    output_ref, back_one_ref, back_own_ref, back_other_ref, wide_keep, wide_send, lows_ref, sums_ref,
    proj_w, expand_w, shrink_w, slope_s, wide_s, weight_sems, wide_sems, *, chunk,
):
    step = pl.program_id(0)
    half = D // 2
    ff = expand_w.shape[1]
    chunks = ff // chunk
    hc = core[0]
    loads = [
        pltpu.make_async_copy(proj_hbm.at[pl.ds(hc * half, half)], proj_w.at[pl.ds(0, half)], weight_sems.at[0]),
        pltpu.make_async_copy(
            proj_hbm.at[pl.ds((1 - hc) * half, half)], proj_w.at[pl.ds(half, half)], weight_sems.at[1]
        ),
        pltpu.make_async_copy(expand_hbm, expand_w, weight_sems.at[2]),
        pltpu.make_async_copy(shrink_hbm, shrink_w, weight_sems.at[3]),
    ]

    @pl.when(step == 0)
    def _():
        for load in loads:
            load.start()
        sums_ref[...] = jnp.zeros_like(sums_ref)
        for load in loads:
            load.wait()

    def vector(row):
        return vector_ref[pl.ds(row, 1), :]

    slot = lax.rem(step, 2)
    tile = x_ref.shape[0]

    def wide_copies(slot, first_row):
        copies = []
        for which in range(2):
            for side, out in enumerate((wide_keep, wide_send)):
                first = pl.multiple_of((hc if side == 0 else 1 - hc) * (ff // 2), ff // 2)
                copies.append(
                    pltpu.make_async_copy(
                        wide_s.at[slot, which, :, pl.ds(first, ff // 2)],
                        out.at[which, pl.ds(pl.multiple_of(first_row, tile), tile)],
                        wide_sems.at[slot, 2 * which + side],
                    )
                )
        return copies

    @pl.when(step >= 2)
    def _():
        for copy in wide_copies(slot, 0):
            copy.wait()

    context = jnp.concatenate([own_ref[...], other_ref[...]], axis=1)
    resid = x_ref[...].astype(f32) + dot_nn(context, proj_w[...]) + vector(0)
    normed_one, scale_one = norm_parts(resid)
    hidden = normed_one * vector(1) + vector(2)
    low = hidden.astype(bf16)
    lows_ref[0] = low
    resid_two = hidden + vector(3)

    for part in range(chunks):
        cols = slice(part * chunk, (part + 1) * chunk)
        inner = dot_nn(low, expand_w[:, cols]) + expand_bias_ref[:, cols]
        active, slope = gelu_pair(inner)
        active = active.astype(bf16)
        wide_s[slot, 0, :, cols] = active
        slope_s[:, cols] = slope.astype(bf16)
        resid_two = resid_two + dot_nn(active, shrink_w[cols, :])
    normed_two, scale_two = norm_parts(resid_two)
    output_ref[...] = (normed_two * vector(4) + vector(5)).astype(bf16)
    cot = cot_ref[...].astype(f32)
    back_two = norm_back(vector(4) * cot, normed_two, scale_two)
    low_two = back_two.astype(bf16)
    lows_ref[1] = low_two
    sums_ref[3:4, :] += column_sum(low_two.astype(f32))
    sums_ref[4:5, :] += column_sum(cot * normed_two)
    sums_ref[5:6, :] += column_sum(cot)
    back = back_two
    for part in range(chunks):
        cols = slice(part * chunk, (part + 1) * chunk)
        back_inner = (dot_nt(low_two, shrink_w[cols, :]) * slope_s[:, cols].astype(f32)).astype(bf16)
        wide_s[slot, 1, :, cols] = back_inner
        sums_ref[8 + part : 9 + part, :] += column_sum(back_inner.astype(f32))
        back = back + dot_nt(back_inner, expand_w[:, cols])
    sums_ref[1:2, :] += column_sum(back * normed_one)
    sums_ref[2:3, :] += column_sum(back)
    back_one = norm_back(vector(1) * back, normed_one, scale_one)
    back_one_ref[...] = back_one
    low_one = back_one.astype(bf16)
    lows_ref[2] = low_one
    sums_ref[0:1, :] += column_sum(low_one.astype(f32))
    back_context = dot_nt(low_one, proj_w[...]).astype(bf16)
    back_own_ref[...] = back_context[:, :half]
    back_other_ref[...] = back_context[:, half:]
    for copy in wide_copies(slot, step * tile):
        copy.start()

    @pl.when(step == pl.num_programs(0) - 1)
    def _():
        for other in range(2):
            for copy in wide_copies(other, 0):
                copy.wait()


def middle(core, own, other, x, cot, vectors, expand_bias, proj_weight, expand_weight, shrink_weight):
    rows = x.shape[0]
    ff = expand_weight.shape[1]
    half = D // 2
    tile = 256
    kept = pl.BlockSpec(memory_space=pl.ANY)
    assert ff // D == 4
    return pl.pallas_call(
        partial(middle_kernel, chunk=D),
        grid_spec=pltpu.PrefetchScalarGridSpec(
            num_scalar_prefetch=1,
            grid=(rows // tile,),
            in_specs=[row_spec(tile, half)] * 2
            + [row_spec(tile, D)] * 2
            + [whole_spec(vectors.shape), whole_spec(expand_bias.shape), kept, kept, kept],
            out_specs=[row_spec(tile, D)] * 2
            + [row_spec(tile, half)] * 2
            + [kept] * 2
            + [stack_spec(3, tile, D), whole_spec((16, D))],
            scratch_shapes=[
                pltpu.VMEM((D, D), bf16),
                pltpu.VMEM((D, ff), bf16),
                pltpu.VMEM((ff, D), bf16),
                pltpu.VMEM((tile, ff), bf16),
                pltpu.VMEM((2, 2, tile, ff), bf16),
                pltpu.SemaphoreType.DMA((4,)),
                pltpu.SemaphoreType.DMA((2, 4)),
            ],
        ),
        out_shape=[
            jax.ShapeDtypeStruct((rows, D), bf16),
            jax.ShapeDtypeStruct((rows, D), f32),
            jax.ShapeDtypeStruct((rows, half), bf16),
            jax.ShapeDtypeStruct((rows, half), bf16),
            jax.ShapeDtypeStruct((2, rows, ff // 2), bf16),
            jax.ShapeDtypeStruct((2, rows, ff // 2), bf16),
            jax.ShapeDtypeStruct((3, rows, D), bf16),
            jax.ShapeDtypeStruct((16, D), f32),
        ],
        compiler_params=pltpu.CompilerParams(vmem_limit_bytes=60 << 20),
        cost_estimate=pl.CostEstimate(flops=10**9, bytes_accessed=10**7, transcendentals=10**6),
        name="middle",
    )(core, own, other, x, cot, vectors, expand_bias, proj_weight, expand_weight, shrink_weight)


def weights_kernel(
    places, wide_own, wide_other, lows_own, lows_other, context_ref, sums_own, sums_other, *refs
):
    packed = refs[:4]
    shrink_g, expand_g, proj_g = refs[4:]
    step = pl.program_id(0)
    half = D // 2

    @pl.when(step == 0)
    def _():
        shrink_g[...] = jnp.zeros_like(shrink_g)
        expand_g[...] = jnp.zeros_like(expand_g)
        proj_g[...] = jnp.zeros_like(proj_g)
        proj_g[half : half + 16, :] = sums_own[...] + sums_other[...]

    def add(wide, lows):
        shrink_g[...] += dot_tn(wide[0], lows[1])
        expand_g[...] += dot_tn(lows[0], wide[1])
        proj_g[:half, :] += dot_tn(context_ref[...], lows[2])

    @pl.when(step < pl.num_programs(0) // 2)
    def _():
        add(wide_own, lows_own)

    @pl.when(step >= pl.num_programs(0) // 2)
    def _():
        add(wide_other, lows_other)

    @pl.when(step == pl.num_programs(0) - 1)
    def _():
        rows = shrink_g.shape[0] // PIECES
        extra = proj_g.shape[0] // (2 * PIECES)
        wide = expand_g.shape[1] // D
        for piece in range(PIECES):
            place = piece % (PIECES // 2)
            first = piece ^ places[0]
            second = piece ^ places[1]
            out = packed[piece // (PIECES // 2)]
            out[place, :rows, :] = shrink_g[pl.ds(pl.multiple_of(first * rows, rows), rows), :].astype(bf16)
            out[place, rows:, :] = proj_g[pl.ds(pl.multiple_of(first * extra, extra), extra), :].astype(bf16)
            out = packed[2 + piece // (PIECES // 2)]
            down = pl.ds(pl.multiple_of((second // wide) * rows, rows), rows)
            across = pl.ds(pl.multiple_of(lax.rem(second, wide) * D, D), D)
            out[place, :rows, :] = expand_g[down, across].astype(bf16)
            part = pl.ds(pl.multiple_of((PIECES + second) * extra, extra), extra)
            out[place, rows:, :] = proj_g[part, :].astype(bf16)


def weight_grads(places, wide_own, wide_other, lows_own, lows_other, context, sums_own, sums_other):
    _, rows, wide = wide_own.shape
    half = D // 2
    per = rows // TILE
    piece_rows = wide // PIECES + (half + VECTOR_ROWS) // (2 * PIECES)

    def own(count, width):
        return pl.BlockSpec((count, TILE, width), lambda step, *_: (0, jnp.minimum(step, per - 1), 0))

    def other(count, width):
        return pl.BlockSpec((count, TILE, width), lambda step, *_: (0, jnp.maximum(step - per, 0), 0))

    packed_shape = (PIECES // 2, piece_rows, D)
    return pl.pallas_call(
        weights_kernel,
        grid_spec=pltpu.PrefetchScalarGridSpec(
            num_scalar_prefetch=1,
            grid=(2 * per,),
            in_specs=[own(2, wide), other(2, wide), own(3, D), other(3, D), row_spec(TILE, half)]
            + [whole_spec((16, D))] * 2,
            out_specs=[whole_spec(packed_shape)] * 4,
            scratch_shapes=[
                pltpu.VMEM((wide, D), f32),
                pltpu.VMEM((D, wide), f32),
                pltpu.VMEM((half + VECTOR_ROWS, D), f32),
            ],
        ),
        out_shape=[jax.ShapeDtypeStruct(packed_shape, bf16)] * 4,
        compiler_params=pltpu.CompilerParams(vmem_limit_bytes=60 << 20),
        cost_estimate=pl.CostEstimate(flops=10**9, bytes_accessed=10**7, transcendentals=0),
        name="weight_grads",
    )(places, wide_own, wide_other, lows_own, lows_other, context, sums_own, sums_other)


def halves_spec(per):
    return [
        pl.BlockSpec((TILE, D), lambda step, *_: (jnp.minimum(step, per - 1), 0)),
        pl.BlockSpec((TILE, D), lambda step, *_: (jnp.maximum(step - per, 0), 0)),
    ]


def input_kernel(core, *refs, count, per):
    weights, arrays, outs = refs[:count], refs[count:-2], refs[-2:]
    pairs = len(arrays) // count
    step = pl.program_id(0)
    total = None
    for which in range(count):
        back = jnp.concatenate([ref[...] for ref in arrays[which * pairs : (which + 1) * pairs]], axis=1)
        part = dot_nt(back, weights[which][...])
        total = part if total is None else total + part

    @pl.when(step < per)
    def _():
        outs[0][...] = total.astype(bf16)

    @pl.when(step >= per)
    def _():
        outs[1][...] = total.astype(bf16)


def input_part(core, qkv_weight, groups, weights, first, rows, name):
    token = pl.BlockSpec((TILE, 128), lambda step, *_: (first // TILE + step, 0))
    arrays = [array for group in groups for array in group]
    per = rows // TILE
    half_shape = jax.ShapeDtypeStruct((rows, D), bf16)
    return pl.pallas_call(
        partial(input_kernel, count=len(groups), per=per),
        grid_spec=pltpu.PrefetchScalarGridSpec(
            num_scalar_prefetch=1,
            grid=(2 * per,),
            in_specs=[own_weight(which) for which in weights] + [token] * len(arrays),
            out_specs=halves_spec(per),
        ),
        out_shape=[half_shape, half_shape],
        compiler_params=pltpu.CompilerParams(vmem_limit_bytes=60 << 20),
        cost_estimate=pl.CostEstimate(flops=10**9, bytes_accessed=10**7, transcendentals=0),
        name=name,
    )(core, *[qkv_weight] * len(weights), *arrays)


QKV_PIECES = 16


def joined_kernel(places, core, *refs, tiles, pairs):
    x_refs = refs[:4]
    arrays = refs[4 : 4 + 3 * pairs]
    packed = refs[4 + 3 * pairs : 8 + 3 * pairs]
    total, sums = refs[8 + 3 * pairs :]
    step = pl.program_id(0)
    half = D // 2
    per = tiles // 4

    @pl.when(step == 0)
    def _():
        total[...] = jnp.zeros_like(total)
        sums[...] = jnp.zeros_like(sums)

    def joined(first, last):
        return jnp.concatenate([ref[...] for ref in arrays[first * pairs : last * pairs]], axis=1)

    for piece in range(4):

        @pl.when((step >= piece * per) & (step < (piece + 1) * per))
        def _():
            first = 0 if piece < 2 else 1
            back = joined(first, 3)
            total[:, first * half : 3 * half] += dot_tn(x_refs[piece][...], back)
            sums[0:1, first * half :] += column_sum(back.astype(f32))

    @pl.when(step == tiles - 1)
    def _():
        rows = D // QKV_PIECES
        q_sums = jnp.transpose(jnp.broadcast_to(sums[0:1, :half], (128, half)))
        v_sums = jnp.transpose(jnp.broadcast_to(sums[0:1, 2 * half :], (128, half)))
        total[:half, 3 * half :] = q_sums
        total[half:, 3 * half :] = v_sums
        width = packed[0].shape[2]
        for color in range(2):
            cols = slice(color * width, (color + 1) * width)
            for piece in range(QKV_PIECES):
                part = pl.ds(pl.multiple_of((piece ^ places[color]) * rows, rows), rows)
                out = packed[2 * color + piece // (QKV_PIECES // 2)]
                out[piece % (QKV_PIECES // 2)] = total[part, cols].astype(bf16)


def joined_grads(places, core, xs, back_qs, back_ks, back_vs):
    rows = xs[0].shape[0]
    pairs = len(back_qs)
    per = rows // TILE
    tiles = 4 * per
    width = D // 2 + 256
    token = pl.BlockSpec((TILE, 128), lambda step, *_: (step, 0))
    query = pl.BlockSpec((TILE, 128), lambda step, *_: (jnp.minimum(step, 2 * per - 1), 0))
    packed = pl.BlockSpec((QKV_PIECES // 2, D // QKV_PIECES, width), lambda step, *_: (0, 0, 0))
    packed_shape = jax.ShapeDtypeStruct((QKV_PIECES // 2, D // QKV_PIECES, width), bf16)
    return pl.pallas_call(
        partial(joined_kernel, tiles=tiles, pairs=pairs),
        grid_spec=pltpu.PrefetchScalarGridSpec(
            num_scalar_prefetch=2,
            grid=(tiles,),
            in_specs=[piece_spec(piece, per, D) for piece in range(4)] + [query] * pairs + [token] * (2 * pairs),
            out_specs=[packed] * 4,
            scratch_shapes=[pltpu.VMEM((D, 2 * width), f32), pltpu.VMEM((8, 3 * D // 2), f32)],
        ),
        out_shape=[packed_shape] * 4,
        compiler_params=pltpu.CompilerParams(vmem_limit_bytes=60 << 20),
        cost_estimate=pl.CostEstimate(flops=10**9, bytes_accessed=10**7, transcendentals=0),
        name="joined_grads",
    )(places, core, *xs, *back_qs, *back_ks, *back_vs)


def input_near_kernel(core, *refs):
    w_q, w_k, w_v, out = refs[0], refs[1], refs[2], refs[-1]
    arrays = refs[3:-1]
    pairs = len(arrays) // 3

    def joined(which):
        return jnp.concatenate([ref[...] for ref in arrays[which * pairs : (which + 1) * pairs]], axis=1)

    out[...] = (dot_nt(joined(0), w_q[...]) + dot_nt(joined(1), w_k[...]) + dot_nt(joined(2), w_v[...])).astype(bf16)


def input_near(core, qkv_weight, back_qs, back_ks, back_vs):
    rows = back_qs[0].shape[0]
    token = pl.BlockSpec((TILE, 128), lambda step, *_: (step, 0))
    arrays = list(back_qs) + list(back_ks) + list(back_vs)
    return pl.pallas_call(
        input_near_kernel,
        grid_spec=pltpu.PrefetchScalarGridSpec(
            num_scalar_prefetch=1,
            grid=(rows // TILE,),
            in_specs=[own_weight(0), own_weight(1), own_weight(2)] + [token] * len(arrays),
            out_specs=pl.BlockSpec((TILE, D), lambda step, *_: (step, 0)),
        ),
        out_shape=jax.ShapeDtypeStruct((rows, D), bf16),
        compiler_params=pltpu.CompilerParams(vmem_limit_bytes=60 << 20),
        cost_estimate=pl.CostEstimate(flops=10**9, bytes_accessed=10**7, transcendentals=0),
        name="input_near",
    )(core, qkv_weight, qkv_weight, qkv_weight, *arrays)


GROUP = 8


def unpack_kernel(numbers, *refs, parts, outs, held):
    sources = refs[:2]
    targets = refs[2 + held : 2 + held + outs]
    stages = refs[2 + held + outs : -1]
    sems = refs[-1]
    step = pl.program_id(0)
    count = numbers.shape[0] // 2 // GROUP
    at = lax.rem(step, 2)

    def copy(color, which, slot, number):
        part = parts[color][which]
        row, col = part["place"](number)
        rows, cols = part["rows"][1] - part["rows"][0], part["cols"][1] - part["cols"][0]
        target = targets[part["out"]].at[pl.ds(pl.multiple_of(row, rows), rows), pl.ds(pl.multiple_of(col, 128), cols)]
        at = part["at"]
        source = stages[color].at[slot, pl.ds(at[0], rows), pl.ds(at[1], cols)]
        return pltpu.make_async_copy(source, target, sems.at[color, which, slot])

    def wait(color, slot):
        for which in range(len(parts[color])):
            copy(color, which, slot, 0).wait()

    for color, source in enumerate(sources):

        @pl.when(step // count == color)
        def _():
            for within in range(GROUP):
                slot = lax.rem(step, 2) * GROUP + within
                number = numbers[step * GROUP + within]

                @pl.when(step - color * count >= 2)
                def _():
                    wait(color, slot)

                stages[color][slot] = source[within].astype(f32)
                for which in range(len(parts[color])):
                    copy(color, which, slot, number).start()

    @pl.when(step == pl.num_programs(0) - 1)
    def _():
        for color in range(2):
            for slot in range(min(2, count) * GROUP):
                wait(color, slot)


def unpack(numbers, sources, parts, out_shapes, held, name):
    count, rows, width = sources[0].shape
    groups = count // GROUP
    assert groups == 2
    most = max(len(part) for part in parts)
    kept = pl.BlockSpec(memory_space=pl.ANY)
    return pl.pallas_call(
        partial(unpack_kernel, parts=parts, outs=len(out_shapes), held=len(held)),
        grid_spec=pltpu.PrefetchScalarGridSpec(
            num_scalar_prefetch=1,
            grid=(2 * groups,),
            in_specs=[
                pl.BlockSpec((GROUP, rows, width), lambda step, *_: (jnp.minimum(step, groups - 1), 0, 0)),
                pl.BlockSpec((GROUP, rows, width), lambda step, *_: (jnp.maximum(step - groups, 0), 0, 0)),
            ]
            + [kept] * len(held),
            out_specs=[kept] * len(out_shapes),
            scratch_shapes=[pltpu.VMEM((2 * GROUP, rows, width), f32)] * 2
            + [pltpu.SemaphoreType.DMA((2, most, 2 * GROUP))],
        ),
        out_shape=[jax.ShapeDtypeStruct(shape, f32) for shape in out_shapes],
        input_output_aliases={3 + place: place for place in range(len(held))},
        compiler_params=pltpu.CompilerParams(vmem_limit_bytes=60 << 20),
        cost_estimate=pl.CostEstimate(flops=10**6, bytes_accessed=10**6, transcendentals=0),
        name=name,
    )(numbers, *sources, *held)


def part_of(rows, cols, out, place):
    return {"rows": rows, "cols": cols, "at": (rows[0], cols[0]), "out": out, "place": place}


def swap(value, axis, bit=1):
    size = lax.axis_size(axis)
    return lax.ppermute(value, axis, [(place, place ^ bit) for place in range(size)])


def place_of(order):
    number = jnp.zeros((), jnp.int32)
    for axis, bit in order:
        number = 2 * number + ((lax.axis_index(axis) & bit) // bit).astype(jnp.int32)
    return number


def add_low(left, right):
    return (left.astype(f32) + right.astype(f32)).astype(bf16)


class Chain:
    def __init__(self, scatter_order, gather_order, keep, first):
        self.orders = list(scatter_order) + list(gather_order) + [("hc", 1)]
        self.steps = len(scatter_order)
        self.keep, self.first, self.arrived = keep, first, None
        self.at = 0
        self.gathered = None

    def left(self):
        return len(self.orders) - self.at

    def send(self):
        if self.at < self.steps:
            if self.at == 0:
                return self.first
            half = self.keep.shape[0] // 2
            high = add_low(self.keep[half:], self.arrived[half:])
            self.keep = add_low(self.keep[:half], self.arrived[:half])
            return high
        if self.at == self.steps:
            total = add_low(self.keep, self.arrived)
            bit = 8
            while bit < lax.axis_size("dp"):
                total = add_low(total, swap(total, "dp", bit))
                bit *= 2
            self.gathered = total
        else:
            self.gathered = jnp.concatenate([self.gathered, self.arrived], axis=0)
        return self.gathered

    def move(self, value):
        if self.at >= self.steps:
            self.gathered = value
        axis, bit = self.orders[self.at]
        self.arrived = swap(value, axis, bit)
        self.at += 1


def gathered_numbers(number, scatter_order, gather_order):
    count = 1 << len(scatter_order)
    places = jnp.arange(count, dtype=jnp.int32)
    turned = jnp.zeros((count,), jnp.int32)
    for at, name in enumerate(gather_order):
        turned = turned + (((places >> at) & 1) << (len(scatter_order) - 1 - scatter_order.index(name)))
    return turned ^ number


def ready(*values):
    return lax.optimization_barrier(values)


def per_device(
    inputs, doc_lengths, random_blocks, qkv_weight, query_bias, value_bias, proj_weight, proj_bias,
    first_gain, first_shift, expand_weight, expand_bias, shrink_weight, shrink_bias,
    second_gain, second_shift, cotangent,
):
    hx = lax.axis_index("hx")
    hc = lax.axis_index("hc")
    docs, rows, _ = inputs.shape
    assert docs == 1 and lax.axis_size("hx") == 2 and lax.axis_size("hc") == 2
    half = D // 2
    ff = expand_weight.shape[1]
    pairs = half // 128
    x = inputs.reshape(rows, D)
    x_far = swap(x, "hx")
    x_near = swap(x, "hc")
    row_blocks = rows // BLOCK
    flip = (hx * 2 + hc).astype(jnp.int32) * row_blocks
    plan = block_plan(doc_lengths[0], random_blocks[0], flip, 2 * row_blocks)
    flip = flip.reshape(1)
    core = hc.astype(jnp.int32).reshape(1)
    chip_steps = {"x": ("hx", 1), "y": ("dp", 1), "n": ("dp", 2), "f": ("dp", 4)}
    orders = {
        name: tuple([chip_steps[step] for step in part] for part in text.split())
        for name, text in ORDERS.items()
    }

    def places_of(letter):
        return jnp.stack([place_of(orders[f"{letter}{color}"][0]) for color in range(2)])

    def numbers_of(letter, places):
        own = [gathered_numbers(places[color], *orders[f"{letter}{color}"]) for color in range(2)]
        own = jnp.concatenate(own)
        return own + PIECES * core, own + PIECES * (1 - core)

    middle_places, joined_places = places_of("M"), places_of("Q")
    numbers = numbers_of("M", middle_places) + numbers_of("Q", joined_places)
    vectors = jnp.concatenate(
        [proj_bias, first_gain, first_shift, shrink_bias, second_gain, second_shift, query_bias, value_bias]
    ).reshape(8, D)
    vectors = vectors.astype(f32)
    bias_q, bias_v = vectors[6:7], vectors[7:8]
    expand_row = expand_bias.astype(f32).reshape(1, ff)

    q, k, v = project_chip(core, x, x_near, qkv_weight, bias_q, bias_v)
    x_far, q, expand_row, vectors, middle_places, joined_places, *rest = ready(
        x_far, q, expand_row, vectors, middle_places, joined_places, *numbers, *plan
    )
    numbers, plan = rest[:4], rest[4:]
    x_far_near = swap(x_far, "hc")
    k, v = project_far(core, x_far, x_far_near, qkv_weight, bias_v, k, v)
    context, logsum = attend(plan, doc_lengths, flip, q, k, v)
    other_context = swap(context[rows:], "hc")
    output, back_one, back_own, back_other, wide_keep, wide_send, lows, sums = middle(
        core, context, other_context, x, cotangent.reshape(rows, D), vectors,
        expand_row, proj_weight, expand_weight, shrink_weight,
    )
    from_other = swap(back_other, "hc")
    wide_send, lows_send, sums_send, from_other = ready(wide_send, lows, sums, from_other)
    back = jnp.concatenate([back_own, from_other], axis=0)
    wide_other, lows_other, sums_other = swap(wide_send, "hc"), swap(lows_send, "hc"), swap(sums_send, "hc")

    held = {"last": back}
    chains = {}

    def tie(value):
        value, held["last"] = ready(value, held["last"])
        return value

    def pairs_of(which):
        return [held["grads", pair][which] for pair in range(pairs)]

    def both(letter, side):
        return [getattr(chains[f"{letter}{color}"], side) for color in range(2)]

    rows_each, extra, wide = ff // 2 // PIECES, (D // 2 + VECTOR_ROWS) // (2 * PIECES), ff // 2 // D
    proj_pieces = half // extra

    def split(number):
        return number // PIECES, lax.rem(number, PIECES)

    def expand_place(number):
        side, piece = split(number)
        return piece // wide * rows_each, (side * wide + lax.rem(piece, wide)) * D

    def extra_place(color):
        def place(number):
            side, piece = split(number)
            return ((2 * color + side) * PIECES + piece) * extra, number * 0

        return place

    def joined_place(which, offset):
        def place(number):
            side, piece = split(number)
            return piece * (D // QKV_PIECES), which * D + side * half + offset

        return place

    def bias_place(number):
        side, piece = split(number)
        return (side * QKV_PIECES + piece) * (D // QKV_PIECES), number * 0

    each = D // QKV_PIECES
    middle_parts = [
        [
            part_of((0, rows_each), (0, D), 0, lambda n: (n * rows_each, n * 0)),
            part_of((rows_each, rows_each + extra), (0, D), 2, extra_place(0)),
        ],
        [
            part_of((0, rows_each), (0, D), 1, expand_place),
            part_of((rows_each, rows_each + extra), (0, D), 2, extra_place(1)),
        ],
    ]
    joined_parts = [
        [
            part_of((0, each), (0, half), 0, joined_place(0, 0)),
            part_of((0, each), (half, half + 256), 0, joined_place(1, 0)),
        ],
        [
            part_of((0, each), (0, 128), 0, joined_place(1, 256)),
            part_of((0, each), (128, 128 + half), 0, joined_place(2, 0)),
            part_of((0, each), (128 + half, 256 + half), 1, bias_place),
        ],
    ]
    layouts = {
        "M": (middle_parts, [(ff, D), (D, ff), (4 * PIECES * extra, D)], numbers[:2]),
        "Q": (joined_parts, [(D, 3 * D), (2 * D, 128)], numbers[2:]),
    }

    def run(name):
        if name.startswith("attend"):
            pair = int(name[-1])
            held["grads", pair] = attend_back(plan, doc_lengths, flip, pair, q, k, v, tie(back), context, logsum)
            held["last"] = held["grads", pair][0]
        elif name == "weights":
            packed = weight_grads(
                middle_places, tie(wide_keep), wide_other, lows, lows_other, context, sums, sums_other
            )
            held["last"] = packed[0]
            for color in range(2):
                chains[f"M{color}"] = Chain(*orders[f"M{color}"], packed[2 * color], packed[2 * color + 1])
        elif name == "joined":
            back_qs = pairs_of(0)
            back_qs[0] = tie(back_qs[0])
            packed = joined_grads(
                joined_places, core, (x, x_near, x_far, x_far_near), back_qs, pairs_of(1), pairs_of(2)
            )
            held["last"] = packed[0]
            for color in range(2):
                chains[f"Q{color}"] = Chain(*orders[f"Q{color}"], packed[2 * color], packed[2 * color + 1])
        elif name == "far":
            back_ks = pairs_of(1)
            back_ks[0] = tie(back_ks[0])
            mine, others = input_part(core, qkv_weight, (back_ks, pairs_of(2)), (1, 2), 2 * rows, rows, "input_far")
            held["last"] = mine
            held["far"] = mine, swap(others, "hc")
        elif name == "dx":
            value = tie(add_low(*held["far"]))
            held["last"] = value
            held["from_far"] = swap(value, "hx")
        elif name == "near":
            back_qs = pairs_of(0)
            back_qs[0] = tie(back_qs[0])
            groups = (back_qs, pairs_of(1), pairs_of(2))
            mine, others = input_part(core, qkv_weight, groups, (0, 1, 2), 0, rows, "input_near")
            held["last"] = mine
            held["near"] = mine, swap(others, "hc")
        elif name == "input":
            near, from_near = held["near"]
            near = tie(near)
            value = back_one + near.astype(f32) + from_near.astype(f32) + held["from_far"].astype(f32)
            held["last"] = held["input"] = value
        elif name.startswith("own") or name.startswith("other"):
            letter = name[-1]
            parts, shapes, places = layouts[letter]
            mine = name.startswith("own")
            sources = both(letter, "gathered" if mine else "arrived")
            sources[0] = tie(sources[0])
            held["out", letter] = unpack(
                places[0 if mine else 1], sources, parts, shapes, () if mine else held["out", letter],
                f"unpack_{letter}",
            )
            held["last"] = held["out", letter][0]
        else:
            chain = chains[name]
            value = tie(chain.send())
            chain.move(value)
            held["last"] = value

    for names in SEQUENCE:
        for name in names.split():
            run(name)
    assert all(chain.left() == 0 for chain in chains.values())
    grad_shrink, grad_expand, proj_rows = held["out", "M"]
    grad_qkv, bias = held["out", "Q"]
    low_rows = PIECES * extra
    rest = half - low_rows
    second = 2 * low_rows
    grad_proj = jnp.concatenate(
        [
            proj_rows[:low_rows],
            proj_rows[second : second + rest],
            proj_rows[low_rows:second],
            proj_rows[second + low_rows : second + low_rows + rest],
        ],
        axis=0,
    )
    vector = proj_rows[second + rest : second + low_rows]
    grad_query_bias = jnp.concatenate([bias[:half, 0], bias[D : D + half, 0]])
    grad_value_bias = jnp.concatenate([bias[half:D, 0], bias[D + half :, 0]])
    grad_expand_bias = vector[8 : 8 + ff // D].reshape(ff)
    return (
        output.reshape(docs, rows, D),
        held["input"].reshape(docs, rows, D),
        grad_qkv, grad_query_bias, grad_value_bias, grad_proj, vector[0], vector[1], vector[2],
        grad_expand, grad_expand_bias, grad_shrink, vector[3], vector[4], vector[5],
    )


ORDERS = {"M0": "nyxf fnyx", "M1": "xnfy fyxn", "Q0": "ynfx fnxy", "Q1": "yxnf xfny"}
SEQUENCE = (
    "attend0 weights M1 M0",
    "attend1 attend2 M1 M0",
    "joined M1 Q1 M0",
    "Q0 far M1 Q1",
    "M0 dx Q0 M1",
    "Q1 M0 Q0 near",
    "M1 Q1 M0 Q0",
    "Q1 M1 Q0 Q1",
    "M0 Q0 input Q1",
    "Q0 M1 Q1 M0",
    "Q0 Q1 Q0 ownQ",
    "M1 otherQ M0 ownM",
    "otherM",
)


def solution(mesh):
    dp = mesh.shape["dp"]
    heads = mesh.shape["heads"]
    split = Mesh(mesh.devices.reshape(dp, heads // 2, 2), ("dp", "hx", "hc"))
    rows = P("dp", ("hx", "hc"), None)
    in_specs = (rows, P("dp"), P("dp", None, None)) + (P(),) * 13 + (rows,)
    out_specs = (rows, rows) + (P(),) * 13
    return jax.shard_map(
        per_device, mesh=split, in_specs=in_specs, out_specs=out_specs, check_vma=False
    )
```

```python
from functools import partial

import jax
import jax.numpy as jnp
from jax import lax
from jax.experimental import pallas as pl
from jax.experimental.pallas import tpu as pltpu
from jax.sharding import Mesh
from jax.sharding import PartitionSpec as P

D = 768
HEADS = 12
HEAD_DIM = 64
BLOCK = 64
SLOTS = 8
norm_epsilon = 1e-12
masked_score = -1e30
f32 = jnp.float32
bf16 = jnp.bfloat16


def dot_nn(left, right):
    return lax.dot_general(left, right, (((1,), (0,)), ((), ())), preferred_element_type=f32)


def dot_nt(left, right):
    return lax.dot_general(left, right, (((1,), (1,)), ((), ())), preferred_element_type=f32)


def dot_tn(left, right):
    return lax.dot_general(left, right, (((0,), (0,)), ((), ())), preferred_element_type=f32)


def layer_norm(values, scaling, offset):
    center = values - jnp.mean(values, axis=-1, keepdims=True)
    spread = jnp.mean(center * center, axis=-1, keepdims=True)
    return center * lax.rsqrt(spread + norm_epsilon) * scaling + offset


def block_plan(length, randoms, flip, query_blocks):
    blocks = randoms.shape[0]
    last = (length + BLOCK - 1) // BLOCK - 1
    places = jnp.arange(query_blocks, dtype=jnp.int32) ^ flip
    own_randoms = jnp.take_along_axis(randoms, places[:, None], axis=0)
    zero = jnp.zeros((query_blocks,), jnp.int32)
    candidates = jnp.concatenate(
        [
            jnp.stack([places - 1, places, places + 1, zero, zero + last], axis=1),
            own_randoms,
        ],
        axis=1,
    )
    usable = (candidates >= 0) & (candidates < blocks)
    same = candidates[:, :, None] == candidates[:, None, :]
    before = jnp.arange(SLOTS)[:, None] > jnp.arange(SLOTS)[None, :]
    usable = usable & ~jnp.any(same & before[None], axis=2)
    is_global = (places == 0) | (places == last)
    usable = usable & ~is_global[:, None]
    names = jnp.clip(candidates, 0, blocks - 1) ^ flip
    global_name = jnp.where((flip ^ last) < query_blocks, flip ^ last, flip)
    every = jnp.arange(blocks, dtype=jnp.int32).reshape(blocks // SLOTS, SLOTS)
    query_names = jnp.concatenate(
        [
            jnp.arange(query_blocks, dtype=jnp.int32),
            jnp.zeros((blocks // SLOTS,), jnp.int32) + global_name,
        ]
    )
    key_names = jnp.concatenate([names, every])
    bias_names = jnp.concatenate([jnp.where(usable, names, blocks), every])
    return query_names, key_names, bias_names, global_name.reshape(1)


GROUPS = ((0, 256), (256, 128))


def spread_heads(rows):
    lane = lax.broadcasted_iota(jnp.int32, rows.shape, 1)
    zero = jnp.zeros_like(rows)
    heads = rows.shape[1] // HEAD_DIM
    return jnp.concatenate([jnp.where(lane // HEAD_DIM == head, rows, zero) for head in range(heads)], axis=0)


def join_heads(stacked):
    width = stacked.shape[1]
    lane = lax.broadcasted_iota(jnp.int32, (BLOCK, width), 1)
    joined = stacked[:BLOCK]
    for head in range(1, width // HEAD_DIM):
        joined = jnp.where(lane // HEAD_DIM == head, stacked[head * BLOCK : (head + 1) * BLOCK], joined)
    return joined


def wide(bias, width):
    return jnp.concatenate([bias] * (width // bias.shape[1]), axis=1)


def lanes_spec(rows, first, width):
    return pl.BlockSpec((rows, width), lambda step, *_: (0, first // width))


def block_rows(name):
    return pl.ds(pl.multiple_of(name * BLOCK, BLOCK), BLOCK)


def gather_blocks(ref, names):
    return jnp.concatenate([ref[block_rows(name), :] for name in names], axis=0)


def fill_length_bias(bias_scratch, length, flip):
    rows = bias_scratch.shape[0] - BLOCK
    place = lax.broadcasted_iota(jnp.int32, bias_scratch.shape, 0)
    token = (((place // BLOCK) ^ flip) * BLOCK) + place % BLOCK
    live = (token < length) & (place < rows)
    bias_scratch[...] = jnp.where(live, 0.0, masked_score)


def forward_kernel(
    key_names, bias_names, global_name, lengths, flips,
    q_ref, k_ref, v_ref, context_ref, logsum_ref, bias_scratch, score_scratch, *, unroll, query_blocks,
):
    width = q_ref.shape[1]
    fill_length_bias(bias_scratch, lengths[0], flips[0])

    def put(block, context, largest, total):
        context_ref[block_rows(block), :] = join_heads(context).astype(bf16)
        logsum_ref[pl.ds(block, 1), :] = largest + jnp.log(total)

    def one(block):
        queries = spread_heads(q_ref[block_rows(block), :])
        names = [key_names[block, slot] for slot in range(SLOTS)]
        biases = [bias_names[block, slot] for slot in range(SLOTS)]
        scores = dot_nt(gather_blocks(k_ref, names), queries) + wide(gather_blocks(bias_scratch, biases), width)
        largest = jnp.max(scores, axis=0, keepdims=True)
        weights = jnp.exp(scores - largest)
        total = jnp.sum(weights, axis=0, keepdims=True)
        shares = (weights * (1.0 / total)).astype(bf16)
        put(block, dot_tn(shares, gather_blocks(v_ref, names)), largest, total)

    def body(step, carry):
        for within in range(unroll):
            one(step * unroll + within)
        return carry

    lax.fori_loop(0, query_blocks // unroll, body, 0)
    block = global_name[0]
    queries = spread_heads(q_ref[block_rows(block), :])
    tokens = k_ref.shape[0]
    chunk = SLOTS * BLOCK
    together = 4

    def score_chunk(step, largest):
        for within in range(together):
            rows = pl.ds(pl.multiple_of((step * together + within) * chunk, chunk), chunk)
            scores = dot_nt(k_ref[rows, :], queries) + wide(bias_scratch[rows, :], width)
            score_scratch[rows, :] = scores
            largest = jnp.maximum(largest, jnp.max(scores, axis=0, keepdims=True))
        return largest

    steps = tokens // chunk // together
    lanes = width
    largest = lax.fori_loop(0, steps, score_chunk, jnp.full((1, lanes), masked_score, f32))

    def value_chunk(step, carry):
        total, context = carry
        for within in range(together):
            rows = pl.ds(pl.multiple_of((step * together + within) * chunk, chunk), chunk)
            weights = jnp.exp(score_scratch[rows, :] - largest)
            total = total + jnp.sum(weights, axis=0, keepdims=True)
            context = context + dot_tn(weights.astype(bf16), v_ref[rows, :])
        return total, context

    total, context = lax.fori_loop(
        0, steps, value_chunk, (jnp.zeros((1, lanes), f32), jnp.zeros((lanes, lanes), f32))
    )
    context = context * jnp.transpose(jnp.broadcast_to(1.0 / total, (lanes, lanes)))
    put(block, context, largest, total)


def attend(plan, length, flip, group, q, k, v):
    first, width = group
    query_names, key_names, bias_names, global_name = plan
    query_rows = q.shape[0]
    tokens = k.shape[0]
    query_blocks = query_rows // BLOCK
    k_spec = lanes_spec(tokens, first, width)
    return pl.pallas_call(
        partial(forward_kernel, unroll=query_blocks, query_blocks=query_blocks),
        grid_spec=pltpu.PrefetchScalarGridSpec(
            num_scalar_prefetch=5,
            grid=(1,),
            in_specs=[lanes_spec(query_rows, first, width), k_spec, k_spec],
            out_specs=[lanes_spec(query_rows, 0, width), lanes_spec(query_blocks, 0, width)],
            scratch_shapes=[
                pltpu.VMEM((tokens + BLOCK, 128), f32),
                pltpu.VMEM((tokens, width), f32),
            ],
        ),
        out_shape=[
            jax.ShapeDtypeStruct((query_rows, width), bf16),
            jax.ShapeDtypeStruct((query_blocks, width), f32),
        ],
        compiler_params=pltpu.CompilerParams(vmem_limit_bytes=60 << 20),
        cost_estimate=pl.CostEstimate(flops=10**9, bytes_accessed=10**6, transcendentals=10**5),
        name="attend_forward",
    )(key_names, bias_names, global_name, length, flip, q, k, v)


def backward_kernel(
    query_names, key_names, bias_names, lengths, flips,
    q_ref, k_ref, v_ref, back_ref, context_ref, logsum_ref,
    back_q_ref, back_k_ref, back_v_ref, bias_scratch, q_scratch, k_scratch, v_scratch, *, unroll, items,
):
    width = q_ref.shape[1]
    fill_length_bias(bias_scratch, lengths[0], flips[0])
    q_scratch[...] = jnp.zeros_like(q_scratch)
    k_scratch[...] = jnp.zeros_like(k_scratch)
    v_scratch[...] = jnp.zeros_like(v_scratch)
    ones = jnp.ones((16, width), bf16)

    def one(item):
        block = query_names[item]
        rows = block_rows(block)
        queries = spread_heads(q_ref[rows, :])
        back = back_ref[rows, :]
        backs = spread_heads(back)
        product = (back.astype(f32) * context_ref[rows, :].astype(f32)).astype(bf16)
        inner = dot_nt(ones, spread_heads(product))[0:1]
        logsum = logsum_ref[pl.ds(block, 1), :]
        names = [key_names[item, slot] for slot in range(SLOTS)]
        biases = [bias_names[item, slot] for slot in range(SLOTS)]
        keys = gather_blocks(k_ref, names)
        scores = dot_nt(keys, queries) + wide(gather_blocks(bias_scratch, biases), width)
        shares = jnp.exp(scores - logsum)
        back_shares = dot_nt(gather_blocks(v_ref, names), backs)
        back_values = dot_nn(shares.astype(bf16), backs)
        back_scores = (shares * (back_shares - inner)).astype(bf16)
        back_keys = dot_nn(back_scores, queries)
        q_scratch[rows, :] += join_heads(dot_tn(back_scores, keys))
        for slot in range(SLOTS):
            part = slice(slot * BLOCK, (slot + 1) * BLOCK)
            v_scratch[block_rows(names[slot]), :] += back_values[part]
            k_scratch[block_rows(names[slot]), :] += back_keys[part]

    def body(step, carry):
        for within in range(unroll):
            one(step * unroll + within)
        return carry

    lax.fori_loop(0, items // unroll, body, 0)
    back_q_ref[...] = (q_scratch[...] * HEAD_DIM ** (-0.5)).astype(bf16)
    back_k_ref[...] = k_scratch[...].astype(bf16)
    back_v_ref[...] = v_scratch[...].astype(bf16)


def attend_back(plan, length, flip, group, q, k, v, back, context, logsum):
    first, width = group
    query_names, key_names, bias_names, _ = plan
    query_rows = q.shape[0]
    tokens = k.shape[0]
    query_blocks = query_rows // BLOCK
    q_in, k_in = lanes_spec(query_rows, first, width), lanes_spec(tokens, first, width)
    q_out, k_out = lanes_spec(query_rows, 0, width), lanes_spec(tokens, 0, width)
    return pl.pallas_call(
        partial(backward_kernel, unroll=8, items=query_names.shape[0]),
        grid_spec=pltpu.PrefetchScalarGridSpec(
            num_scalar_prefetch=5,
            grid=(1,),
            in_specs=[q_in, k_in, k_in, q_in, q_out, lanes_spec(query_blocks, 0, width)],
            out_specs=[q_out, k_out, k_out],
            scratch_shapes=[
                pltpu.VMEM((tokens + BLOCK, 128), f32),
                pltpu.VMEM((query_rows, width), f32),
                pltpu.VMEM((tokens, width), f32),
                pltpu.VMEM((tokens, width), f32),
            ],
        ),
        out_shape=[
            jax.ShapeDtypeStruct((query_rows, width), bf16),
            jax.ShapeDtypeStruct((tokens, width), bf16),
            jax.ShapeDtypeStruct((tokens, width), bf16),
        ],
        compiler_params=pltpu.CompilerParams(vmem_limit_bytes=60 << 20),
        cost_estimate=pl.CostEstimate(flops=10**9, bytes_accessed=10**6, transcendentals=10**5),
        name="attend_backward",
    )(query_names, key_names, bias_names, length, flip, q, k, v, back, context, logsum)


def project_kernel(core, x_ref, x_near_ref, w_q, w_k, w_v, b_q, b_v, q_ref, k_ref, v_ref):
    step = pl.program_id(0)

    def project(tile):
        q = (dot_nn(tile, w_q[...]) + b_q[...]).astype(bf16)
        q_ref[...] = q * jnp.asarray(HEAD_DIM ** (-0.5), bf16)
        k_ref[...] = dot_nn(tile, w_k[...]).astype(bf16)
        v_ref[...] = (dot_nn(tile, w_v[...]) + b_v[...]).astype(bf16)

    @pl.when(step < pl.num_programs(0) // 2)
    def _():
        project(x_ref[...])

    @pl.when(step >= pl.num_programs(0) // 2)
    def _():
        project(x_near_ref[...])


def project_far_kernel(core, x_ref, x_near_ref, w_k, w_v, b_v, k_old, v_old, k_ref, v_ref):
    step = pl.program_id(0)

    def project(tile):
        k_ref[...] = dot_nn(tile, w_k[...]).astype(bf16)
        v_ref[...] = (dot_nn(tile, w_v[...]) + b_v[...]).astype(bf16)

    @pl.when(step < pl.num_programs(0) // 2)
    def _():
        project(x_ref[...])

    @pl.when(step >= pl.num_programs(0) // 2)
    def _():
        project(x_near_ref[...])


TILE = 512


def piece_spec(piece, per, width):
    return pl.BlockSpec((TILE, width), lambda step, *_: (jnp.clip(step - piece * per, 0, per - 1), 0))


def own_weight(which):
    return pl.BlockSpec((D, D // 2), lambda step, core, *_: (0, 2 * which + core[0]))


def own_bias():
    return pl.BlockSpec((1, D // 2), lambda step, core, *_: (0, core[0]))


def project_chip(core, x, x_near, qkv_weight, query_bias, value_bias):
    rows = x.shape[0]
    half = D // 2
    per = rows // TILE
    out = pl.BlockSpec((TILE, half), lambda step, *_: (step, 0))
    return pl.pallas_call(
        project_kernel,
        grid_spec=pltpu.PrefetchScalarGridSpec(
            num_scalar_prefetch=1,
            grid=(2 * per,),
            in_specs=[piece_spec(0, per, D), piece_spec(1, per, D)]
            + [own_weight(0), own_weight(1), own_weight(2), own_bias(), own_bias()],
            out_specs=[out, out, out],
        ),
        out_shape=[
            jax.ShapeDtypeStruct((2 * rows, half), bf16),
            jax.ShapeDtypeStruct((4 * rows, half), bf16),
            jax.ShapeDtypeStruct((4 * rows, half), bf16),
        ],
        compiler_params=pltpu.CompilerParams(vmem_limit_bytes=60 << 20),
        cost_estimate=pl.CostEstimate(flops=4 * 10**9, bytes_accessed=10**7, transcendentals=0),
        name="project_chip",
    )(core, x, x_near, qkv_weight, qkv_weight, qkv_weight, query_bias, value_bias)


def project_far(core, x_far, x_far_near, qkv_weight, value_bias, k, v):
    rows = x_far.shape[0]
    half = D // 2
    per = rows // TILE
    out = pl.BlockSpec((TILE, half), lambda step, *_: (2 * per + step, 0))
    kept = pl.BlockSpec(memory_space=pl.ANY)
    return pl.pallas_call(
        project_far_kernel,
        grid_spec=pltpu.PrefetchScalarGridSpec(
            num_scalar_prefetch=1,
            grid=(2 * per,),
            in_specs=[piece_spec(0, per, D), piece_spec(1, per, D)]
            + [own_weight(1), own_weight(2), own_bias(), kept, kept],
            out_specs=[out, out],
        ),
        out_shape=[jax.ShapeDtypeStruct(k.shape, bf16), jax.ShapeDtypeStruct(v.shape, bf16)],
        input_output_aliases={6: 0, 7: 1},
        compiler_params=pltpu.CompilerParams(vmem_limit_bytes=60 << 20),
        cost_estimate=pl.CostEstimate(flops=3 * 10**9, bytes_accessed=10**7, transcendentals=0),
        name="project_far",
    )(core, x_far, x_far_near, qkv_weight, qkv_weight, value_bias, k, v)


def gelu_pair(x):
    t = 1.0 / (1.0 + (0.3275911 * 0.5**0.5) * jnp.abs(x))
    bell = jnp.exp(-0.5 * x * x)
    poly = 0.7107068705 + t * (-0.7265760135 + t * 0.5307027145)
    tail = t * (0.127414796 + t * (-0.142248368 + t * poly)) * bell
    cdf = jnp.where(x < 0, tail, 1.0 - tail)
    return x * cdf, cdf + x * bell * 0.3989422804014327


def norm_parts(value):
    center = value - jnp.mean(value, axis=-1, keepdims=True)
    spread = jnp.mean(center * center, axis=-1, keepdims=True)
    scale = lax.rsqrt(spread + norm_epsilon)
    return center * scale, scale


def norm_back(slope, normed, scale):
    along = jnp.mean(slope * normed, axis=-1, keepdims=True)
    return scale * (slope - jnp.mean(slope, axis=-1, keepdims=True) - normed * along)


def column_sum(value):
    return jnp.sum(value, axis=0, keepdims=True)


PIECES = 16
VECTOR_ROWS = 128


def row_spec(tile, width):
    return pl.BlockSpec((tile, width), lambda step, *_: (step, 0))


def stack_spec(count, tile, width):
    return pl.BlockSpec((count, tile, width), lambda step, *_: (0, step, 0))


def whole_spec(shape):
    return pl.BlockSpec(shape, lambda step, *_: (0,) * len(shape))


def middle_kernel(
    core,
    own_ref, own_more, other_ref, other_more,
    x_ref, cot_ref, vector_ref, expand_bias_ref, proj_hbm, expand_hbm, shrink_hbm,
    output_ref, back_one_ref, back_own_ref, back_other_ref, wide_keep, wide_send, lows_ref, sums_ref,
    proj_w, expand_w, shrink_w, slope_s, wide_s, weight_sems, wide_sems, *, chunk,
):
    step = pl.program_id(0)
    half = D // 2
    ff = expand_w.shape[1]
    chunks = ff // chunk
    hc = core[0]
    loads = [
        pltpu.make_async_copy(proj_hbm.at[pl.ds(hc * half, half)], proj_w.at[pl.ds(0, half)], weight_sems.at[0]),
        pltpu.make_async_copy(
            proj_hbm.at[pl.ds((1 - hc) * half, half)], proj_w.at[pl.ds(half, half)], weight_sems.at[1]
        ),
        pltpu.make_async_copy(expand_hbm, expand_w, weight_sems.at[2]),
        pltpu.make_async_copy(shrink_hbm, shrink_w, weight_sems.at[3]),
    ]

    @pl.when(step == 0)
    def _():
        for load in loads:
            load.start()
        sums_ref[...] = jnp.zeros_like(sums_ref)
        for load in loads:
            load.wait()

    def vector(row):
        return vector_ref[pl.ds(row, 1), :]

    slot = lax.rem(step, 2)
    tile = x_ref.shape[0]

    def wide_copies(slot, first_row):
        copies = []
        for which in range(2):
            for side, out in enumerate((wide_keep, wide_send)):
                first = pl.multiple_of((hc if side == 0 else 1 - hc) * (ff // 2), ff // 2)
                copies.append(
                    pltpu.make_async_copy(
                        wide_s.at[slot, which, :, pl.ds(first, ff // 2)],
                        out.at[which, pl.ds(pl.multiple_of(first_row, tile), tile)],
                        wide_sems.at[slot, 2 * which + side],
                    )
                )
        return copies

    @pl.when(step >= 2)
    def _():
        for copy in wide_copies(slot, 0):
            copy.wait()

    context = jnp.concatenate([ref[...] for ref in (own_ref, own_more, other_ref, other_more)], axis=1)
    resid = x_ref[...].astype(f32) + dot_nn(context, proj_w[...]) + vector(0)
    normed_one, scale_one = norm_parts(resid)
    hidden = normed_one * vector(1) + vector(2)
    low = hidden.astype(bf16)
    lows_ref[0] = low
    resid_two = hidden + vector(3)

    for part in range(chunks):
        cols = slice(part * chunk, (part + 1) * chunk)
        inner = dot_nn(low, expand_w[:, cols]) + expand_bias_ref[:, cols]
        active, slope = gelu_pair(inner)
        active = active.astype(bf16)
        wide_s[slot, 0, :, cols] = active
        slope_s[:, cols] = slope.astype(bf16)
        resid_two = resid_two + dot_nn(active, shrink_w[cols, :])
    normed_two, scale_two = norm_parts(resid_two)
    output_ref[...] = (normed_two * vector(4) + vector(5)).astype(bf16)
    cot = cot_ref[...].astype(f32)
    back_two = norm_back(vector(4) * cot, normed_two, scale_two)
    low_two = back_two.astype(bf16)
    lows_ref[1] = low_two
    sums_ref[3:4, :] += column_sum(low_two.astype(f32))
    sums_ref[4:5, :] += column_sum(cot * normed_two)
    sums_ref[5:6, :] += column_sum(cot)
    back = back_two
    for part in range(chunks):
        cols = slice(part * chunk, (part + 1) * chunk)
        back_inner = (dot_nt(low_two, shrink_w[cols, :]) * slope_s[:, cols].astype(f32)).astype(bf16)
        wide_s[slot, 1, :, cols] = back_inner
        sums_ref[8 + part : 9 + part, :] += column_sum(back_inner.astype(f32))
        back = back + dot_nt(back_inner, expand_w[:, cols])
    sums_ref[1:2, :] += column_sum(back * normed_one)
    sums_ref[2:3, :] += column_sum(back)
    back_one = norm_back(vector(1) * back, normed_one, scale_one)
    back_one_ref[...] = back_one
    low_one = back_one.astype(bf16)
    lows_ref[2] = low_one
    sums_ref[0:1, :] += column_sum(low_one.astype(f32))
    back_context = dot_nt(low_one, proj_w[...]).astype(bf16)
    back_own_ref[...] = back_context[:, :half]
    back_other_ref[...] = back_context[:, half:]
    for copy in wide_copies(slot, step * tile):
        copy.start()

    @pl.when(step == pl.num_programs(0) - 1)
    def _():
        for other in range(2):
            for copy in wide_copies(other, 0):
                copy.wait()


def middle(core, own, other, x, cot, vectors, expand_bias, proj_weight, expand_weight, shrink_weight):
    rows = x.shape[0]
    ff = expand_weight.shape[1]
    half = D // 2
    tile = 256
    kept = pl.BlockSpec(memory_space=pl.ANY)
    assert ff // D == 4
    return pl.pallas_call(
        partial(middle_kernel, chunk=D),
        grid_spec=pltpu.PrefetchScalarGridSpec(
            num_scalar_prefetch=1,
            grid=(rows // tile,),
            in_specs=[row_spec(tile, width) for _, width in GROUPS] * 2
            + [row_spec(tile, D)] * 2
            + [whole_spec(vectors.shape), whole_spec(expand_bias.shape), kept, kept, kept],
            out_specs=[row_spec(tile, D)] * 2
            + [row_spec(tile, half)] * 2
            + [kept] * 2
            + [stack_spec(3, tile, D), whole_spec((16, D))],
            scratch_shapes=[
                pltpu.VMEM((D, D), bf16),
                pltpu.VMEM((D, ff), bf16),
                pltpu.VMEM((ff, D), bf16),
                pltpu.VMEM((tile, ff), bf16),
                pltpu.VMEM((2, 2, tile, ff), bf16),
                pltpu.SemaphoreType.DMA((4,)),
                pltpu.SemaphoreType.DMA((2, 4)),
            ],
        ),
        out_shape=[
            jax.ShapeDtypeStruct((rows, D), bf16),
            jax.ShapeDtypeStruct((rows, D), f32),
            jax.ShapeDtypeStruct((rows, half), bf16),
            jax.ShapeDtypeStruct((rows, half), bf16),
            jax.ShapeDtypeStruct((2, rows, ff // 2), bf16),
            jax.ShapeDtypeStruct((2, rows, ff // 2), bf16),
            jax.ShapeDtypeStruct((3, rows, D), bf16),
            jax.ShapeDtypeStruct((16, D), f32),
        ],
        compiler_params=pltpu.CompilerParams(vmem_limit_bytes=60 << 20),
        cost_estimate=pl.CostEstimate(flops=10**9, bytes_accessed=10**7, transcendentals=10**6),
        name="middle",
    )(core, *own, *other, x, cot, vectors, expand_bias, proj_weight, expand_weight, shrink_weight)


def weights_kernel(
    places, wide_own, wide_other, lows_own, lows_other, context_ref, context_more, sums_own, sums_other, *refs
):
    packed = refs[:4]
    shrink_g, expand_g, proj_g = refs[4:]
    step = pl.program_id(0)
    half = D // 2

    @pl.when(step == 0)
    def _():
        shrink_g[...] = jnp.zeros_like(shrink_g)
        expand_g[...] = jnp.zeros_like(expand_g)
        proj_g[...] = jnp.zeros_like(proj_g)
        proj_g[half : half + 16, :] = sums_own[...] + sums_other[...]

    def add(wide, lows):
        shrink_g[...] += dot_tn(wide[0], lows[1])
        expand_g[...] += dot_tn(lows[0], wide[1])
        context = jnp.concatenate([context_ref[...], context_more[...]], axis=1)
        proj_g[:half, :] += dot_tn(context, lows[2])

    @pl.when(step < pl.num_programs(0) // 2)
    def _():
        add(wide_own, lows_own)

    @pl.when(step >= pl.num_programs(0) // 2)
    def _():
        add(wide_other, lows_other)

    @pl.when(step == pl.num_programs(0) - 1)
    def _():
        rows = shrink_g.shape[0] // PIECES
        extra = proj_g.shape[0] // (2 * PIECES)
        wide = expand_g.shape[1] // D
        for piece in range(PIECES):
            place = piece % (PIECES // 2)
            first = piece ^ places[0]
            second = piece ^ places[1]
            out = packed[piece // (PIECES // 2)]
            out[place, :rows, :] = shrink_g[pl.ds(pl.multiple_of(first * rows, rows), rows), :].astype(bf16)
            out[place, rows:, :] = proj_g[pl.ds(pl.multiple_of(first * extra, extra), extra), :].astype(bf16)
            out = packed[2 + piece // (PIECES // 2)]
            down = pl.ds(pl.multiple_of((second // wide) * rows, rows), rows)
            across = pl.ds(pl.multiple_of(lax.rem(second, wide) * D, D), D)
            out[place, :rows, :] = expand_g[down, across].astype(bf16)
            part = pl.ds(pl.multiple_of((PIECES + second) * extra, extra), extra)
            out[place, rows:, :] = proj_g[part, :].astype(bf16)


def weight_grads(places, wide_own, wide_other, lows_own, lows_other, context, sums_own, sums_other):
    _, rows, wide = wide_own.shape
    half = D // 2
    per = rows // TILE
    piece_rows = wide // PIECES + (half + VECTOR_ROWS) // (2 * PIECES)

    def own(count, width):
        return pl.BlockSpec((count, TILE, width), lambda step, *_: (0, jnp.minimum(step, per - 1), 0))

    def other(count, width):
        return pl.BlockSpec((count, TILE, width), lambda step, *_: (0, jnp.maximum(step - per, 0), 0))

    packed_shape = (PIECES // 2, piece_rows, D)
    return pl.pallas_call(
        weights_kernel,
        grid_spec=pltpu.PrefetchScalarGridSpec(
            num_scalar_prefetch=1,
            grid=(2 * per,),
            in_specs=[own(2, wide), other(2, wide), own(3, D), other(3, D)]
            + [row_spec(TILE, width) for _, width in GROUPS]
            + [whole_spec((16, D))] * 2,
            out_specs=[whole_spec(packed_shape)] * 4,
            scratch_shapes=[
                pltpu.VMEM((wide, D), f32),
                pltpu.VMEM((D, wide), f32),
                pltpu.VMEM((half + VECTOR_ROWS, D), f32),
            ],
        ),
        out_shape=[jax.ShapeDtypeStruct(packed_shape, bf16)] * 4,
        compiler_params=pltpu.CompilerParams(vmem_limit_bytes=60 << 20),
        cost_estimate=pl.CostEstimate(flops=10**9, bytes_accessed=10**7, transcendentals=0),
        name="weight_grads",
    )(places, wide_own, wide_other, lows_own, lows_other, *context, sums_own, sums_other)


def halves_spec(per):
    return [
        pl.BlockSpec((TILE, D), lambda step, *_: (jnp.minimum(step, per - 1), 0)),
        pl.BlockSpec((TILE, D), lambda step, *_: (jnp.maximum(step - per, 0), 0)),
    ]


def input_kernel(core, *refs, count, per):
    weights, arrays, outs = refs[:count], refs[count:-2], refs[-2:]
    pairs = len(arrays) // count
    step = pl.program_id(0)
    total = None
    for which in range(count):
        back = jnp.concatenate([ref[...] for ref in arrays[which * pairs : (which + 1) * pairs]], axis=1)
        part = dot_nt(back, weights[which][...])
        total = part if total is None else total + part

    @pl.when(step < per)
    def _():
        outs[0][...] = total.astype(bf16)

    @pl.when(step >= per)
    def _():
        outs[1][...] = total.astype(bf16)


def input_part(core, qkv_weight, groups, weights, first, rows, name):
    arrays = [array for group in groups for array in group]
    tokens = [pl.BlockSpec((TILE, array.shape[1]), lambda step, *_: (first // TILE + step, 0)) for array in arrays]
    per = rows // TILE
    half_shape = jax.ShapeDtypeStruct((rows, D), bf16)
    return pl.pallas_call(
        partial(input_kernel, count=len(groups), per=per),
        grid_spec=pltpu.PrefetchScalarGridSpec(
            num_scalar_prefetch=1,
            grid=(2 * per,),
            in_specs=[own_weight(which) for which in weights] + tokens,
            out_specs=halves_spec(per),
        ),
        out_shape=[half_shape, half_shape],
        compiler_params=pltpu.CompilerParams(vmem_limit_bytes=60 << 20),
        cost_estimate=pl.CostEstimate(flops=10**9, bytes_accessed=10**7, transcendentals=0),
        name=name,
    )(core, *[qkv_weight] * len(weights), *arrays)


QKV_PIECES = 16


def joined_kernel(places, core, *refs, tiles, pairs):
    x_refs = refs[:4]
    arrays = refs[4 : 4 + 3 * pairs]
    packed = refs[4 + 3 * pairs : 8 + 3 * pairs]
    total, sums = refs[8 + 3 * pairs :]
    step = pl.program_id(0)
    half = D // 2
    per = tiles // 4

    @pl.when(step == 0)
    def _():
        total[...] = jnp.zeros_like(total)
        sums[...] = jnp.zeros_like(sums)

    def joined(first, last):
        return jnp.concatenate([ref[...] for ref in arrays[first * pairs : last * pairs]], axis=1)

    for piece in range(4):

        @pl.when((step >= piece * per) & (step < (piece + 1) * per))
        def _():
            first = 0 if piece < 2 else 1
            back = joined(first, 3)
            total[:, first * half : 3 * half] += dot_tn(x_refs[piece][...], back)
            sums[0:1, first * half :] += column_sum(back.astype(f32))

    @pl.when(step == tiles - 1)
    def _():
        rows = D // QKV_PIECES
        q_sums = jnp.transpose(jnp.broadcast_to(sums[0:1, :half], (128, half)))
        v_sums = jnp.transpose(jnp.broadcast_to(sums[0:1, 2 * half :], (128, half)))
        total[:half, 3 * half :] = q_sums
        total[half:, 3 * half :] = v_sums
        width = packed[0].shape[2]
        for color in range(2):
            cols = slice(color * width, (color + 1) * width)
            for piece in range(QKV_PIECES):
                part = pl.ds(pl.multiple_of((piece ^ places[color]) * rows, rows), rows)
                out = packed[2 * color + piece // (QKV_PIECES // 2)]
                out[piece % (QKV_PIECES // 2)] = total[part, cols].astype(bf16)


def joined_grads(places, core, xs, back_qs, back_ks, back_vs):
    rows = xs[0].shape[0]
    pairs = len(back_qs)
    per = rows // TILE
    tiles = 4 * per
    width = D // 2 + 256
    tokens = [row_spec(TILE, array.shape[1]) for array in back_ks]
    queries = [
        pl.BlockSpec((TILE, array.shape[1]), lambda step, *_: (jnp.minimum(step, 2 * per - 1), 0)) for array in back_qs
    ]
    packed = pl.BlockSpec((QKV_PIECES // 2, D // QKV_PIECES, width), lambda step, *_: (0, 0, 0))
    packed_shape = jax.ShapeDtypeStruct((QKV_PIECES // 2, D // QKV_PIECES, width), bf16)
    return pl.pallas_call(
        partial(joined_kernel, tiles=tiles, pairs=pairs),
        grid_spec=pltpu.PrefetchScalarGridSpec(
            num_scalar_prefetch=2,
            grid=(tiles,),
            in_specs=[piece_spec(piece, per, D) for piece in range(4)] + queries + 2 * tokens,
            out_specs=[packed] * 4,
            scratch_shapes=[pltpu.VMEM((D, 2 * width), f32), pltpu.VMEM((8, 3 * D // 2), f32)],
        ),
        out_shape=[packed_shape] * 4,
        compiler_params=pltpu.CompilerParams(vmem_limit_bytes=60 << 20),
        cost_estimate=pl.CostEstimate(flops=10**9, bytes_accessed=10**7, transcendentals=0),
        name="joined_grads",
    )(places, core, *xs, *back_qs, *back_ks, *back_vs)


def input_near_kernel(core, *refs):
    w_q, w_k, w_v, out = refs[0], refs[1], refs[2], refs[-1]
    arrays = refs[3:-1]
    pairs = len(arrays) // 3

    def joined(which):
        return jnp.concatenate([ref[...] for ref in arrays[which * pairs : (which + 1) * pairs]], axis=1)

    out[...] = (dot_nt(joined(0), w_q[...]) + dot_nt(joined(1), w_k[...]) + dot_nt(joined(2), w_v[...])).astype(bf16)


def input_near(core, qkv_weight, back_qs, back_ks, back_vs):
    rows = back_qs[0].shape[0]
    token = pl.BlockSpec((TILE, 128), lambda step, *_: (step, 0))
    arrays = list(back_qs) + list(back_ks) + list(back_vs)
    return pl.pallas_call(
        input_near_kernel,
        grid_spec=pltpu.PrefetchScalarGridSpec(
            num_scalar_prefetch=1,
            grid=(rows // TILE,),
            in_specs=[own_weight(0), own_weight(1), own_weight(2)] + [token] * len(arrays),
            out_specs=pl.BlockSpec((TILE, D), lambda step, *_: (step, 0)),
        ),
        out_shape=jax.ShapeDtypeStruct((rows, D), bf16),
        compiler_params=pltpu.CompilerParams(vmem_limit_bytes=60 << 20),
        cost_estimate=pl.CostEstimate(flops=10**9, bytes_accessed=10**7, transcendentals=0),
        name="input_near",
    )(core, qkv_weight, qkv_weight, qkv_weight, *arrays)


GROUP = 8


def unpack_kernel(numbers, *refs, parts, outs, held):
    sources = refs[:2]
    targets = refs[2 + held : 2 + held + outs]
    stages = refs[2 + held + outs : -1]
    sems = refs[-1]
    step = pl.program_id(0)
    count = numbers.shape[0] // 2 // GROUP
    at = lax.rem(step, 2)

    def copy(color, which, slot, number, elsewhere=False):
        part = parts[color][which]
        out, place = (part["instead"][1:]) if elsewhere else (part["out"], part["place"])
        row, col = place(number)
        rows, cols = part["rows"][1] - part["rows"][0], part["cols"][1] - part["cols"][0]
        target = targets[out].at[pl.ds(pl.multiple_of(row, rows), rows), pl.ds(pl.multiple_of(col, 128), cols)]
        at = part["at"]
        source = stages[color].at[slot, pl.ds(at[0], rows), pl.ds(at[1], cols)]
        return pltpu.make_async_copy(source, target, sems.at[color, which, slot])

    def wait(color, slot):
        for which in range(len(parts[color])):
            copy(color, which, slot, 0).wait()

    for color, source in enumerate(sources):

        @pl.when(step // count == color)
        def _():
            for within in range(GROUP):
                slot = lax.rem(step, 2) * GROUP + within
                number = numbers[step * GROUP + within]

                @pl.when(step - color * count >= 2)
                def _():
                    wait(color, slot)

                stages[color][slot] = source[within].astype(f32)
                for which, part in enumerate(parts[color]):
                    if part["instead"] is None:
                        copy(color, which, slot, number).start()
                        continue
                    elsewhere = part["instead"][0](number)

                    @pl.when(elsewhere)
                    def _():
                        copy(color, which, slot, number, True).start()

                    @pl.when(jnp.logical_not(elsewhere))
                    def _():
                        copy(color, which, slot, number).start()

    @pl.when(step == pl.num_programs(0) - 1)
    def _():
        for color in range(2):
            for slot in range(min(2, count) * GROUP):
                wait(color, slot)


def unpack(numbers, sources, parts, out_shapes, held, name):
    count, rows, width = sources[0].shape
    groups = count // GROUP
    assert groups == 2
    most = max(len(part) for part in parts)
    kept = pl.BlockSpec(memory_space=pl.ANY)
    return pl.pallas_call(
        partial(unpack_kernel, parts=parts, outs=len(out_shapes), held=len(held)),
        grid_spec=pltpu.PrefetchScalarGridSpec(
            num_scalar_prefetch=1,
            grid=(2 * groups,),
            in_specs=[
                pl.BlockSpec((GROUP, rows, width), lambda step, *_: (jnp.minimum(step, groups - 1), 0, 0)),
                pl.BlockSpec((GROUP, rows, width), lambda step, *_: (jnp.maximum(step - groups, 0), 0, 0)),
            ]
            + [kept] * len(held),
            out_specs=[kept] * len(out_shapes),
            scratch_shapes=[pltpu.VMEM((2 * GROUP, rows, width), f32)] * 2
            + [pltpu.SemaphoreType.DMA((2, most, 2 * GROUP))],
        ),
        out_shape=[jax.ShapeDtypeStruct(shape, f32) for shape in out_shapes],
        input_output_aliases={3 + place: place for place in range(len(held))},
        compiler_params=pltpu.CompilerParams(vmem_limit_bytes=60 << 20),
        cost_estimate=pl.CostEstimate(flops=10**6, bytes_accessed=10**6, transcendentals=0),
        name=name,
    )(numbers, *sources, *held)


def part_of(rows, cols, out, place, instead=None):
    return {"rows": rows, "cols": cols, "at": (rows[0], cols[0]), "out": out, "place": place, "instead": instead}


def swap(value, axis, bit=1):
    size = lax.axis_size(axis)
    return lax.ppermute(value, axis, [(place, place ^ bit) for place in range(size)])


def place_of(order):
    number = jnp.zeros((), jnp.int32)
    for axis, bit in order:
        number = 2 * number + ((lax.axis_index(axis) & bit) // bit).astype(jnp.int32)
    return number


def add_low(left, right):
    return (left.astype(f32) + right.astype(f32)).astype(bf16)


class Chain:
    def __init__(self, scatter_order, gather_order, keep, first):
        self.orders = list(scatter_order) + list(gather_order) + [("hc", 1)]
        self.steps = len(scatter_order)
        self.keep, self.first, self.arrived = keep, first, None
        self.at = 0
        self.gathered = None

    def left(self):
        return len(self.orders) - self.at

    def send(self):
        if self.at < self.steps:
            if self.at == 0:
                return self.first
            half = self.keep.shape[0] // 2
            high = add_low(self.keep[half:], self.arrived[half:])
            self.keep = add_low(self.keep[:half], self.arrived[:half])
            return high
        if self.at == self.steps:
            total = add_low(self.keep, self.arrived)
            bit = 8
            while bit < lax.axis_size("dp"):
                total = add_low(total, swap(total, "dp", bit))
                bit *= 2
            self.gathered = total
        else:
            self.gathered = jnp.concatenate([self.gathered, self.arrived], axis=0)
        return self.gathered

    def move(self, value):
        if self.at >= self.steps:
            self.gathered = value
        axis, bit = self.orders[self.at]
        self.arrived = swap(value, axis, bit)
        self.at += 1


def gathered_numbers(number, scatter_order, gather_order):
    count = 1 << len(scatter_order)
    places = jnp.arange(count, dtype=jnp.int32)
    turned = jnp.zeros((count,), jnp.int32)
    for at, name in enumerate(gather_order):
        turned = turned + (((places >> at) & 1) << (len(scatter_order) - 1 - scatter_order.index(name)))
    return turned ^ number


def ready(*values):
    return lax.optimization_barrier(values)


def per_device(
    inputs, doc_lengths, random_blocks, qkv_weight, query_bias, value_bias, proj_weight, proj_bias,
    first_gain, first_shift, expand_weight, expand_bias, shrink_weight, shrink_bias,
    second_gain, second_shift, cotangent,
):
    hx = lax.axis_index("hx")
    hc = lax.axis_index("hc")
    docs, rows, _ = inputs.shape
    assert docs == 1 and lax.axis_size("hx") == 2 and lax.axis_size("hc") == 2
    half = D // 2
    ff = expand_weight.shape[1]
    x = inputs.reshape(rows, D)
    x_far = swap(x, "hx")
    x_near = swap(x, "hc")
    row_blocks = rows // BLOCK
    flip = (hx * 2 + hc).astype(jnp.int32) * row_blocks
    plan = block_plan(doc_lengths[0], random_blocks[0], flip, 2 * row_blocks)
    flip = flip.reshape(1)
    core = hc.astype(jnp.int32).reshape(1)
    chip_steps = {"x": ("hx", 1), "y": ("dp", 1), "n": ("dp", 2), "f": ("dp", 4)}
    orders = {
        name: tuple([chip_steps[step] for step in part] for part in text.split())
        for name, text in ORDERS.items()
    }

    def places_of(letter):
        return jnp.stack([place_of(orders[f"{letter}{color}"][0]) for color in range(2)])

    def numbers_of(letter, places):
        own = [gathered_numbers(places[color], *orders[f"{letter}{color}"]) for color in range(2)]
        own = jnp.concatenate(own)
        return own + PIECES * core, own + PIECES * (1 - core)

    middle_places, joined_places = places_of("M"), places_of("Q")
    numbers = numbers_of("M", middle_places) + numbers_of("Q", joined_places)
    vectors = jnp.concatenate(
        [proj_bias, first_gain, first_shift, shrink_bias, second_gain, second_shift, query_bias, value_bias]
    ).reshape(8, D)
    vectors = vectors.astype(f32)
    bias_q, bias_v = vectors[6:7], vectors[7:8]
    expand_row = expand_bias.astype(f32).reshape(1, ff)

    q, k, v = project_chip(core, x, x_near, qkv_weight, bias_q, bias_v)
    x_far, q, expand_row, vectors, middle_places, joined_places, *rest = ready(
        x_far, q, expand_row, vectors, middle_places, joined_places, *numbers, *plan
    )
    numbers, plan = rest[:4], rest[4:]
    x_far_near = swap(x_far, "hc")
    k, v = project_far(core, x_far, x_far_near, qkv_weight, bias_v, k, v)
    context, logsum, other_context = [], [], []
    for group in GROUPS:
        if context:
            q = ready(q, context[0])[0]
        part, logs = attend(plan, doc_lengths, flip, group, q, k, v)
        context.append(part)
        logsum.append(logs)
        other_context.append(swap(part[rows:], "hc"))
    output, back_one, back_own, back_other, wide_keep, wide_send, lows, sums = middle(
        core, context, other_context, x, cotangent.reshape(rows, D), vectors,
        expand_row, proj_weight, expand_weight, shrink_weight,
    )
    from_other = swap(back_other, "hc")
    wide_send, lows_send, sums_send, from_other = ready(wide_send, lows, sums, from_other)
    back = jnp.concatenate([back_own, from_other], axis=0)
    wide_other, lows_other, sums_other = swap(wide_send, "hc"), swap(lows_send, "hc"), swap(sums_send, "hc")

    held = {"last": back}
    chains = {}

    def tie(value):
        value, held["last"] = ready(value, held["last"])
        return value

    def pairs_of(which):
        return [held["grads", pair][which] for pair in range(len(GROUPS))]

    def both(letter, side):
        return [getattr(chains[f"{letter}{color}"], side) for color in range(2)]

    rows_each, extra, wide = ff // 2 // PIECES, (D // 2 + VECTOR_ROWS) // (2 * PIECES), ff // 2 // D
    proj_pieces = half // extra

    def split(number):
        return number // PIECES, lax.rem(number, PIECES)

    def expand_place(number):
        side, piece = split(number)
        return piece // wide * rows_each, (side * wide + lax.rem(piece, wide)) * D

    def proj_place(color):
        def place(number):
            side, piece = split(number)
            return side * half + (color * PIECES + piece) * extra, number * 0

        return place

    def vector_place(number):
        side, piece = split(number)
        return (side * (2 * PIECES - proj_pieces) + PIECES + piece - proj_pieces) * extra, number * 0

    def joined_place(which, offset):
        def place(number):
            side, piece = split(number)
            return piece * (D // QKV_PIECES), which * D + side * half + offset

        return place

    def bias_place(number):
        side, piece = split(number)
        return (side * QKV_PIECES + piece) * (D // QKV_PIECES), number * 0

    each = D // QKV_PIECES
    middle_parts = [
        [
            part_of((0, rows_each), (0, D), 0, lambda n: (n * rows_each, n * 0)),
            part_of((rows_each, rows_each + extra), (0, D), 2, proj_place(0)),
        ],
        [
            part_of((0, rows_each), (0, D), 1, expand_place),
            part_of(
                (rows_each, rows_each + extra), (0, D), 2, proj_place(1),
                (lambda n: lax.rem(n, PIECES) >= proj_pieces - PIECES, 3, vector_place),
            ),
        ],
    ]
    joined_parts = [
        [
            part_of((0, each), (0, half), 0, joined_place(0, 0)),
            part_of((0, each), (half, half + 256), 0, joined_place(1, 0)),
        ],
        [
            part_of((0, each), (0, 128), 0, joined_place(1, 256)),
            part_of((0, each), (128, 128 + half), 0, joined_place(2, 0)),
            part_of((0, each), (128 + half, 256 + half), 1, bias_place),
        ],
    ]
    layouts = {
        "M": (middle_parts, [(ff, D), (D, ff), (D, D), (2 * VECTOR_ROWS, D)], numbers[:2]),
        "Q": (joined_parts, [(D, 3 * D), (2 * D, 128)], numbers[2:]),
    }

    def run(name):
        if name.startswith("attend"):
            pair = int(name[-1])
            held["grads", pair] = attend_back(
                plan, doc_lengths, flip, GROUPS[pair], q, k, v, tie(back), context[pair], logsum[pair]
            )
            held["last"] = held["grads", pair][0]
        elif name == "weights":
            packed = weight_grads(
                middle_places, tie(wide_keep), wide_other, lows, lows_other, context, sums, sums_other
            )
            held["last"] = packed[0]
            for color in range(2):
                chains[f"M{color}"] = Chain(*orders[f"M{color}"], packed[2 * color], packed[2 * color + 1])
        elif name == "joined":
            back_qs = pairs_of(0)
            back_qs[0] = tie(back_qs[0])
            packed = joined_grads(
                joined_places, core, (x, x_near, x_far, x_far_near), back_qs, pairs_of(1), pairs_of(2)
            )
            held["last"] = packed[0]
            for color in range(2):
                chains[f"Q{color}"] = Chain(*orders[f"Q{color}"], packed[2 * color], packed[2 * color + 1])
        elif name == "far":
            back_ks = pairs_of(1)
            back_ks[0] = tie(back_ks[0])
            mine, others = input_part(core, qkv_weight, (back_ks, pairs_of(2)), (1, 2), 2 * rows, rows, "input_far")
            held["last"] = mine
            held["far"] = mine, swap(others, "hc")
        elif name == "dx":
            value = tie(add_low(*held["far"]))
            held["last"] = value
            held["from_far"] = swap(value, "hx")
        elif name == "near":
            back_qs = pairs_of(0)
            back_qs[0] = tie(back_qs[0])
            groups = (back_qs, pairs_of(1), pairs_of(2))
            mine, others = input_part(core, qkv_weight, groups, (0, 1, 2), 0, rows, "input_near")
            held["last"] = mine
            held["near"] = mine, swap(others, "hc")
        elif name == "input":
            near, from_near = held["near"]
            near = tie(near)
            value = back_one + near.astype(f32) + from_near.astype(f32) + held["from_far"].astype(f32)
            held["last"] = held["input"] = value
        elif name.startswith("own") or name.startswith("other"):
            letter = name[-1]
            parts, shapes, places = layouts[letter]
            mine = name.startswith("own")
            sources = both(letter, "gathered" if mine else "arrived")
            sources[0] = tie(sources[0])
            held["out", letter] = unpack(
                places[0 if mine else 1], sources, parts, shapes, () if mine else held["out", letter],
                f"unpack_{letter}",
            )
            held["last"] = held["out", letter][0]
        else:
            chain = chains[name]
            value = tie(chain.send())
            chain.move(value)
            held["last"] = value

    for names in SEQUENCE:
        for name in names.split():
            run(name)
    assert all(chain.left() == 0 for chain in chains.values())
    grad_shrink, grad_expand, grad_proj, vector = held["out", "M"]
    grad_qkv, bias = held["out", "Q"]
    grad_query_bias = jnp.concatenate([bias[:half, 0], bias[D : D + half, 0]])
    grad_value_bias = jnp.concatenate([bias[half:D, 0], bias[D + half :, 0]])
    grad_expand_bias = vector[8 : 8 + ff // D].reshape(ff)
    return (
        output.reshape(docs, rows, D),
        held["input"].reshape(docs, rows, D),
        grad_qkv, grad_query_bias, grad_value_bias, grad_proj, vector[0], vector[1], vector[2],
        grad_expand, grad_expand_bias, grad_shrink, vector[3], vector[4], vector[5],
    )


ORDERS = {"M0": "xynf fnyx", "M1": "nfxy fyxn", "Q0": "xynf yfnx", "Q1": "nxyf xfny"}
SEQUENCE = (
    "attend0 weights M1 M0",
    "attend1 joined M1 Q1",
    "M0 Q0 far near",
    "M0 Q1 Q0 M1",
    "dx Q1 M0 Q0",
    "M1 Q1 Q0 M1",
    "Q1 Q0 M0 Q0",
    "M1 M0 M1 Q0",
    "Q1 M0 input Q0",
    "Q1 M1 M0 Q1",
    "Q0 Q1 ownQ otherQ",
    "M1 M0 ownM otherM",
)


def solution(mesh):
    dp = mesh.shape["dp"]
    heads = mesh.shape["heads"]
    split = Mesh(mesh.devices.reshape(dp, heads // 2, 2), ("dp", "hx", "hc"))
    rows = P("dp", ("hx", "hc"), None)
    in_specs = (rows, P("dp"), P("dp", None, None)) + (P(),) * 13 + (rows,)
    out_specs = (rows, rows) + (P(),) * 13
    return jax.shard_map(
        per_device, mesh=split, in_specs=in_specs, out_specs=out_specs, check_vma=False
    )
```

```python
from functools import partial

import jax
import jax.numpy as jnp
from jax import lax
from jax.experimental import pallas as pl
from jax.experimental.pallas import tpu as pltpu
from jax.sharding import Mesh
from jax.sharding import PartitionSpec as P

D = 768
HEADS = 12
HEAD_DIM = 64
BLOCK = 64
SLOTS = 8
norm_epsilon = 1e-12
masked_score = -1e30
f32 = jnp.float32
bf16 = jnp.bfloat16


def dot_nn(left, right):
    return lax.dot_general(left, right, (((1,), (0,)), ((), ())), preferred_element_type=f32)


def dot_nt(left, right):
    return lax.dot_general(left, right, (((1,), (1,)), ((), ())), preferred_element_type=f32)


def dot_tn(left, right):
    return lax.dot_general(left, right, (((0,), (0,)), ((), ())), preferred_element_type=f32)


def layer_norm(values, scaling, offset):
    center = values - jnp.mean(values, axis=-1, keepdims=True)
    spread = jnp.mean(center * center, axis=-1, keepdims=True)
    return center * lax.rsqrt(spread + norm_epsilon) * scaling + offset


def block_plan(length, randoms, flip, query_blocks):
    blocks = randoms.shape[0]
    last = (length + BLOCK - 1) // BLOCK - 1
    places = jnp.arange(query_blocks, dtype=jnp.int32) ^ flip
    own_randoms = jnp.take_along_axis(randoms, places[:, None], axis=0)
    zero = jnp.zeros((query_blocks,), jnp.int32)
    candidates = jnp.concatenate(
        [
            jnp.stack([places - 1, places, places + 1, zero, zero + last], axis=1),
            own_randoms,
        ],
        axis=1,
    )
    usable = (candidates >= 0) & (candidates < blocks)
    same = candidates[:, :, None] == candidates[:, None, :]
    before = jnp.arange(SLOTS)[:, None] > jnp.arange(SLOTS)[None, :]
    usable = usable & ~jnp.any(same & before[None], axis=2)
    is_global = (places == 0) | (places == last)
    usable = usable & ~is_global[:, None]
    names = jnp.clip(candidates, 0, blocks - 1) ^ flip
    global_name = jnp.where((flip ^ last) < query_blocks, flip ^ last, flip)
    every = jnp.arange(blocks, dtype=jnp.int32).reshape(blocks // SLOTS, SLOTS)
    query_names = jnp.concatenate(
        [
            jnp.arange(query_blocks, dtype=jnp.int32),
            jnp.zeros((blocks // SLOTS,), jnp.int32) + global_name,
        ]
    )
    key_names = jnp.concatenate([names, every])
    bias_names = jnp.concatenate([jnp.where(usable, names, blocks), every])
    return query_names, key_names, bias_names, global_name.reshape(1)


GROUPS = ((0, 256), (256, 128))


def spread_heads(rows):
    lane = lax.broadcasted_iota(jnp.int32, rows.shape, 1)
    zero = jnp.zeros_like(rows)
    heads = rows.shape[1] // HEAD_DIM
    return jnp.concatenate([jnp.where(lane // HEAD_DIM == head, rows, zero) for head in range(heads)], axis=0)


def join_heads(stacked):
    width = stacked.shape[1]
    lane = lax.broadcasted_iota(jnp.int32, (BLOCK, width), 1)
    joined = stacked[:BLOCK]
    for head in range(1, width // HEAD_DIM):
        joined = jnp.where(lane // HEAD_DIM == head, stacked[head * BLOCK : (head + 1) * BLOCK], joined)
    return joined


def wide(bias, width):
    return jnp.concatenate([bias] * (width // bias.shape[1]), axis=1)


def lanes_spec(rows, first, width):
    return pl.BlockSpec((rows, width), lambda step, *_: (0, first // width))


def block_rows(name):
    return pl.ds(pl.multiple_of(name * BLOCK, BLOCK), BLOCK)


def gather_blocks(ref, names):
    return jnp.concatenate([ref[block_rows(name), :] for name in names], axis=0)


def fill_length_bias(bias_scratch, length, flip):
    rows = bias_scratch.shape[0] - BLOCK
    place = lax.broadcasted_iota(jnp.int32, bias_scratch.shape, 0)
    token = (((place // BLOCK) ^ flip) * BLOCK) + place % BLOCK
    live = (token < length) & (place < rows)
    bias_scratch[...] = jnp.where(live, 0.0, masked_score)


def forward_kernel(
    key_names, bias_names, global_name, lengths, flips,
    q_ref, k_ref, v_ref, context_ref, logsum_ref, bias_scratch, score_scratch, *, unroll, query_blocks,
):
    width = q_ref.shape[1]

    @pl.when(pl.program_id(0) == 0)
    def _():
        fill_length_bias(bias_scratch, lengths[0], flips[0])

    def put(block, context, largest, total):
        context_ref[block_rows(block), :] = join_heads(context).astype(bf16)
        logsum_ref[pl.ds(block, 1), :] = largest + jnp.log(total)

    def one(block):
        queries = spread_heads(q_ref[block_rows(block), :])
        names = [key_names[block, slot] for slot in range(SLOTS)]
        biases = [bias_names[block, slot] for slot in range(SLOTS)]
        scores = dot_nt(gather_blocks(k_ref, names), queries) + wide(gather_blocks(bias_scratch, biases), width)
        largest = jnp.max(scores, axis=0, keepdims=True)
        weights = jnp.exp(scores - largest)
        total = jnp.sum(weights, axis=0, keepdims=True)
        shares = (weights * (1.0 / total)).astype(bf16)
        put(block, dot_tn(shares, gather_blocks(v_ref, names)), largest, total)

    def body(step, carry):
        for within in range(unroll):
            one(step * unroll + within)
        return carry

    lax.fori_loop(0, query_blocks // unroll, body, 0)
    block = global_name[0]
    queries = spread_heads(q_ref[block_rows(block), :])
    tokens = k_ref.shape[0]
    chunk = SLOTS * BLOCK
    together = 4

    def score_chunk(step, largest):
        for within in range(together):
            rows = pl.ds(pl.multiple_of((step * together + within) * chunk, chunk), chunk)
            scores = dot_nt(k_ref[rows, :], queries) + wide(bias_scratch[rows, :], width)
            score_scratch[rows, :] = scores
            largest = jnp.maximum(largest, jnp.max(scores, axis=0, keepdims=True))
        return largest

    steps = tokens // chunk // together
    lanes = width
    largest = lax.fori_loop(0, steps, score_chunk, jnp.full((1, lanes), masked_score, f32))

    def value_chunk(step, carry):
        total, context = carry
        for within in range(together):
            rows = pl.ds(pl.multiple_of((step * together + within) * chunk, chunk), chunk)
            weights = jnp.exp(score_scratch[rows, :] - largest)
            total = total + jnp.sum(weights, axis=0, keepdims=True)
            context = context + dot_tn(weights.astype(bf16), v_ref[rows, :])
        return total, context

    total, context = lax.fori_loop(
        0, steps, value_chunk, (jnp.zeros((1, lanes), f32), jnp.zeros((lanes, lanes), f32))
    )
    context = context * jnp.transpose(jnp.broadcast_to(1.0 / total, (lanes, lanes)))
    put(block, context, largest, total)


def attend(plan, length, flip, q, k, v):
    query_names, key_names, bias_names, global_name = plan
    query_rows, lanes = q.shape
    tokens = k.shape[0]
    query_blocks = query_rows // BLOCK
    width = 128

    def lanes_of(rows):
        return pl.BlockSpec((rows, width), lambda step, *_: (0, step))

    return pl.pallas_call(
        partial(forward_kernel, unroll=query_blocks, query_blocks=query_blocks),
        grid_spec=pltpu.PrefetchScalarGridSpec(
            num_scalar_prefetch=5,
            grid=(lanes // width,),
            in_specs=[lanes_of(query_rows), lanes_of(tokens), lanes_of(tokens)],
            out_specs=[lanes_of(query_rows), lanes_of(query_blocks)],
            scratch_shapes=[
                pltpu.VMEM((tokens + BLOCK, 128), f32),
                pltpu.VMEM((tokens, width), f32),
            ],
        ),
        out_shape=[
            jax.ShapeDtypeStruct((query_rows, lanes), bf16),
            jax.ShapeDtypeStruct((query_blocks, lanes), f32),
        ],
        compiler_params=pltpu.CompilerParams(vmem_limit_bytes=60 << 20),
        cost_estimate=pl.CostEstimate(flops=10**9, bytes_accessed=10**6, transcendentals=10**5),
        name="attend_forward",
    )(key_names, bias_names, global_name, length, flip, q, k, v)


def backward_kernel(
    query_names, key_names, bias_names, lengths, flips,
    q_ref, k_ref, v_ref, back_ref, context_ref, logsum_ref,
    back_q_ref, back_k_ref, back_v_ref, bias_scratch, q_scratch, k_scratch, v_scratch, *, unroll, items,
):
    width = q_ref.shape[1]
    fill_length_bias(bias_scratch, lengths[0], flips[0])
    q_scratch[...] = jnp.zeros_like(q_scratch)
    k_scratch[...] = jnp.zeros_like(k_scratch)
    v_scratch[...] = jnp.zeros_like(v_scratch)
    ones = jnp.ones((16, width), bf16)

    def one(item):
        block = query_names[item]
        rows = block_rows(block)
        queries = spread_heads(q_ref[rows, :])
        back = back_ref[rows, :]
        backs = spread_heads(back)
        product = (back.astype(f32) * context_ref[rows, :].astype(f32)).astype(bf16)
        inner = dot_nt(ones, spread_heads(product))[0:1]
        logsum = logsum_ref[pl.ds(block, 1), :]
        names = [key_names[item, slot] for slot in range(SLOTS)]
        biases = [bias_names[item, slot] for slot in range(SLOTS)]
        keys = gather_blocks(k_ref, names)
        scores = dot_nt(keys, queries) + wide(gather_blocks(bias_scratch, biases), width)
        shares = jnp.exp(scores - logsum)
        back_shares = dot_nt(gather_blocks(v_ref, names), backs)
        back_values = dot_nn(shares.astype(bf16), backs)
        back_scores = (shares * (back_shares - inner)).astype(bf16)
        back_keys = dot_nn(back_scores, queries)
        q_scratch[rows, :] += join_heads(dot_tn(back_scores, keys))
        for slot in range(SLOTS):
            part = slice(slot * BLOCK, (slot + 1) * BLOCK)
            v_scratch[block_rows(names[slot]), :] += back_values[part]
            k_scratch[block_rows(names[slot]), :] += back_keys[part]

    def body(step, carry):
        for within in range(unroll):
            one(step * unroll + within)
        return carry

    lax.fori_loop(0, items // unroll, body, 0)
    back_q_ref[...] = (q_scratch[...] * HEAD_DIM ** (-0.5)).astype(bf16)
    back_k_ref[...] = k_scratch[...].astype(bf16)
    back_v_ref[...] = v_scratch[...].astype(bf16)


def attend_back(plan, length, flip, group, q, k, v, back, context, logsum):
    first, width = group
    query_names, key_names, bias_names, _ = plan
    query_rows = q.shape[0]
    tokens = k.shape[0]
    query_blocks = query_rows // BLOCK
    q_in, k_in = lanes_spec(query_rows, first, width), lanes_spec(tokens, first, width)
    q_out, k_out = lanes_spec(query_rows, 0, width), lanes_spec(tokens, 0, width)
    return pl.pallas_call(
        partial(backward_kernel, unroll=8, items=query_names.shape[0]),
        grid_spec=pltpu.PrefetchScalarGridSpec(
            num_scalar_prefetch=5,
            grid=(1,),
            in_specs=[q_in, k_in, k_in, q_in, q_in, lanes_spec(query_blocks, first, width)],
            out_specs=[q_out, k_out, k_out],
            scratch_shapes=[
                pltpu.VMEM((tokens + BLOCK, 128), f32),
                pltpu.VMEM((query_rows, width), f32),
                pltpu.VMEM((tokens, width), f32),
                pltpu.VMEM((tokens, width), f32),
            ],
        ),
        out_shape=[
            jax.ShapeDtypeStruct((query_rows, width), bf16),
            jax.ShapeDtypeStruct((tokens, width), bf16),
            jax.ShapeDtypeStruct((tokens, width), bf16),
        ],
        compiler_params=pltpu.CompilerParams(vmem_limit_bytes=60 << 20),
        cost_estimate=pl.CostEstimate(flops=10**9, bytes_accessed=10**6, transcendentals=10**5),
        name="attend_backward",
    )(query_names, key_names, bias_names, length, flip, q, k, v, back, context, logsum)


def project_kernel(core, x_ref, x_near_ref, w_q, w_k, w_v, b_q, b_v, q_ref, k_ref, v_ref):
    step = pl.program_id(0)

    def project(tile):
        q = (dot_nn(tile, w_q[...]) + b_q[...]).astype(bf16)
        q_ref[...] = q * jnp.asarray(HEAD_DIM ** (-0.5), bf16)
        k_ref[...] = dot_nn(tile, w_k[...]).astype(bf16)
        v_ref[...] = (dot_nn(tile, w_v[...]) + b_v[...]).astype(bf16)

    @pl.when(step < pl.num_programs(0) // 2)
    def _():
        project(x_ref[...])

    @pl.when(step >= pl.num_programs(0) // 2)
    def _():
        project(x_near_ref[...])


def project_far_kernel(core, x_ref, x_near_ref, w_k, w_v, b_v, k_old, v_old, k_ref, v_ref):
    step = pl.program_id(0)

    def project(tile):
        k_ref[...] = dot_nn(tile, w_k[...]).astype(bf16)
        v_ref[...] = (dot_nn(tile, w_v[...]) + b_v[...]).astype(bf16)

    @pl.when(step < pl.num_programs(0) // 2)
    def _():
        project(x_ref[...])

    @pl.when(step >= pl.num_programs(0) // 2)
    def _():
        project(x_near_ref[...])


TILE = 512


def piece_spec(piece, per, width, tile=TILE):
    return pl.BlockSpec((tile, width), lambda step, *_: (jnp.clip(step - piece * per, 0, per - 1), 0))


def own_weight(which):
    return pl.BlockSpec((D, D // 2), lambda step, core, *_: (0, 2 * which + core[0]))


def own_bias():
    return pl.BlockSpec((1, D // 2), lambda step, core, *_: (0, core[0]))


def project_chip(core, x, x_near, qkv_weight, query_bias, value_bias):
    rows = x.shape[0]
    half = D // 2
    per = rows // TILE
    out = pl.BlockSpec((TILE, half), lambda step, *_: (step, 0))
    return pl.pallas_call(
        project_kernel,
        grid_spec=pltpu.PrefetchScalarGridSpec(
            num_scalar_prefetch=1,
            grid=(2 * per,),
            in_specs=[piece_spec(0, per, D), piece_spec(1, per, D)]
            + [own_weight(0), own_weight(1), own_weight(2), own_bias(), own_bias()],
            out_specs=[out, out, out],
        ),
        out_shape=[
            jax.ShapeDtypeStruct((2 * rows, half), bf16),
            jax.ShapeDtypeStruct((4 * rows, half), bf16),
            jax.ShapeDtypeStruct((4 * rows, half), bf16),
        ],
        compiler_params=pltpu.CompilerParams(vmem_limit_bytes=60 << 20),
        cost_estimate=pl.CostEstimate(flops=4 * 10**9, bytes_accessed=10**7, transcendentals=0),
        name="project_chip",
    )(core, x, x_near, qkv_weight, qkv_weight, qkv_weight, query_bias, value_bias)


def project_far(core, x_far, x_far_near, qkv_weight, value_bias, k, v):
    rows = x_far.shape[0]
    half = D // 2
    per = rows // TILE
    out = pl.BlockSpec((TILE, half), lambda step, *_: (2 * per + step, 0))
    kept = pl.BlockSpec(memory_space=pl.ANY)
    return pl.pallas_call(
        project_far_kernel,
        grid_spec=pltpu.PrefetchScalarGridSpec(
            num_scalar_prefetch=1,
            grid=(2 * per,),
            in_specs=[piece_spec(0, per, D), piece_spec(1, per, D)]
            + [own_weight(1), own_weight(2), own_bias(), kept, kept],
            out_specs=[out, out],
        ),
        out_shape=[jax.ShapeDtypeStruct(k.shape, bf16), jax.ShapeDtypeStruct(v.shape, bf16)],
        input_output_aliases={6: 0, 7: 1},
        compiler_params=pltpu.CompilerParams(vmem_limit_bytes=60 << 20),
        cost_estimate=pl.CostEstimate(flops=3 * 10**9, bytes_accessed=10**7, transcendentals=0),
        name="project_far",
    )(core, x_far, x_far_near, qkv_weight, qkv_weight, value_bias, k, v)


def gelu_pair(x):
    t = 1.0 / (1.0 + (0.3275911 * 0.5**0.5) * jnp.abs(x))
    bell = jnp.exp(-0.5 * x * x)
    poly = 0.7107068705 + t * (-0.7265760135 + t * 0.5307027145)
    tail = t * (0.127414796 + t * (-0.142248368 + t * poly)) * bell
    cdf = jnp.where(x < 0, tail, 1.0 - tail)
    return x * cdf, cdf + x * bell * 0.3989422804014327


def norm_parts(value):
    center = value - jnp.mean(value, axis=-1, keepdims=True)
    spread = jnp.mean(center * center, axis=-1, keepdims=True)
    scale = lax.rsqrt(spread + norm_epsilon)
    return center * scale, scale


def norm_back(slope, normed, scale):
    along = jnp.mean(slope * normed, axis=-1, keepdims=True)
    return scale * (slope - jnp.mean(slope, axis=-1, keepdims=True) - normed * along)


def column_sum(value):
    return jnp.sum(value, axis=0, keepdims=True)


PIECES = 16
VECTOR_ROWS = 128


def row_spec(tile, width):
    return pl.BlockSpec((tile, width), lambda step, *_: (step, 0))


def stack_spec(count, tile, width):
    return pl.BlockSpec((count, tile, width), lambda step, *_: (0, step, 0))


def whole_spec(shape):
    return pl.BlockSpec(shape, lambda step, *_: (0,) * len(shape))


def middle_kernel(
    core,
    own_ref, other_ref, x_ref, cot_ref, vector_ref, expand_bias_ref, proj_hbm, expand_hbm, shrink_hbm,
    output_ref, back_one_ref, back_own_ref, back_other_ref, wide_keep, wide_send, lows_ref, sums_ref,
    proj_w, expand_w, shrink_w, slope_s, wide_s, weight_sems, wide_sems, *, chunk,
):
    step = pl.program_id(0)
    half = D // 2
    ff = expand_w.shape[1]
    chunks = ff // chunk
    hc = core[0]
    loads = [
        pltpu.make_async_copy(proj_hbm.at[pl.ds(hc * half, half)], proj_w.at[pl.ds(0, half)], weight_sems.at[0]),
        pltpu.make_async_copy(
            proj_hbm.at[pl.ds((1 - hc) * half, half)], proj_w.at[pl.ds(half, half)], weight_sems.at[1]
        ),
        pltpu.make_async_copy(expand_hbm, expand_w, weight_sems.at[2]),
        pltpu.make_async_copy(shrink_hbm, shrink_w, weight_sems.at[3]),
    ]

    @pl.when(step == 0)
    def _():
        for load in loads:
            load.start()
        sums_ref[...] = jnp.zeros_like(sums_ref)
        for load in loads:
            load.wait()

    def vector(row):
        return vector_ref[pl.ds(row, 1), :]

    slot = lax.rem(step, 2)
    tile = x_ref.shape[0]

    def wide_copies(slot, first_row):
        copies = []
        for which in range(2):
            for side, out in enumerate((wide_keep, wide_send)):
                first = pl.multiple_of((hc if side == 0 else 1 - hc) * (ff // 2), ff // 2)
                copies.append(
                    pltpu.make_async_copy(
                        wide_s.at[slot, which, :, pl.ds(first, ff // 2)],
                        out.at[which, pl.ds(pl.multiple_of(first_row, tile), tile)],
                        wide_sems.at[slot, 2 * which + side],
                    )
                )
        return copies

    @pl.when(step >= 2)
    def _():
        for copy in wide_copies(slot, 0):
            copy.wait()

    context = jnp.concatenate([own_ref[...], other_ref[...]], axis=1)
    resid = x_ref[...].astype(f32) + dot_nn(context, proj_w[...]) + vector(0)
    normed_one, scale_one = norm_parts(resid)
    hidden = normed_one * vector(1) + vector(2)
    low = hidden.astype(bf16)
    lows_ref[0] = low
    resid_two = hidden + vector(3)

    for part in range(chunks):
        cols = slice(part * chunk, (part + 1) * chunk)
        inner = dot_nn(low, expand_w[:, cols]) + expand_bias_ref[:, cols]
        active, slope = gelu_pair(inner)
        active = active.astype(bf16)
        wide_s[slot, 0, :, cols] = active
        slope_s[:, cols] = slope.astype(bf16)
        resid_two = resid_two + dot_nn(active, shrink_w[cols, :])
    normed_two, scale_two = norm_parts(resid_two)
    output_ref[...] = (normed_two * vector(4) + vector(5)).astype(bf16)
    cot = cot_ref[...].astype(f32)
    back_two = norm_back(vector(4) * cot, normed_two, scale_two)
    low_two = back_two.astype(bf16)
    lows_ref[1] = low_two
    sums_ref[3:4, :] += column_sum(low_two.astype(f32))
    sums_ref[4:5, :] += column_sum(cot * normed_two)
    sums_ref[5:6, :] += column_sum(cot)
    back = back_two
    for part in range(chunks):
        cols = slice(part * chunk, (part + 1) * chunk)
        back_inner = (dot_nt(low_two, shrink_w[cols, :]) * slope_s[:, cols].astype(f32)).astype(bf16)
        wide_s[slot, 1, :, cols] = back_inner
        sums_ref[8 + part : 9 + part, :] += column_sum(back_inner.astype(f32))
        back = back + dot_nt(back_inner, expand_w[:, cols])
    sums_ref[1:2, :] += column_sum(back * normed_one)
    sums_ref[2:3, :] += column_sum(back)
    back_one = norm_back(vector(1) * back, normed_one, scale_one)
    back_one_ref[...] = back_one
    low_one = back_one.astype(bf16)
    lows_ref[2] = low_one
    sums_ref[0:1, :] += column_sum(low_one.astype(f32))
    back_context = dot_nt(low_one, proj_w[...]).astype(bf16)
    back_own_ref[...] = back_context[:, :half]
    back_other_ref[...] = back_context[:, half:]
    for copy in wide_copies(slot, step * tile):
        copy.start()

    @pl.when(step == pl.num_programs(0) - 1)
    def _():
        for other in range(2):
            for copy in wide_copies(other, 0):
                copy.wait()


def middle(core, own, other, x, cot, vectors, expand_bias, proj_weight, expand_weight, shrink_weight):
    rows = x.shape[0]
    ff = expand_weight.shape[1]
    half = D // 2
    tile = 256
    kept = pl.BlockSpec(memory_space=pl.ANY)
    assert ff // D == 4
    return pl.pallas_call(
        partial(middle_kernel, chunk=D),
        grid_spec=pltpu.PrefetchScalarGridSpec(
            num_scalar_prefetch=1,
            grid=(rows // tile,),
            in_specs=[row_spec(tile, half)] * 2
            + [row_spec(tile, D)] * 2
            + [whole_spec(vectors.shape), whole_spec(expand_bias.shape), kept, kept, kept],
            out_specs=[row_spec(tile, D)] * 2
            + [row_spec(tile, half)] * 2
            + [kept] * 2
            + [stack_spec(3, tile, D), whole_spec((16, D))],
            scratch_shapes=[
                pltpu.VMEM((D, D), bf16),
                pltpu.VMEM((D, ff), bf16),
                pltpu.VMEM((ff, D), bf16),
                pltpu.VMEM((tile, ff), bf16),
                pltpu.VMEM((2, 2, tile, ff), bf16),
                pltpu.SemaphoreType.DMA((4,)),
                pltpu.SemaphoreType.DMA((2, 4)),
            ],
        ),
        out_shape=[
            jax.ShapeDtypeStruct((rows, D), bf16),
            jax.ShapeDtypeStruct((rows, D), f32),
            jax.ShapeDtypeStruct((rows, half), bf16),
            jax.ShapeDtypeStruct((rows, half), bf16),
            jax.ShapeDtypeStruct((2, rows, ff // 2), bf16),
            jax.ShapeDtypeStruct((2, rows, ff // 2), bf16),
            jax.ShapeDtypeStruct((3, rows, D), bf16),
            jax.ShapeDtypeStruct((16, D), f32),
        ],
        compiler_params=pltpu.CompilerParams(vmem_limit_bytes=60 << 20),
        cost_estimate=pl.CostEstimate(flops=10**9, bytes_accessed=10**7, transcendentals=10**6),
        name="middle",
    )(core, own, other, x, cot, vectors, expand_bias, proj_weight, expand_weight, shrink_weight)


def weights_kernel(
    places, wide_own, wide_other, lows_own, lows_other, context_ref, sums_own, sums_other, *refs
):
    packed = refs[:4]
    shrink_g, expand_g, proj_g = refs[4:]
    step = pl.program_id(0)
    half = D // 2

    @pl.when(step == 0)
    def _():
        shrink_g[...] = jnp.zeros_like(shrink_g)
        expand_g[...] = jnp.zeros_like(expand_g)
        proj_g[...] = jnp.zeros_like(proj_g)
        proj_g[half : half + 16, :] = sums_own[...] + sums_other[...]

    def add(wide, lows):
        shrink_g[...] += dot_tn(wide[0], lows[1])
        expand_g[...] += dot_tn(lows[0], wide[1])
        proj_g[:half, :] += dot_tn(context_ref[...], lows[2])

    @pl.when(step < pl.num_programs(0) // 2)
    def _():
        add(wide_own, lows_own)

    @pl.when(step >= pl.num_programs(0) // 2)
    def _():
        add(wide_other, lows_other)

    @pl.when(step == pl.num_programs(0) - 1)
    def _():
        rows = shrink_g.shape[0] // PIECES
        extra = proj_g.shape[0] // (2 * PIECES)
        wide = expand_g.shape[1] // D
        for piece in range(PIECES):
            place = piece % (PIECES // 2)
            first = piece ^ places[0]
            second = piece ^ places[1]
            out = packed[piece // (PIECES // 2)]
            out[place, :rows, :] = shrink_g[pl.ds(pl.multiple_of(first * rows, rows), rows), :].astype(bf16)
            out[place, rows:, :] = proj_g[pl.ds(pl.multiple_of(first * extra, extra), extra), :].astype(bf16)
            out = packed[2 + piece // (PIECES // 2)]
            down = pl.ds(pl.multiple_of((second // wide) * rows, rows), rows)
            across = pl.ds(pl.multiple_of(lax.rem(second, wide) * D, D), D)
            out[place, :rows, :] = expand_g[down, across].astype(bf16)
            part = pl.ds(pl.multiple_of((PIECES + second) * extra, extra), extra)
            out[place, rows:, :] = proj_g[part, :].astype(bf16)


def weight_grads(places, wide_own, wide_other, lows_own, lows_other, context, sums_own, sums_other):
    _, rows, wide = wide_own.shape
    half = D // 2
    per = rows // TILE
    piece_rows = wide // PIECES + (half + VECTOR_ROWS) // (2 * PIECES)

    def own(count, width):
        return pl.BlockSpec((count, TILE, width), lambda step, *_: (0, jnp.minimum(step, per - 1), 0))

    def other(count, width):
        return pl.BlockSpec((count, TILE, width), lambda step, *_: (0, jnp.maximum(step - per, 0), 0))

    packed_shape = (PIECES // 2, piece_rows, D)
    return pl.pallas_call(
        weights_kernel,
        grid_spec=pltpu.PrefetchScalarGridSpec(
            num_scalar_prefetch=1,
            grid=(2 * per,),
            in_specs=[own(2, wide), other(2, wide), own(3, D), other(3, D), row_spec(TILE, half)]
            + [whole_spec((16, D))] * 2,
            out_specs=[whole_spec(packed_shape)] * 4,
            scratch_shapes=[
                pltpu.VMEM((wide, D), f32),
                pltpu.VMEM((D, wide), f32),
                pltpu.VMEM((half + VECTOR_ROWS, D), f32),
            ],
        ),
        out_shape=[jax.ShapeDtypeStruct(packed_shape, bf16)] * 4,
        compiler_params=pltpu.CompilerParams(vmem_limit_bytes=60 << 20),
        cost_estimate=pl.CostEstimate(flops=10**9, bytes_accessed=10**7, transcendentals=0),
        name="weight_grads",
    )(places, wide_own, wide_other, lows_own, lows_other, context, sums_own, sums_other)


def quarters_spec(place, per):
    return pl.BlockSpec((TILE, D), lambda step, *_: (jnp.clip(step - place * per, 0, per - 1), 0))


def input_kernel(core, *refs, per):
    weights, arrays, outs = refs[:3], refs[3:-4], refs[-4:]
    pairs = len(arrays) // 3
    step = pl.program_id(0)

    def through(which):
        back = jnp.concatenate([ref[...] for ref in arrays[which * pairs : (which + 1) * pairs]], axis=1)
        return dot_nt(back, weights[which][...])

    for place in range(4):

        @pl.when((step >= place * per) & (step < (place + 1) * per))
        def _():
            total = through(1) + through(2)
            if place >= 2:
                total = total + through(0)
            outs[place][...] = total.astype(bf16)


def input_parts(core, qkv_weight, back_qs, back_ks, back_vs, rows):
    per = rows // TILE
    tokens = [
        pl.BlockSpec((TILE, array.shape[1]), lambda step, *_: (lax.rem(step + 2 * per, 4 * per), 0)) for array in back_ks
    ]
    queries = [
        pl.BlockSpec((TILE, array.shape[1]), lambda step, *_: (jnp.maximum(step - 2 * per, 0), 0)) for array in back_qs
    ]
    return pl.pallas_call(
        partial(input_kernel, per=per),
        grid_spec=pltpu.PrefetchScalarGridSpec(
            num_scalar_prefetch=1,
            grid=(4 * per,),
            in_specs=[own_weight(which) for which in range(3)] + queries + 2 * tokens,
            out_specs=[quarters_spec(place, per) for place in range(4)],
        ),
        out_shape=[jax.ShapeDtypeStruct((rows, D), bf16)] * 4,
        compiler_params=pltpu.CompilerParams(vmem_limit_bytes=60 << 20),
        cost_estimate=pl.CostEstimate(flops=10**9, bytes_accessed=10**7, transcendentals=0),
        name="input_parts",
    )(core, *[qkv_weight] * 3, *back_qs, *back_ks, *back_vs)


QKV_PIECES = 16
JOINED_TILE = 1024


def joined_kernel(places, core, *refs, tiles, pairs):
    x_refs = refs[:4]
    arrays = refs[4 : 4 + 3 * pairs]
    packed = refs[4 + 3 * pairs : 8 + 3 * pairs]
    total, sums = refs[8 + 3 * pairs :]
    step = pl.program_id(0)
    half = D // 2
    per = tiles // 4

    @pl.when(step == 0)
    def _():
        total[...] = jnp.zeros_like(total)
        sums[...] = jnp.zeros_like(sums)

    def joined(first, last):
        return jnp.concatenate([ref[...] for ref in arrays[first * pairs : last * pairs]], axis=1)

    for piece in range(4):

        @pl.when((step >= piece * per) & (step < (piece + 1) * per))
        def _():
            first = 0 if piece < 2 else 1
            back = joined(first, 3)
            total[:, first * half : 3 * half] += dot_tn(x_refs[piece][...], back)
            sums[0:1, first * half :] += column_sum(back.astype(f32))

    @pl.when(step == tiles - 1)
    def _():
        rows = D // QKV_PIECES
        q_sums = jnp.transpose(jnp.broadcast_to(sums[0:1, :half], (128, half)))
        v_sums = jnp.transpose(jnp.broadcast_to(sums[0:1, 2 * half :], (128, half)))
        total[:half, 3 * half :] = q_sums
        total[half:, 3 * half :] = v_sums
        width = packed[0].shape[2]
        for color in range(2):
            cols = slice(color * width, (color + 1) * width)
            for piece in range(QKV_PIECES):
                part = pl.ds(pl.multiple_of((piece ^ places[color]) * rows, rows), rows)
                out = packed[2 * color + piece // (QKV_PIECES // 2)]
                out[piece % (QKV_PIECES // 2)] = total[part, cols].astype(bf16)


def joined_grads(places, core, xs, back_qs, back_ks, back_vs):
    rows = xs[0].shape[0]
    pairs = len(back_qs)
    per = rows // JOINED_TILE
    tiles = 4 * per
    width = D // 2 + 256
    tokens = [row_spec(JOINED_TILE, array.shape[1]) for array in back_ks]
    queries = [
        pl.BlockSpec((JOINED_TILE, array.shape[1]), lambda step, *_: (jnp.minimum(step, 2 * per - 1), 0)) for array in back_qs
    ]
    packed = pl.BlockSpec((QKV_PIECES // 2, D // QKV_PIECES, width), lambda step, *_: (0, 0, 0))
    packed_shape = jax.ShapeDtypeStruct((QKV_PIECES // 2, D // QKV_PIECES, width), bf16)
    return pl.pallas_call(
        partial(joined_kernel, tiles=tiles, pairs=pairs),
        grid_spec=pltpu.PrefetchScalarGridSpec(
            num_scalar_prefetch=2,
            grid=(tiles,),
            in_specs=[piece_spec(piece, per, D, JOINED_TILE) for piece in range(4)] + queries + 2 * tokens,
            out_specs=[packed] * 4,
            scratch_shapes=[pltpu.VMEM((D, 2 * width), f32), pltpu.VMEM((8, 3 * D // 2), f32)],
        ),
        out_shape=[packed_shape] * 4,
        compiler_params=pltpu.CompilerParams(vmem_limit_bytes=60 << 20),
        cost_estimate=pl.CostEstimate(flops=10**9, bytes_accessed=10**7, transcendentals=0),
        name="joined_grads",
    )(places, core, *xs, *back_qs, *back_ks, *back_vs)


def input_near_kernel(core, *refs):
    w_q, w_k, w_v, out = refs[0], refs[1], refs[2], refs[-1]
    arrays = refs[3:-1]
    pairs = len(arrays) // 3

    def joined(which):
        return jnp.concatenate([ref[...] for ref in arrays[which * pairs : (which + 1) * pairs]], axis=1)

    out[...] = (dot_nt(joined(0), w_q[...]) + dot_nt(joined(1), w_k[...]) + dot_nt(joined(2), w_v[...])).astype(bf16)


def input_near(core, qkv_weight, back_qs, back_ks, back_vs):
    rows = back_qs[0].shape[0]
    token = pl.BlockSpec((JOINED_TILE, 128), lambda step, *_: (step, 0))
    arrays = list(back_qs) + list(back_ks) + list(back_vs)
    return pl.pallas_call(
        input_near_kernel,
        grid_spec=pltpu.PrefetchScalarGridSpec(
            num_scalar_prefetch=1,
            grid=(rows // JOINED_TILE,),
            in_specs=[own_weight(0), own_weight(1), own_weight(2)] + [token] * len(arrays),
            out_specs=pl.BlockSpec((JOINED_TILE, D), lambda step, *_: (step, 0)),
        ),
        out_shape=jax.ShapeDtypeStruct((rows, D), bf16),
        compiler_params=pltpu.CompilerParams(vmem_limit_bytes=60 << 20),
        cost_estimate=pl.CostEstimate(flops=10**9, bytes_accessed=10**7, transcendentals=0),
        name="input_near",
    )(core, qkv_weight, qkv_weight, qkv_weight, *arrays)


GROUP = 8


def unpack_kernel(numbers, *refs, parts, outs, held):
    sources = refs[:4]
    targets = refs[4 + held : 4 + held + outs]
    stages = refs[4 + held + outs : -1]
    sems = refs[-1]
    step = pl.program_id(0)

    def copy(color, which, slot, number, elsewhere=False):
        part = parts[color][which]
        out, place = part["instead"][1:] if elsewhere else (part["out"], part["place"])
        row, col = place(number)
        rows, cols = part["rows"][1] - part["rows"][0], part["cols"][1] - part["cols"][0]
        target = targets[out].at[pl.ds(pl.multiple_of(row, rows), rows), pl.ds(pl.multiple_of(col, 128), cols)]
        at = part["at"]
        source = stages[color].at[slot, pl.ds(at[0], rows), pl.ds(at[1], cols)]
        return pltpu.make_async_copy(source, target, sems.at[color, which, slot])

    for place, source in enumerate(sources):
        color, side = place // 2, place % 2

        @pl.when(step == place)
        def _():
            for within in range(GROUP):
                slot = side * GROUP + within
                number = numbers[place * GROUP + within]
                stages[color][slot] = source[within].astype(f32)
                for which, part in enumerate(parts[color]):
                    if part["instead"] is None:
                        copy(color, which, slot, number).start()
                        continue
                    elsewhere = part["instead"][0](number)

                    @pl.when(elsewhere)
                    def _():
                        copy(color, which, slot, number, True).start()

                    @pl.when(jnp.logical_not(elsewhere))
                    def _():
                        copy(color, which, slot, number).start()

    @pl.when(step == pl.num_programs(0) - 1)
    def _():
        for color in range(2):
            for slot in range(2 * GROUP):
                for which in range(len(parts[color])):
                    copy(color, which, slot, 0).wait()


def unpack(numbers, sources, parts, out_shapes, held, name):
    count, rows, width = sources[0].shape
    assert count == GROUP and len(sources) == 4
    most = max(len(part) for part in parts)
    kept = pl.BlockSpec(memory_space=pl.ANY)
    return pl.pallas_call(
        partial(unpack_kernel, parts=parts, outs=len(out_shapes), held=len(held)),
        grid_spec=pltpu.PrefetchScalarGridSpec(
            num_scalar_prefetch=1,
            grid=(len(sources),),
            in_specs=[pl.BlockSpec((GROUP, rows, width), lambda step, *_: (0, 0, 0))] * len(sources) + [kept] * len(held),
            out_specs=[kept] * len(out_shapes),
            scratch_shapes=[pltpu.VMEM((2 * GROUP, rows, width), f32)] * 2
            + [pltpu.SemaphoreType.DMA((2, most, 2 * GROUP))],
        ),
        out_shape=[jax.ShapeDtypeStruct(shape, f32) for shape in out_shapes],
        input_output_aliases={1 + len(sources) + place: place for place in range(len(held))},
        compiler_params=pltpu.CompilerParams(vmem_limit_bytes=60 << 20),
        cost_estimate=pl.CostEstimate(flops=10**6, bytes_accessed=10**6, transcendentals=0),
        name=name,
    )(numbers, *sources, *held)


def part_of(rows, cols, out, place, instead=None):
    return {"rows": rows, "cols": cols, "at": (rows[0], cols[0]), "out": out, "place": place, "instead": instead}


def swap(value, axis, bit=1):
    size = lax.axis_size(axis)
    return lax.ppermute(value, axis, [(place, place ^ bit) for place in range(size)])


def place_of(order):
    number = jnp.zeros((), jnp.int32)
    for axis, bit in order:
        number = 2 * number + ((lax.axis_index(axis) & bit) // bit).astype(jnp.int32)
    return number


def add_low(left, right):
    return (left.astype(f32) + right.astype(f32)).astype(bf16)


class Chain:
    def __init__(self, scatter_order, gather_order, keep, first):
        self.orders = list(scatter_order) + list(gather_order)
        self.steps = len(scatter_order)
        self.keep, self.first, self.arrived = keep, first, None
        self.at = 0
        self.gathered = None
        self.other_gathered = None
        self.other_arrived = None

    def left(self):
        return len(self.orders) + 1 - self.at

    def send(self):
        if self.at < self.steps:
            if self.at == 0:
                return self.first
            half = self.keep.shape[0] // 2
            high = add_low(self.keep[half:], self.arrived[half:])
            self.keep = add_low(self.keep[:half], self.arrived[:half])
            return high
        if self.at == self.steps:
            total = add_low(self.keep, self.arrived)
            bit = 8
            while bit < lax.axis_size("dp"):
                total = add_low(total, swap(total, "dp", bit))
                bit *= 2
            self.gathered = total
        elif self.at < len(self.orders):
            self.gathered = jnp.concatenate([self.gathered, self.arrived], axis=0)
        else:
            return self.arrived
        return self.gathered

    def move(self, value):
        if self.at == len(self.orders):
            self.arrived, self.other_arrived = value, swap(value, "hc")
            self.at += 1
            return
        if self.at >= self.steps:
            self.gathered = value
        axis, bit = self.orders[self.at]
        self.arrived = swap(value, axis, bit)
        self.at += 1
        if self.at == len(self.orders):
            self.other_gathered = swap(value, "hc")


def gathered_numbers(number, scatter_order, gather_order):
    count = 1 << len(scatter_order)
    places = jnp.arange(count, dtype=jnp.int32)
    turned = jnp.zeros((count,), jnp.int32)
    for at, name in enumerate(gather_order):
        turned = turned + (((places >> at) & 1) << (len(scatter_order) - 1 - scatter_order.index(name)))
    return turned ^ number


def ready(*values):
    return lax.optimization_barrier(values)


def per_device(
    inputs, doc_lengths, random_blocks, qkv_weight, query_bias, value_bias, proj_weight, proj_bias,
    first_gain, first_shift, expand_weight, expand_bias, shrink_weight, shrink_bias,
    second_gain, second_shift, cotangent,
):
    hx = lax.axis_index("hx")
    hc = lax.axis_index("hc")
    docs, rows, _ = inputs.shape
    assert docs == 1 and lax.axis_size("hx") == 2 and lax.axis_size("hc") == 2
    half = D // 2
    ff = expand_weight.shape[1]
    x = inputs.reshape(rows, D)
    x_far = swap(x, "hx")
    x_near = swap(x, "hc")
    row_blocks = rows // BLOCK
    flip = (hx * 2 + hc).astype(jnp.int32) * row_blocks
    plan = block_plan(doc_lengths[0], random_blocks[0], flip, 2 * row_blocks)
    flip = flip.reshape(1)
    core = hc.astype(jnp.int32).reshape(1)
    chip_steps = {"x": ("hx", 1), "y": ("dp", 1), "n": ("dp", 2), "f": ("dp", 4)}
    orders = {
        name: tuple([chip_steps[step] for step in part] for part in text.split())
        for name, text in ORDERS.items()
    }

    def places_of(letter):
        return jnp.stack([place_of(orders[f"{letter}{color}"][0]) for color in range(2)])

    def numbers_of(letter, places):
        own = [gathered_numbers(places[color], *orders[f"{letter}{color}"]) for color in range(2)]
        parts = [slice(0, GROUP), slice(GROUP, 2 * GROUP)]
        return tuple(
            jnp.concatenate([own[color][part] + PIECES * side for color in range(2) for side in (core, 1 - core)])
            for part in parts
        )

    middle_places, joined_places = places_of("M"), places_of("Q")
    numbers = numbers_of("M", middle_places) + numbers_of("Q", joined_places)
    vectors = jnp.concatenate(
        [proj_bias, first_gain, first_shift, shrink_bias, second_gain, second_shift, query_bias, value_bias]
    ).reshape(8, D)
    vectors = vectors.astype(f32)
    bias_q, bias_v = vectors[6:7], vectors[7:8]
    expand_row = expand_bias.astype(f32).reshape(1, ff)

    q, k, v = project_chip(core, x, x_near, qkv_weight, bias_q, bias_v)
    x_far, q, expand_row, vectors, middle_places, joined_places, *rest = ready(
        x_far, q, expand_row, vectors, middle_places, joined_places, *numbers, *plan
    )
    numbers, plan = rest[:4], rest[4:]
    x_far_near = swap(x_far, "hc")
    k, v = project_far(core, x_far, x_far_near, qkv_weight, bias_v, k, v)
    context, logsum = attend(plan, doc_lengths, flip, q, k, v)
    other_context = swap(context[rows:], "hc")
    output, back_one, back_own, back_other, wide_keep, wide_send, lows, sums = middle(
        core, context, other_context, x, cotangent.reshape(rows, D), vectors,
        expand_row, proj_weight, expand_weight, shrink_weight,
    )
    from_other = swap(back_other, "hc")
    wide_send, lows_send, sums_send, from_other = ready(wide_send, lows, sums, from_other)
    back = jnp.concatenate([back_own, from_other], axis=0)
    wide_other, lows_other, sums_other = swap(wide_send, "hc"), swap(lows_send, "hc"), swap(sums_send, "hc")

    held = {"last": back}
    chains = {}

    def tie(value):
        value, held["last"] = ready(value, held["last"])
        return value

    def pairs_of(which):
        return [held["grads", pair][which] for pair in range(len(GROUPS))]

    rows_each, extra, wide_blocks = ff // 2 // PIECES, (D // 2 + VECTOR_ROWS) // (2 * PIECES), ff // 2 // D
    proj_pieces = half // extra

    def split(number):
        return number // PIECES, lax.rem(number, PIECES)

    def expand_place(number):
        side, piece = split(number)
        return piece // wide_blocks * rows_each, (side * wide_blocks + lax.rem(piece, wide_blocks)) * D

    def proj_place(color):
        def place(number):
            side, piece = split(number)
            return side * half + (color * PIECES + piece) * extra, number * 0

        return place

    def vector_place(number):
        side, piece = split(number)
        return (side * (2 * PIECES - proj_pieces) + PIECES + piece - proj_pieces) * extra, number * 0

    def joined_place(which, offset):
        def place(number):
            side, piece = split(number)
            return piece * (D // QKV_PIECES), which * D + side * half + offset

        return place

    def bias_place(number):
        side, piece = split(number)
        return (side * QKV_PIECES + piece) * (D // QKV_PIECES), number * 0

    each = D // QKV_PIECES
    middle_parts = [
        [
            part_of((0, rows_each), (0, D), 0, lambda n: (n * rows_each, n * 0)),
            part_of((rows_each, rows_each + extra), (0, D), 2, proj_place(0)),
        ],
        [
            part_of((0, rows_each), (0, D), 1, expand_place),
            part_of(
                (rows_each, rows_each + extra), (0, D), 2, proj_place(1),
                (lambda n: lax.rem(n, PIECES) >= proj_pieces - PIECES, 3, vector_place),
            ),
        ],
    ]
    joined_parts = [
        [
            part_of((0, each), (0, half), 0, joined_place(0, 0)),
            part_of((0, each), (half, half + 256), 0, joined_place(1, 0)),
        ],
        [
            part_of((0, each), (0, 128), 0, joined_place(1, 256)),
            part_of((0, each), (128, 128 + half), 0, joined_place(2, 0)),
            part_of((0, each), (128 + half, 256 + half), 1, bias_place),
        ],
    ]
    layouts = {
        "M": (middle_parts, [(ff, D), (D, ff), (D, D), (2 * VECTOR_ROWS, D)], numbers[:2]),
        "Q": (joined_parts, [(D, 3 * D), (2 * D, 128)], numbers[2:]),
    }

    def run(name):
        if name.startswith("attend"):
            pair = int(name[-1])
            held["grads", pair] = attend_back(
                plan, doc_lengths, flip, GROUPS[pair], q, k, v, tie(back), context, logsum
            )
            held["last"] = held["grads", pair][0]
        elif name == "weights":
            packed = weight_grads(
                middle_places, tie(wide_keep), wide_other, lows, lows_other, context, sums, sums_other
            )
            held["last"] = packed[0]
            for color in range(2):
                chains[f"M{color}"] = Chain(*orders[f"M{color}"], packed[2 * color], packed[2 * color + 1])
        elif name == "joined":
            back_qs = pairs_of(0)
            back_qs[0] = tie(back_qs[0])
            packed = joined_grads(
                joined_places, core, (x, x_near, x_far, x_far_near), back_qs, pairs_of(1), pairs_of(2)
            )
            held["last"] = packed[0]
            for color in range(2):
                chains[f"Q{color}"] = Chain(*orders[f"Q{color}"], packed[2 * color], packed[2 * color + 1])
        elif name == "inputs":
            back_ks = pairs_of(1)
            back_ks[0] = tie(back_ks[0])
            far, far_others, near, near_others = input_parts(core, qkv_weight, pairs_of(0), back_ks, pairs_of(2), rows)
            held["last"] = far
            held["far"] = far, swap(far_others, "hc")
            held["near"] = near, swap(near_others, "hc")
        elif name == "dx":
            value = tie(add_low(*held["far"]))
            held["last"] = value
            held["from_far"] = swap(value, "hx")
        elif name == "input":
            near, from_near = held["near"]
            near = tie(near)
            value = back_one + near.astype(f32) + from_near.astype(f32) + held["from_far"].astype(f32)
            held["last"] = held["input"] = value
        elif name.startswith("early") or name.startswith("late"):
            letter = name[-1]
            parts, shapes, places = layouts[letter]
            early = name.startswith("early")
            sides = ("gathered", "other_gathered") if early else ("arrived", "other_arrived")
            sources = [getattr(chains[f"{letter}{color}"], side) for color in range(2) for side in sides]
            sources[0] = tie(sources[0])
            held["out", letter] = unpack(
                places[0 if early else 1], sources, parts, shapes, () if early else held["out", letter],
                f"unpack_{letter}",
            )
            held["last"] = held["out", letter][0]
        else:
            chain = chains[name]
            value = tie(chain.send())
            chain.move(value)
            held["last"] = value

    for names in SEQUENCE:
        for name in names.split():
            run(name)
    assert all(chain.left() == 0 for chain in chains.values())
    grad_shrink, grad_expand, grad_proj, vector = held["out", "M"]
    grad_qkv, bias = held["out", "Q"]
    grad_query_bias = jnp.concatenate([bias[:half, 0], bias[D : D + half, 0]])
    grad_value_bias = jnp.concatenate([bias[half:D, 0], bias[D + half :, 0]])
    grad_expand_bias = vector[8 : 8 + ff // D].reshape(ff)
    return (
        output.reshape(docs, rows, D),
        held["input"].reshape(docs, rows, D),
        grad_qkv, grad_query_bias, grad_value_bias, grad_proj, vector[0], vector[1], vector[2],
        grad_expand, grad_expand_bias, grad_shrink, vector[3], vector[4], vector[5],
    )


ORDERS = {"M0": "xnyf fynx", "M1": "nxyf fnxy", "Q0": "xynf xyfn", "Q1": "xynf xyfn"}
SEQUENCE = (
    "attend0 weights M0 M1",
    "attend1 inputs M0 M1",
    "joined Q0 M0 Q1",
    "M1 dx M0 Q0",
    "M1 M0 Q0 Q1",
    "M1 Q1 Q0 M0",
    "Q1 M1 Q0 Q1",
    "M0 M1 Q0 Q1",
    "input Q0 Q1 M0",
    "M1 Q0 earlyM Q1",
    "Q0 earlyQ M0 Q1",
    "M1 lateQ lateM",
)


def solution(mesh):
    dp = mesh.shape["dp"]
    heads = mesh.shape["heads"]
    split = Mesh(mesh.devices.reshape(dp, heads // 2, 2), ("dp", "hx", "hc"))
    rows = P("dp", ("hx", "hc"), None)
    in_specs = (rows, P("dp"), P("dp", None, None)) + (P(),) * 13 + (rows,)
    out_specs = (rows, rows) + (P(),) * 13
    return jax.shard_map(
        per_device, mesh=split, in_specs=in_specs, out_specs=out_specs, check_vma=False
    )
```

```python
from functools import partial

import jax
import jax.numpy as jnp
from jax import lax
from jax.experimental import pallas as pl
from jax.experimental.pallas import tpu as pltpu
from jax.sharding import Mesh
from jax.sharding import PartitionSpec as P

D = 768
HEADS = 12
HEAD_DIM = 64
BLOCK = 64
SLOTS = 8
norm_epsilon = 1e-12
masked_score = -1e30
f32 = jnp.float32
bf16 = jnp.bfloat16


def dot_nn(left, right):
    return lax.dot_general(left, right, (((1,), (0,)), ((), ())), preferred_element_type=f32)


def dot_nt(left, right):
    return lax.dot_general(left, right, (((1,), (1,)), ((), ())), preferred_element_type=f32)


def dot_tn(left, right):
    return lax.dot_general(left, right, (((0,), (0,)), ((), ())), preferred_element_type=f32)


def layer_norm(values, scaling, offset):
    center = values - jnp.mean(values, axis=-1, keepdims=True)
    spread = jnp.mean(center * center, axis=-1, keepdims=True)
    return center * lax.rsqrt(spread + norm_epsilon) * scaling + offset


def block_plan(length, randoms, flip, query_blocks):
    blocks = randoms.shape[0]
    last = (length + BLOCK - 1) // BLOCK - 1
    places = jnp.arange(query_blocks, dtype=jnp.int32) ^ flip
    own_randoms = jnp.take_along_axis(randoms, places[:, None], axis=0)
    zero = jnp.zeros((query_blocks,), jnp.int32)
    candidates = jnp.concatenate(
        [
            jnp.stack([places - 1, places, places + 1, zero, zero + last], axis=1),
            own_randoms,
        ],
        axis=1,
    )
    usable = (candidates >= 0) & (candidates < blocks)
    same = candidates[:, :, None] == candidates[:, None, :]
    before = jnp.arange(SLOTS)[:, None] > jnp.arange(SLOTS)[None, :]
    usable = usable & ~jnp.any(same & before[None], axis=2)
    is_global = (places == 0) | (places == last)
    usable = usable & ~is_global[:, None]
    names = jnp.clip(candidates, 0, blocks - 1) ^ flip
    global_name = jnp.where((flip ^ last) < query_blocks, flip ^ last, flip)
    every = jnp.arange(blocks, dtype=jnp.int32).reshape(blocks // SLOTS, SLOTS)
    query_names = jnp.concatenate(
        [
            jnp.arange(query_blocks, dtype=jnp.int32),
            jnp.zeros((blocks // SLOTS,), jnp.int32) + global_name,
        ]
    )
    key_names = jnp.concatenate([names, every])
    bias_names = jnp.concatenate([jnp.where(usable, names, blocks), every])
    return query_names, key_names, bias_names, global_name.reshape(1)


GROUPS = ((0, 256), (256, 128))


def spread_heads(rows):
    lane = lax.broadcasted_iota(jnp.int32, rows.shape, 1)
    zero = jnp.zeros_like(rows)
    heads = rows.shape[1] // HEAD_DIM
    return jnp.concatenate([jnp.where(lane // HEAD_DIM == head, rows, zero) for head in range(heads)], axis=0)


def join_heads(stacked):
    width = stacked.shape[1]
    lane = lax.broadcasted_iota(jnp.int32, (BLOCK, width), 1)
    joined = stacked[:BLOCK]
    for head in range(1, width // HEAD_DIM):
        joined = jnp.where(lane // HEAD_DIM == head, stacked[head * BLOCK : (head + 1) * BLOCK], joined)
    return joined


def wide(bias, width):
    return jnp.concatenate([bias] * (width // bias.shape[1]), axis=1)


def lanes_spec(rows, first, width):
    return pl.BlockSpec((rows, width), lambda step, *_: (0, first // width))


def block_rows(name):
    return pl.ds(pl.multiple_of(name * BLOCK, BLOCK), BLOCK)


def gather_blocks(ref, names):
    return jnp.concatenate([ref[block_rows(name), :] for name in names], axis=0)


def fill_length_bias(bias_scratch, length, flip):
    rows = bias_scratch.shape[0] - BLOCK
    place = lax.broadcasted_iota(jnp.int32, bias_scratch.shape, 0)
    token = (((place // BLOCK) ^ flip) * BLOCK) + place % BLOCK
    live = (token < length) & (place < rows)
    bias_scratch[...] = jnp.where(live, 0.0, masked_score)


def forward_kernel(
    key_names, bias_names, global_name, lengths, flips,
    q_ref, k_ref, v_ref, context_ref, logsum_ref, bias_scratch, score_scratch, *, unroll, query_blocks,
):
    width = q_ref.shape[1]

    @pl.when(pl.program_id(0) == 0)
    def _():
        fill_length_bias(bias_scratch, lengths[0], flips[0])

    def put(block, context, largest, total):
        context_ref[block_rows(block), :] = join_heads(context).astype(bf16)
        logsum_ref[pl.ds(block, 1), :] = largest + jnp.log(total)

    def one(block):
        queries = spread_heads(q_ref[block_rows(block), :])
        names = [key_names[block, slot] for slot in range(SLOTS)]
        biases = [bias_names[block, slot] for slot in range(SLOTS)]
        scores = dot_nt(gather_blocks(k_ref, names), queries) + wide(gather_blocks(bias_scratch, biases), width)
        largest = jnp.max(scores, axis=0, keepdims=True)
        weights = jnp.exp(scores - largest)
        total = jnp.sum(weights, axis=0, keepdims=True)
        shares = (weights * (1.0 / total)).astype(bf16)
        put(block, dot_tn(shares, gather_blocks(v_ref, names)), largest, total)

    def body(step, carry):
        for within in range(unroll):
            one(step * unroll + within)
        return carry

    lax.fori_loop(0, query_blocks // unroll, body, 0)
    block = global_name[0]
    queries = spread_heads(q_ref[block_rows(block), :])
    tokens = k_ref.shape[0]
    chunk = SLOTS * BLOCK
    together = 4

    def score_chunk(step, largest):
        for within in range(together):
            rows = pl.ds(pl.multiple_of((step * together + within) * chunk, chunk), chunk)
            scores = dot_nt(k_ref[rows, :], queries) + wide(bias_scratch[rows, :], width)
            score_scratch[rows, :] = scores
            largest = jnp.maximum(largest, jnp.max(scores, axis=0, keepdims=True))
        return largest

    steps = tokens // chunk // together
    lanes = width
    largest = lax.fori_loop(0, steps, score_chunk, jnp.full((1, lanes), masked_score, f32))

    def value_chunk(step, carry):
        total, context = carry
        for within in range(together):
            rows = pl.ds(pl.multiple_of((step * together + within) * chunk, chunk), chunk)
            weights = jnp.exp(score_scratch[rows, :] - largest)
            total = total + jnp.sum(weights, axis=0, keepdims=True)
            context = context + dot_tn(weights.astype(bf16), v_ref[rows, :])
        return total, context

    total, context = lax.fori_loop(
        0, steps, value_chunk, (jnp.zeros((1, lanes), f32), jnp.zeros((lanes, lanes), f32))
    )
    context = context * jnp.transpose(jnp.broadcast_to(1.0 / total, (lanes, lanes)))
    put(block, context, largest, total)


def attend(plan, length, flip, q, k, v):
    query_names, key_names, bias_names, global_name = plan
    query_rows, lanes = q.shape
    tokens = k.shape[0]
    query_blocks = query_rows // BLOCK
    width = 128

    def lanes_of(rows):
        return pl.BlockSpec((rows, width), lambda step, *_: (0, step))

    return pl.pallas_call(
        partial(forward_kernel, unroll=query_blocks, query_blocks=query_blocks),
        grid_spec=pltpu.PrefetchScalarGridSpec(
            num_scalar_prefetch=5,
            grid=(lanes // width,),
            in_specs=[lanes_of(query_rows), lanes_of(tokens), lanes_of(tokens)],
            out_specs=[lanes_of(query_rows), lanes_of(query_blocks)],
            scratch_shapes=[
                pltpu.VMEM((tokens + BLOCK, 128), f32),
                pltpu.VMEM((tokens, width), f32),
            ],
        ),
        out_shape=[
            jax.ShapeDtypeStruct((query_rows, lanes), bf16),
            jax.ShapeDtypeStruct((query_blocks, lanes), f32),
        ],
        compiler_params=pltpu.CompilerParams(vmem_limit_bytes=60 << 20),
        cost_estimate=pl.CostEstimate(flops=10**9, bytes_accessed=10**6, transcendentals=10**5),
        name="attend_forward",
    )(key_names, bias_names, global_name, length, flip, q, k, v)


def backward_kernel(
    query_names, key_names, bias_names, lengths, flips,
    q_ref, k_ref, v_ref, back_ref, context_ref, logsum_ref,
    back_q_ref, back_k_ref, back_v_ref, bias_scratch, q_scratch, k_scratch, v_scratch, *, unroll, items,
):
    width = q_ref.shape[1]
    fill_length_bias(bias_scratch, lengths[0], flips[0])
    q_scratch[...] = jnp.zeros_like(q_scratch)
    k_scratch[...] = jnp.zeros_like(k_scratch)
    v_scratch[...] = jnp.zeros_like(v_scratch)
    ones = jnp.ones((16, width), bf16)

    def one(item):
        block = query_names[item]
        rows = block_rows(block)
        queries = spread_heads(q_ref[rows, :])
        back = back_ref[rows, :]
        backs = spread_heads(back)
        product = (back.astype(f32) * context_ref[rows, :].astype(f32)).astype(bf16)
        inner = dot_nt(ones, spread_heads(product))[0:1]
        logsum = logsum_ref[pl.ds(block, 1), :]
        names = [key_names[item, slot] for slot in range(SLOTS)]
        biases = [bias_names[item, slot] for slot in range(SLOTS)]
        keys = gather_blocks(k_ref, names)
        scores = dot_nt(keys, queries) + wide(gather_blocks(bias_scratch, biases), width)
        shares = jnp.exp(scores - logsum)
        back_shares = dot_nt(gather_blocks(v_ref, names), backs)
        back_values = dot_nn(shares.astype(bf16), backs)
        back_scores = (shares * (back_shares - inner)).astype(bf16)
        back_keys = dot_nn(back_scores, queries)
        q_scratch[rows, :] += join_heads(dot_tn(back_scores, keys))
        for slot in range(SLOTS):
            part = slice(slot * BLOCK, (slot + 1) * BLOCK)
            v_scratch[block_rows(names[slot]), :] += back_values[part]
            k_scratch[block_rows(names[slot]), :] += back_keys[part]

    def body(step, carry):
        for within in range(unroll):
            one(step * unroll + within)
        return carry

    lax.fori_loop(0, items // unroll, body, 0)
    back_q_ref[...] = (q_scratch[...] * HEAD_DIM ** (-0.5)).astype(bf16)
    back_k_ref[...] = k_scratch[...].astype(bf16)
    back_v_ref[...] = v_scratch[...].astype(bf16)


def attend_back(plan, length, flip, group, q, k, v, back, context, logsum):
    first, width = group
    query_names, key_names, bias_names, _ = plan
    query_rows = q.shape[0]
    tokens = k.shape[0]
    query_blocks = query_rows // BLOCK
    q_in, k_in = lanes_spec(query_rows, first, width), lanes_spec(tokens, first, width)
    q_out, k_out = lanes_spec(query_rows, 0, width), lanes_spec(tokens, 0, width)
    return pl.pallas_call(
        partial(backward_kernel, unroll=8, items=query_names.shape[0]),
        grid_spec=pltpu.PrefetchScalarGridSpec(
            num_scalar_prefetch=5,
            grid=(1,),
            in_specs=[q_in, k_in, k_in, q_in, q_in, lanes_spec(query_blocks, first, width)],
            out_specs=[q_out, k_out, k_out],
            scratch_shapes=[
                pltpu.VMEM((tokens + BLOCK, 128), f32),
                pltpu.VMEM((query_rows, width), f32),
                pltpu.VMEM((tokens, width), f32),
                pltpu.VMEM((tokens, width), f32),
            ],
        ),
        out_shape=[
            jax.ShapeDtypeStruct((query_rows, width), bf16),
            jax.ShapeDtypeStruct((tokens, width), bf16),
            jax.ShapeDtypeStruct((tokens, width), bf16),
        ],
        compiler_params=pltpu.CompilerParams(vmem_limit_bytes=60 << 20),
        cost_estimate=pl.CostEstimate(flops=10**9, bytes_accessed=10**6, transcendentals=10**5),
        name="attend_backward",
    )(query_names, key_names, bias_names, length, flip, q, k, v, back, context, logsum)


def project_kernel(core, x_ref, x_near_ref, w_q, w_k, w_v, b_q, b_v, q_ref, k_ref, v_ref):
    step = pl.program_id(0)

    def project(tile):
        q = (dot_nn(tile, w_q[...]) + b_q[...]).astype(bf16)
        q_ref[...] = q * jnp.asarray(HEAD_DIM ** (-0.5), bf16)
        k_ref[...] = dot_nn(tile, w_k[...]).astype(bf16)
        v_ref[...] = (dot_nn(tile, w_v[...]) + b_v[...]).astype(bf16)

    @pl.when(step < pl.num_programs(0) // 2)
    def _():
        project(x_ref[...])

    @pl.when(step >= pl.num_programs(0) // 2)
    def _():
        project(x_near_ref[...])


def project_far_kernel(core, x_ref, x_near_ref, w_k, w_v, b_v, k_old, v_old, k_ref, v_ref):
    step = pl.program_id(0)

    def project(tile):
        k_ref[...] = dot_nn(tile, w_k[...]).astype(bf16)
        v_ref[...] = (dot_nn(tile, w_v[...]) + b_v[...]).astype(bf16)

    @pl.when(step < pl.num_programs(0) // 2)
    def _():
        project(x_ref[...])

    @pl.when(step >= pl.num_programs(0) // 2)
    def _():
        project(x_near_ref[...])


TILE = 512


def piece_spec(piece, per, width, tile=TILE):
    return pl.BlockSpec((tile, width), lambda step, *_: (jnp.clip(step - piece * per, 0, per - 1), 0))


def own_weight(which):
    return pl.BlockSpec((D, D // 2), lambda step, core, *_: (0, 2 * which + core[0]))


def own_bias():
    return pl.BlockSpec((1, D // 2), lambda step, core, *_: (0, core[0]))


def project_chip(core, x, x_near, qkv_weight, query_bias, value_bias):
    rows = x.shape[0]
    half = D // 2
    per = rows // TILE
    out = pl.BlockSpec((TILE, half), lambda step, *_: (step, 0))
    return pl.pallas_call(
        project_kernel,
        grid_spec=pltpu.PrefetchScalarGridSpec(
            num_scalar_prefetch=1,
            grid=(2 * per,),
            in_specs=[piece_spec(0, per, D), piece_spec(1, per, D)]
            + [own_weight(0), own_weight(1), own_weight(2), own_bias(), own_bias()],
            out_specs=[out, out, out],
        ),
        out_shape=[
            jax.ShapeDtypeStruct((2 * rows, half), bf16),
            jax.ShapeDtypeStruct((4 * rows, half), bf16),
            jax.ShapeDtypeStruct((4 * rows, half), bf16),
        ],
        compiler_params=pltpu.CompilerParams(vmem_limit_bytes=60 << 20),
        cost_estimate=pl.CostEstimate(flops=4 * 10**9, bytes_accessed=10**7, transcendentals=0),
        name="project_chip",
    )(core, x, x_near, qkv_weight, qkv_weight, qkv_weight, query_bias, value_bias)


def project_far(core, x_far, x_far_near, qkv_weight, value_bias, k, v):
    rows = x_far.shape[0]
    half = D // 2
    per = rows // TILE
    out = pl.BlockSpec((TILE, half), lambda step, *_: (2 * per + step, 0))
    kept = pl.BlockSpec(memory_space=pl.ANY)
    return pl.pallas_call(
        project_far_kernel,
        grid_spec=pltpu.PrefetchScalarGridSpec(
            num_scalar_prefetch=1,
            grid=(2 * per,),
            in_specs=[piece_spec(0, per, D), piece_spec(1, per, D)]
            + [own_weight(1), own_weight(2), own_bias(), kept, kept],
            out_specs=[out, out],
        ),
        out_shape=[jax.ShapeDtypeStruct(k.shape, bf16), jax.ShapeDtypeStruct(v.shape, bf16)],
        input_output_aliases={6: 0, 7: 1},
        compiler_params=pltpu.CompilerParams(vmem_limit_bytes=60 << 20),
        cost_estimate=pl.CostEstimate(flops=3 * 10**9, bytes_accessed=10**7, transcendentals=0),
        name="project_far",
    )(core, x_far, x_far_near, qkv_weight, qkv_weight, value_bias, k, v)


def gelu_pair(x):
    t = 1.0 / (1.0 + (0.3275911 * 0.5**0.5) * jnp.abs(x))
    bell = jnp.exp(-0.5 * x * x)
    poly = 0.7107068705 + t * (-0.7265760135 + t * 0.5307027145)
    tail = t * (0.127414796 + t * (-0.142248368 + t * poly)) * bell
    cdf = jnp.where(x < 0, tail, 1.0 - tail)
    return x * cdf, cdf + x * bell * 0.3989422804014327


def norm_parts(value):
    center = value - jnp.mean(value, axis=-1, keepdims=True)
    spread = jnp.mean(center * center, axis=-1, keepdims=True)
    scale = lax.rsqrt(spread + norm_epsilon)
    return center * scale, scale


def norm_back(slope, normed, scale):
    along = jnp.mean(slope * normed, axis=-1, keepdims=True)
    return scale * (slope - jnp.mean(slope, axis=-1, keepdims=True) - normed * along)


def column_sum(value):
    return jnp.sum(value, axis=0, keepdims=True)


PIECES = 16
VECTOR_ROWS = 128


def row_spec(tile, width):
    return pl.BlockSpec((tile, width), lambda step, *_: (step, 0))


def stack_spec(count, tile, width):
    return pl.BlockSpec((count, tile, width), lambda step, *_: (0, step, 0))


def whole_spec(shape):
    return pl.BlockSpec(shape, lambda step, *_: (0,) * len(shape))


def middle_kernel(
    core,
    own_ref, other_ref, x_ref, cot_ref, vector_ref, expand_bias_ref, proj_hbm, expand_hbm, shrink_hbm,
    output_ref, back_one_ref, back_own_ref, back_other_ref, wide_keep, wide_send, lows_ref, sums_ref,
    proj_w, expand_w, shrink_w, slope_s, wide_s, weight_sems, wide_sems, *, chunk,
):
    step = pl.program_id(0)
    half = D // 2
    ff = expand_w.shape[1]
    chunks = ff // chunk
    hc = core[0]
    loads = [
        pltpu.make_async_copy(proj_hbm.at[pl.ds(hc * half, half)], proj_w.at[pl.ds(0, half)], weight_sems.at[0]),
        pltpu.make_async_copy(
            proj_hbm.at[pl.ds((1 - hc) * half, half)], proj_w.at[pl.ds(half, half)], weight_sems.at[1]
        ),
        pltpu.make_async_copy(expand_hbm, expand_w, weight_sems.at[2]),
        pltpu.make_async_copy(shrink_hbm, shrink_w, weight_sems.at[3]),
    ]

    @pl.when(step == 0)
    def _():
        for load in loads:
            load.start()
        sums_ref[...] = jnp.zeros_like(sums_ref)
        for load in loads:
            load.wait()

    def vector(row):
        return vector_ref[pl.ds(row, 1), :]

    slot = lax.rem(step, 2)
    tile = x_ref.shape[0]

    def wide_copies(slot, first_row):
        copies = []
        for which in range(2):
            for side, out in enumerate((wide_keep, wide_send)):
                first = pl.multiple_of((hc if side == 0 else 1 - hc) * (ff // 2), ff // 2)
                copies.append(
                    pltpu.make_async_copy(
                        wide_s.at[slot, which, :, pl.ds(first, ff // 2)],
                        out.at[which, pl.ds(pl.multiple_of(first_row, tile), tile)],
                        wide_sems.at[slot, 2 * which + side],
                    )
                )
        return copies

    @pl.when(step >= 2)
    def _():
        for copy in wide_copies(slot, 0):
            copy.wait()

    context = jnp.concatenate([own_ref[...], other_ref[...]], axis=1)
    resid = x_ref[...].astype(f32) + dot_nn(context, proj_w[...]) + vector(0)
    normed_one, scale_one = norm_parts(resid)
    hidden = normed_one * vector(1) + vector(2)
    low = hidden.astype(bf16)
    lows_ref[0] = low
    resid_two = hidden + vector(3)

    for part in range(chunks):
        cols = slice(part * chunk, (part + 1) * chunk)
        inner = dot_nn(low, expand_w[:, cols]) + expand_bias_ref[:, cols]
        active, slope = gelu_pair(inner)
        active = active.astype(bf16)
        wide_s[slot, 0, :, cols] = active
        slope_s[:, cols] = slope.astype(bf16)
        resid_two = resid_two + dot_nn(active, shrink_w[cols, :])
    normed_two, scale_two = norm_parts(resid_two)
    output_ref[...] = (normed_two * vector(4) + vector(5)).astype(bf16)
    cot = cot_ref[...].astype(f32)
    back_two = norm_back(vector(4) * cot, normed_two, scale_two)
    low_two = back_two.astype(bf16)
    lows_ref[1] = low_two
    sums_ref[3:4, :] += column_sum(low_two.astype(f32))
    sums_ref[4:5, :] += column_sum(cot * normed_two)
    sums_ref[5:6, :] += column_sum(cot)
    back = back_two
    for part in range(chunks):
        cols = slice(part * chunk, (part + 1) * chunk)
        back_inner = (dot_nt(low_two, shrink_w[cols, :]) * slope_s[:, cols].astype(f32)).astype(bf16)
        wide_s[slot, 1, :, cols] = back_inner
        sums_ref[8 + part : 9 + part, :] += column_sum(back_inner.astype(f32))
        back = back + dot_nt(back_inner, expand_w[:, cols])
    sums_ref[1:2, :] += column_sum(back * normed_one)
    sums_ref[2:3, :] += column_sum(back)
    back_one = norm_back(vector(1) * back, normed_one, scale_one)
    back_one_ref[...] = back_one
    low_one = back_one.astype(bf16)
    lows_ref[2] = low_one
    sums_ref[0:1, :] += column_sum(low_one.astype(f32))
    back_context = dot_nt(low_one, proj_w[...]).astype(bf16)
    back_own_ref[...] = back_context[:, :half]
    back_other_ref[...] = back_context[:, half:]
    for copy in wide_copies(slot, step * tile):
        copy.start()

    @pl.when(step == pl.num_programs(0) - 1)
    def _():
        for other in range(2):
            for copy in wide_copies(other, 0):
                copy.wait()


def middle(core, own, other, x, cot, vectors, expand_bias, proj_weight, expand_weight, shrink_weight):
    rows = x.shape[0]
    ff = expand_weight.shape[1]
    half = D // 2
    tile = 256
    kept = pl.BlockSpec(memory_space=pl.ANY)
    assert ff // D == 4
    return pl.pallas_call(
        partial(middle_kernel, chunk=D),
        grid_spec=pltpu.PrefetchScalarGridSpec(
            num_scalar_prefetch=1,
            grid=(rows // tile,),
            in_specs=[row_spec(tile, half)] * 2
            + [row_spec(tile, D)] * 2
            + [whole_spec(vectors.shape), whole_spec(expand_bias.shape), kept, kept, kept],
            out_specs=[row_spec(tile, D)] * 2
            + [row_spec(tile, half)] * 2
            + [kept] * 2
            + [stack_spec(3, tile, D), whole_spec((16, D))],
            scratch_shapes=[
                pltpu.VMEM((D, D), bf16),
                pltpu.VMEM((D, ff), bf16),
                pltpu.VMEM((ff, D), bf16),
                pltpu.VMEM((tile, ff), bf16),
                pltpu.VMEM((2, 2, tile, ff), bf16),
                pltpu.SemaphoreType.DMA((4,)),
                pltpu.SemaphoreType.DMA((2, 4)),
            ],
        ),
        out_shape=[
            jax.ShapeDtypeStruct((rows, D), bf16),
            jax.ShapeDtypeStruct((rows, D), f32),
            jax.ShapeDtypeStruct((rows, half), bf16),
            jax.ShapeDtypeStruct((rows, half), bf16),
            jax.ShapeDtypeStruct((2, rows, ff // 2), bf16),
            jax.ShapeDtypeStruct((2, rows, ff // 2), bf16),
            jax.ShapeDtypeStruct((3, rows, D), bf16),
            jax.ShapeDtypeStruct((16, D), f32),
        ],
        compiler_params=pltpu.CompilerParams(vmem_limit_bytes=60 << 20),
        cost_estimate=pl.CostEstimate(flops=10**9, bytes_accessed=10**7, transcendentals=10**6),
        name="middle",
    )(core, own, other, x, cot, vectors, expand_bias, proj_weight, expand_weight, shrink_weight)


def weights_kernel(
    places, wide_own, wide_other, lows_own, lows_other, context_ref, sums_own, sums_other, *refs
):
    packed = refs[:4]
    shrink_g, expand_g, proj_g = refs[4:]
    step = pl.program_id(0)
    half = D // 2

    @pl.when(step == 0)
    def _():
        shrink_g[...] = jnp.zeros_like(shrink_g)
        expand_g[...] = jnp.zeros_like(expand_g)
        proj_g[...] = jnp.zeros_like(proj_g)
        proj_g[half : half + 16, :] = sums_own[...] + sums_other[...]

    def add(wide, lows):
        shrink_g[...] += dot_tn(wide[0], lows[1])
        expand_g[...] += dot_tn(lows[0], wide[1])
        proj_g[:half, :] += dot_tn(context_ref[...], lows[2])

    @pl.when(step < pl.num_programs(0) // 2)
    def _():
        add(wide_own, lows_own)

    @pl.when(step >= pl.num_programs(0) // 2)
    def _():
        add(wide_other, lows_other)

    @pl.when(step == pl.num_programs(0) - 1)
    def _():
        rows = shrink_g.shape[0] // PIECES
        extra = proj_g.shape[0] // (2 * PIECES)
        wide = expand_g.shape[1] // D
        for piece in range(PIECES):
            place = piece % (PIECES // 2)
            first = piece ^ places[0]
            second = piece ^ places[1]
            out = packed[piece // (PIECES // 2)]
            out[place, :rows, :] = shrink_g[pl.ds(pl.multiple_of(first * rows, rows), rows), :].astype(bf16)
            out[place, rows:, :] = proj_g[pl.ds(pl.multiple_of(first * extra, extra), extra), :].astype(bf16)
            out = packed[2 + piece // (PIECES // 2)]
            down = pl.ds(pl.multiple_of((second // wide) * rows, rows), rows)
            across = pl.ds(pl.multiple_of(lax.rem(second, wide) * D, D), D)
            out[place, :rows, :] = expand_g[down, across].astype(bf16)
            part = pl.ds(pl.multiple_of((PIECES + second) * extra, extra), extra)
            out[place, rows:, :] = proj_g[part, :].astype(bf16)


def weight_grads(places, wide_own, wide_other, lows_own, lows_other, context, sums_own, sums_other):
    _, rows, wide = wide_own.shape
    half = D // 2
    per = rows // TILE
    piece_rows = wide // PIECES + (half + VECTOR_ROWS) // (2 * PIECES)

    def own(count, width):
        return pl.BlockSpec((count, TILE, width), lambda step, *_: (0, jnp.minimum(step, per - 1), 0))

    def other(count, width):
        return pl.BlockSpec((count, TILE, width), lambda step, *_: (0, jnp.maximum(step - per, 0), 0))

    packed_shape = (PIECES // 2, piece_rows, D)
    return pl.pallas_call(
        weights_kernel,
        grid_spec=pltpu.PrefetchScalarGridSpec(
            num_scalar_prefetch=1,
            grid=(2 * per,),
            in_specs=[own(2, wide), other(2, wide), own(3, D), other(3, D), row_spec(TILE, half)]
            + [whole_spec((16, D))] * 2,
            out_specs=[whole_spec(packed_shape)] * 4,
            scratch_shapes=[
                pltpu.VMEM((wide, D), f32),
                pltpu.VMEM((D, wide), f32),
                pltpu.VMEM((half + VECTOR_ROWS, D), f32),
            ],
        ),
        out_shape=[jax.ShapeDtypeStruct(packed_shape, bf16)] * 4,
        compiler_params=pltpu.CompilerParams(vmem_limit_bytes=60 << 20),
        cost_estimate=pl.CostEstimate(flops=10**9, bytes_accessed=10**7, transcendentals=0),
        name="weight_grads",
    )(places, wide_own, wide_other, lows_own, lows_other, context, sums_own, sums_other)


def quarters_spec(place, per):
    return pl.BlockSpec((TILE, D), lambda step, *_: (jnp.clip(step - place * per, 0, per - 1), 0))


def input_kernel(core, *refs, per):
    weights, arrays, outs = refs[:3], refs[3:-4], refs[-4:]
    pairs = len(arrays) // 3
    step = pl.program_id(0)

    def through(which):
        back = jnp.concatenate([ref[...] for ref in arrays[which * pairs : (which + 1) * pairs]], axis=1)
        return dot_nt(back, weights[which][...])

    for place in range(4):

        @pl.when((step >= place * per) & (step < (place + 1) * per))
        def _():
            total = through(1) + through(2)
            if place >= 2:
                total = total + through(0)
            outs[place][...] = total.astype(bf16)


def input_parts(core, qkv_weight, back_qs, back_ks, back_vs, rows):
    per = rows // TILE
    tokens = [
        pl.BlockSpec((TILE, array.shape[1]), lambda step, *_: (lax.rem(step + 2 * per, 4 * per), 0)) for array in back_ks
    ]
    queries = [
        pl.BlockSpec((TILE, array.shape[1]), lambda step, *_: (jnp.maximum(step - 2 * per, 0), 0)) for array in back_qs
    ]
    return pl.pallas_call(
        partial(input_kernel, per=per),
        grid_spec=pltpu.PrefetchScalarGridSpec(
            num_scalar_prefetch=1,
            grid=(4 * per,),
            in_specs=[own_weight(which) for which in range(3)] + queries + 2 * tokens,
            out_specs=[quarters_spec(place, per) for place in range(4)],
        ),
        out_shape=[jax.ShapeDtypeStruct((rows, D), bf16)] * 4,
        compiler_params=pltpu.CompilerParams(vmem_limit_bytes=60 << 20),
        cost_estimate=pl.CostEstimate(flops=10**9, bytes_accessed=10**7, transcendentals=0),
        name="input_parts",
    )(core, *[qkv_weight] * 3, *back_qs, *back_ks, *back_vs)


QKV_PIECES = 16
JOINED_TILE = 1024


def joined_kernel(places, core, *refs, tiles, pairs):
    x_refs = refs[:4]
    arrays = refs[4 : 4 + 3 * pairs]
    packed = refs[4 + 3 * pairs : 8 + 3 * pairs]
    total, sums = refs[8 + 3 * pairs :]
    step = pl.program_id(0)
    half = D // 2
    per = tiles // 4

    @pl.when(step == 0)
    def _():
        total[...] = jnp.zeros_like(total)
        sums[...] = jnp.zeros_like(sums)

    def joined(first, last):
        return jnp.concatenate([ref[...] for ref in arrays[first * pairs : last * pairs]], axis=1)

    for piece in range(4):

        @pl.when((step >= piece * per) & (step < (piece + 1) * per))
        def _():
            first = 0 if piece < 2 else 1
            back = joined(first, 3)
            total[:, first * half : 3 * half] += dot_tn(x_refs[piece][...], back)
            sums[0:1, first * half :] += column_sum(back.astype(f32))

    @pl.when(step == tiles - 1)
    def _():
        rows = D // QKV_PIECES
        q_sums = jnp.transpose(jnp.broadcast_to(sums[0:1, :half], (128, half)))
        v_sums = jnp.transpose(jnp.broadcast_to(sums[0:1, 2 * half :], (128, half)))
        total[:half, 3 * half :] = q_sums
        total[half:, 3 * half :] = v_sums
        width = packed[0].shape[2]
        for color in range(2):
            cols = slice(color * width, (color + 1) * width)
            for piece in range(QKV_PIECES):
                part = pl.ds(pl.multiple_of((piece ^ places[color]) * rows, rows), rows)
                out = packed[2 * color + piece // (QKV_PIECES // 2)]
                out[piece % (QKV_PIECES // 2)] = total[part, cols].astype(bf16)


def joined_grads(places, core, xs, back_qs, back_ks, back_vs):
    rows = xs[0].shape[0]
    pairs = len(back_qs)
    per = rows // JOINED_TILE
    tiles = 4 * per
    width = D // 2 + 256
    tokens = [row_spec(JOINED_TILE, array.shape[1]) for array in back_ks]
    queries = [
        pl.BlockSpec((JOINED_TILE, array.shape[1]), lambda step, *_: (jnp.minimum(step, 2 * per - 1), 0)) for array in back_qs
    ]
    packed = pl.BlockSpec((QKV_PIECES // 2, D // QKV_PIECES, width), lambda step, *_: (0, 0, 0))
    packed_shape = jax.ShapeDtypeStruct((QKV_PIECES // 2, D // QKV_PIECES, width), bf16)
    return pl.pallas_call(
        partial(joined_kernel, tiles=tiles, pairs=pairs),
        grid_spec=pltpu.PrefetchScalarGridSpec(
            num_scalar_prefetch=2,
            grid=(tiles,),
            in_specs=[piece_spec(piece, per, D, JOINED_TILE) for piece in range(4)] + queries + 2 * tokens,
            out_specs=[packed] * 4,
            scratch_shapes=[pltpu.VMEM((D, 2 * width), f32), pltpu.VMEM((8, 3 * D // 2), f32)],
        ),
        out_shape=[packed_shape] * 4,
        compiler_params=pltpu.CompilerParams(vmem_limit_bytes=60 << 20),
        cost_estimate=pl.CostEstimate(flops=10**9, bytes_accessed=10**7, transcendentals=0),
        name="joined_grads",
    )(places, core, *xs, *back_qs, *back_ks, *back_vs)


def input_near_kernel(core, *refs):
    w_q, w_k, w_v, out = refs[0], refs[1], refs[2], refs[-1]
    arrays = refs[3:-1]
    pairs = len(arrays) // 3

    def joined(which):
        return jnp.concatenate([ref[...] for ref in arrays[which * pairs : (which + 1) * pairs]], axis=1)

    out[...] = (dot_nt(joined(0), w_q[...]) + dot_nt(joined(1), w_k[...]) + dot_nt(joined(2), w_v[...])).astype(bf16)


def input_near(core, qkv_weight, back_qs, back_ks, back_vs):
    rows = back_qs[0].shape[0]
    token = pl.BlockSpec((JOINED_TILE, 128), lambda step, *_: (step, 0))
    arrays = list(back_qs) + list(back_ks) + list(back_vs)
    return pl.pallas_call(
        input_near_kernel,
        grid_spec=pltpu.PrefetchScalarGridSpec(
            num_scalar_prefetch=1,
            grid=(rows // JOINED_TILE,),
            in_specs=[own_weight(0), own_weight(1), own_weight(2)] + [token] * len(arrays),
            out_specs=pl.BlockSpec((JOINED_TILE, D), lambda step, *_: (step, 0)),
        ),
        out_shape=jax.ShapeDtypeStruct((rows, D), bf16),
        compiler_params=pltpu.CompilerParams(vmem_limit_bytes=60 << 20),
        cost_estimate=pl.CostEstimate(flops=10**9, bytes_accessed=10**7, transcendentals=0),
        name="input_near",
    )(core, qkv_weight, qkv_weight, qkv_weight, *arrays)


GROUP = 8


def unpack_kernel(numbers, *refs, parts, outs, held):
    sources = refs[:4]
    targets = refs[4 + held : 4 + held + outs]
    stages = refs[4 + held + outs : -1]
    sems = refs[-1]
    step = pl.program_id(0)

    def copy(color, which, slot, number, elsewhere=False):
        part = parts[color][which]
        out, place = part["instead"][1:] if elsewhere else (part["out"], part["place"])
        row, col = place(number)
        rows, cols = part["rows"][1] - part["rows"][0], part["cols"][1] - part["cols"][0]
        target = targets[out].at[pl.ds(pl.multiple_of(row, rows), rows), pl.ds(pl.multiple_of(col, 128), cols)]
        at = part["at"]
        source = stages[color].at[slot, pl.ds(at[0], rows), pl.ds(at[1], cols)]
        return pltpu.make_async_copy(source, target, sems.at[color, which, slot])

    for place, source in enumerate(sources):
        color, side = place // 2, place % 2

        @pl.when(step == place)
        def _():
            for within in range(GROUP):
                slot = side * GROUP + within
                number = numbers[place * GROUP + within]
                stages[color][slot] = source[within].astype(f32)
                for which, part in enumerate(parts[color]):
                    if part["instead"] is None:
                        copy(color, which, slot, number).start()
                        continue
                    elsewhere = part["instead"][0](number)

                    @pl.when(elsewhere)
                    def _():
                        copy(color, which, slot, number, True).start()

                    @pl.when(jnp.logical_not(elsewhere))
                    def _():
                        copy(color, which, slot, number).start()

    @pl.when(step == pl.num_programs(0) - 1)
    def _():
        for color in range(2):
            for slot in range(2 * GROUP):
                for which in range(len(parts[color])):
                    copy(color, which, slot, 0).wait()


def unpack(numbers, sources, parts, out_shapes, held, name):
    count, rows, width = sources[0].shape
    assert count == GROUP and len(sources) == 4
    most = max(len(part) for part in parts)
    kept = pl.BlockSpec(memory_space=pl.ANY)
    return pl.pallas_call(
        partial(unpack_kernel, parts=parts, outs=len(out_shapes), held=len(held)),
        grid_spec=pltpu.PrefetchScalarGridSpec(
            num_scalar_prefetch=1,
            grid=(len(sources),),
            in_specs=[pl.BlockSpec((GROUP, rows, width), lambda step, *_: (0, 0, 0))] * len(sources) + [kept] * len(held),
            out_specs=[kept] * len(out_shapes),
            scratch_shapes=[pltpu.VMEM((2 * GROUP, rows, width), f32)] * 2
            + [pltpu.SemaphoreType.DMA((2, most, 2 * GROUP))],
        ),
        out_shape=[jax.ShapeDtypeStruct(shape, f32) for shape in out_shapes],
        input_output_aliases={1 + len(sources) + place: place for place in range(len(held))},
        compiler_params=pltpu.CompilerParams(vmem_limit_bytes=60 << 20),
        cost_estimate=pl.CostEstimate(flops=10**6, bytes_accessed=10**6, transcendentals=0),
        name=name,
    )(numbers, *sources, *held)


def part_of(rows, cols, out, place, instead=None):
    return {"rows": rows, "cols": cols, "at": (rows[0], cols[0]), "out": out, "place": place, "instead": instead}


def swap(value, axis, bit=1):
    size = lax.axis_size(axis)
    return lax.ppermute(value, axis, [(place, place ^ bit) for place in range(size)])


def place_of(order):
    number = jnp.zeros((), jnp.int32)
    for axis, bit in order:
        number = 2 * number + ((lax.axis_index(axis) & bit) // bit).astype(jnp.int32)
    return number


def add_low(left, right):
    return (left.astype(f32) + right.astype(f32)).astype(bf16)


class Chain:
    def __init__(self, scatter_order, gather_order, keep, first):
        self.orders = list(scatter_order) + list(gather_order)
        self.steps = len(scatter_order)
        self.keep, self.first, self.arrived = keep, first, None
        self.at = 0
        self.gathered = None
        self.other_gathered = None
        self.other_arrived = None

    def left(self):
        return len(self.orders) + 1 - self.at

    def send(self):
        if self.at < self.steps:
            if self.at == 0:
                return self.first
            half = self.keep.shape[0] // 2
            high = add_low(self.keep[half:], self.arrived[half:])
            self.keep = add_low(self.keep[:half], self.arrived[:half])
            return high
        if self.at == self.steps:
            total = add_low(self.keep, self.arrived)
            bit = 8
            while bit < lax.axis_size("dp"):
                total = add_low(total, swap(total, "dp", bit))
                bit *= 2
            self.gathered = total
        elif self.at < len(self.orders):
            self.gathered = jnp.concatenate([self.gathered, self.arrived], axis=0)
        else:
            return self.arrived
        return self.gathered

    def move(self, value):
        if self.at == len(self.orders):
            self.arrived, self.other_arrived = value, swap(value, "hc")
            self.at += 1
            return
        if self.at >= self.steps:
            self.gathered = value
        axis, bit = self.orders[self.at]
        self.arrived = swap(value, axis, bit)
        self.at += 1
        if self.at == len(self.orders):
            self.other_gathered = swap(value, "hc")


def gathered_numbers(number, scatter_order, gather_order):
    count = 1 << len(scatter_order)
    places = jnp.arange(count, dtype=jnp.int32)
    turned = jnp.zeros((count,), jnp.int32)
    for at, name in enumerate(gather_order):
        turned = turned + (((places >> at) & 1) << (len(scatter_order) - 1 - scatter_order.index(name)))
    return turned ^ number


def ready(*values):
    return lax.optimization_barrier(values)


def per_device(
    inputs, doc_lengths, random_blocks, qkv_weight, query_bias, value_bias, proj_weight, proj_bias,
    first_gain, first_shift, expand_weight, expand_bias, shrink_weight, shrink_bias,
    second_gain, second_shift, cotangent,
):
    hx = lax.axis_index("hx")
    hc = lax.axis_index("hc")
    docs, rows, _ = inputs.shape
    assert docs == 1 and lax.axis_size("hx") == 2 and lax.axis_size("hc") == 2
    half = D // 2
    ff = expand_weight.shape[1]
    x = inputs.reshape(rows, D)
    x_far = swap(x, "hx")
    x_near = swap(x, "hc")
    row_blocks = rows // BLOCK
    flip = (hx * 2 + hc).astype(jnp.int32) * row_blocks
    plan = block_plan(doc_lengths[0], random_blocks[0], flip, 2 * row_blocks)
    flip = flip.reshape(1)
    core = hc.astype(jnp.int32).reshape(1)
    chip_steps = {"x": ("hx", 1), "y": ("dp", 1), "n": ("dp", 2), "f": ("dp", 4)}
    orders = {
        name: tuple([chip_steps[step] for step in part] for part in text.split())
        for name, text in ORDERS.items()
    }

    def places_of(letter):
        return jnp.stack([place_of(orders[f"{letter}{color}"][0]) for color in range(2)])

    def numbers_of(letter, places):
        own = [gathered_numbers(places[color], *orders[f"{letter}{color}"]) for color in range(2)]
        parts = [slice(0, GROUP), slice(GROUP, 2 * GROUP)]
        return tuple(
            jnp.concatenate([own[color][part] + PIECES * side for color in range(2) for side in (core, 1 - core)])
            for part in parts
        )

    middle_places, joined_places = places_of("M"), places_of("Q")
    numbers = numbers_of("M", middle_places) + numbers_of("Q", joined_places)
    vectors = jnp.concatenate(
        [proj_bias, first_gain, first_shift, shrink_bias, second_gain, second_shift, query_bias, value_bias]
    ).reshape(8, D)
    vectors = vectors.astype(f32)
    bias_q, bias_v = vectors[6:7], vectors[7:8]
    expand_row = expand_bias.astype(f32).reshape(1, ff)

    q, k, v = project_chip(core, x, x_near, qkv_weight, bias_q, bias_v)
    x_far, q, expand_row, vectors, middle_places, joined_places, *rest = ready(
        x_far, q, expand_row, vectors, middle_places, joined_places, *numbers, *plan
    )
    numbers, plan = rest[:4], rest[4:]
    x_far_near = swap(x_far, "hc")
    k, v = project_far(core, x_far, x_far_near, qkv_weight, bias_v, k, v)
    context, logsum = attend(plan, doc_lengths, flip, q, k, v)
    other_context = swap(context[rows:], "hc")
    output, back_one, back_own, back_other, wide_keep, wide_send, lows, sums = middle(
        core, context, other_context, x, cotangent.reshape(rows, D), vectors,
        expand_row, proj_weight, expand_weight, shrink_weight,
    )
    from_other = swap(back_other, "hc")
    wide_send, lows_send, sums_send, from_other = ready(wide_send, lows, sums, from_other)
    back = jnp.concatenate([back_own, from_other], axis=0)
    wide_other, lows_other, sums_other = swap(wide_send, "hc"), swap(lows_send, "hc"), swap(sums_send, "hc")

    held = {"last": back}
    chains = {}

    def tie(value):
        value, held["last"] = ready(value, held["last"])
        return value

    def pairs_of(which):
        return [held["grads", pair][which] for pair in range(len(GROUPS))]

    rows_each, extra, wide_blocks = ff // 2 // PIECES, (D // 2 + VECTOR_ROWS) // (2 * PIECES), ff // 2 // D
    proj_pieces = half // extra

    def split(number):
        return number // PIECES, lax.rem(number, PIECES)

    def expand_place(number):
        side, piece = split(number)
        return piece // wide_blocks * rows_each, (side * wide_blocks + lax.rem(piece, wide_blocks)) * D

    def proj_place(color):
        def place(number):
            side, piece = split(number)
            return side * half + (color * PIECES + piece) * extra, number * 0

        return place

    def vector_place(number):
        side, piece = split(number)
        return (side * (2 * PIECES - proj_pieces) + PIECES + piece - proj_pieces) * extra, number * 0

    def joined_place(which, offset):
        def place(number):
            side, piece = split(number)
            return piece * (D // QKV_PIECES), which * D + side * half + offset

        return place

    def bias_place(number):
        side, piece = split(number)
        return (side * QKV_PIECES + piece) * (D // QKV_PIECES), number * 0

    each = D // QKV_PIECES
    middle_parts = [
        [
            part_of((0, rows_each), (0, D), 0, lambda n: (n * rows_each, n * 0)),
            part_of((rows_each, rows_each + extra), (0, D), 2, proj_place(0)),
        ],
        [
            part_of((0, rows_each), (0, D), 1, expand_place),
            part_of(
                (rows_each, rows_each + extra), (0, D), 2, proj_place(1),
                (lambda n: lax.rem(n, PIECES) >= proj_pieces - PIECES, 3, vector_place),
            ),
        ],
    ]
    joined_parts = [
        [
            part_of((0, each), (0, half), 0, joined_place(0, 0)),
            part_of((0, each), (half, half + 256), 0, joined_place(1, 0)),
        ],
        [
            part_of((0, each), (0, 128), 0, joined_place(1, 256)),
            part_of((0, each), (128, 128 + half), 0, joined_place(2, 0)),
            part_of((0, each), (128 + half, 256 + half), 1, bias_place),
        ],
    ]
    layouts = {
        "M": (middle_parts, [(ff, D), (D, ff), (D, D), (2 * VECTOR_ROWS, D)], numbers[:2]),
        "Q": (joined_parts, [(D, 3 * D), (2 * D, 128)], numbers[2:]),
    }

    def run(name):
        if name.startswith("attend"):
            pair = int(name[-1])
            held["grads", pair] = attend_back(
                plan, doc_lengths, flip, GROUPS[pair], q, k, v, tie(back), context, logsum
            )
            held["last"] = held["grads", pair][0]
        elif name == "weights":
            packed = weight_grads(
                middle_places, tie(wide_keep), wide_other, lows, lows_other, context, sums, sums_other
            )
            held["last"] = packed[0]
            for color in range(2):
                chains[f"M{color}"] = Chain(*orders[f"M{color}"], packed[2 * color], packed[2 * color + 1])
        elif name == "joined":
            back_qs = pairs_of(0)
            back_qs[0] = tie(back_qs[0])
            packed = joined_grads(
                joined_places, core, (x, x_near, x_far, x_far_near), back_qs, pairs_of(1), pairs_of(2)
            )
            held["last"] = packed[0]
            for color in range(2):
                chains[f"Q{color}"] = Chain(*orders[f"Q{color}"], packed[2 * color], packed[2 * color + 1])
        elif name == "inputs":
            back_ks = pairs_of(1)
            back_ks[0] = tie(back_ks[0])
            far, far_others, near, near_others = input_parts(core, qkv_weight, pairs_of(0), back_ks, pairs_of(2), rows)
            held["last"] = far
            held["far"] = far, swap(far_others, "hc")
            held["near"] = near, swap(near_others, "hc")
        elif name == "dx":
            value = tie(add_low(*held["far"]))
            held["last"] = value
            held["from_far"] = swap(value, "hx")
        elif name == "input":
            near, from_near = held["near"]
            near = tie(near)
            value = back_one + near.astype(f32) + from_near.astype(f32) + held["from_far"].astype(f32)
            held["last"] = held["input"] = value
        elif name.startswith("early") or name.startswith("late"):
            letter = name[-1]
            parts, shapes, places = layouts[letter]
            early = name.startswith("early")
            sides = ("gathered", "other_gathered") if early else ("arrived", "other_arrived")
            sources = [getattr(chains[f"{letter}{color}"], side) for color in range(2) for side in sides]
            sources[0] = tie(sources[0])
            held["out", letter] = unpack(
                places[0 if early else 1], sources, parts, shapes, () if early else held["out", letter],
                f"unpack_{letter}",
            )
            held["last"] = held["out", letter][0]
        else:
            chain = chains[name]
            value = tie(chain.send())
            chain.move(value)
            held["last"] = value

    for names in SEQUENCE:
        for name in names.split():
            run(name)
    assert all(chain.left() == 0 for chain in chains.values())
    grad_shrink, grad_expand, grad_proj, vector = held["out", "M"]
    grad_qkv, bias = held["out", "Q"]
    grad_query_bias = jnp.concatenate([bias[:half, 0], bias[D : D + half, 0]])
    grad_value_bias = jnp.concatenate([bias[half:D, 0], bias[D + half :, 0]])
    grad_expand_bias = vector[8 : 8 + ff // D].reshape(ff)
    return (
        output.reshape(docs, rows, D),
        held["input"].reshape(docs, rows, D),
        grad_qkv, grad_query_bias, grad_value_bias, grad_proj, vector[0], vector[1], vector[2],
        grad_expand, grad_expand_bias, grad_shrink, vector[3], vector[4], vector[5],
    )


ORDERS = {"M0": "xnyf fnxy", "M1": "nxfy fxyn", "Q0": "nyxf yfnx", "Q1": "yxnf fnyx"}
SEQUENCE = (
    "attend0 weights M1 M0",
    "attend1 inputs M1 M0",
    "dx joined M1 M0",
    "Q1 Q0 M0 M1",
    "Q0 Q1 M1 M0",
    "input Q0 Q1 M1",
    "Q0 Q1 M0 Q0",
    "M1 Q1 Q0 M0",
    "Q1 Q0 Q1 M1",
    "Q0 M0 Q1 earlyQ",
    "earlyM Q1 Q0 lateQ",
    "M1 M0 lateM",
)


def solution(mesh):
    dp = mesh.shape["dp"]
    heads = mesh.shape["heads"]
    split = Mesh(mesh.devices.reshape(dp, heads // 2, 2), ("dp", "hx", "hc"))
    rows = P("dp", ("hx", "hc"), None)
    in_specs = (rows, P("dp"), P("dp", None, None)) + (P(),) * 13 + (rows,)
    out_specs = (rows, rows) + (P(),) * 13
    return jax.shard_map(
        per_device, mesh=split, in_specs=in_specs, out_specs=out_specs, check_vma=False
    )
```

```python
from functools import partial

import jax
import jax.numpy as jnp
from jax import lax
from jax.experimental import pallas as pl
from jax.experimental.pallas import tpu as pltpu
from jax.sharding import Mesh
from jax.sharding import PartitionSpec as P

D = 768
HEADS = 12
HEAD_DIM = 64
BLOCK = 64
SLOTS = 8
norm_epsilon = 1e-12
masked_score = -1e30
f32 = jnp.float32
bf16 = jnp.bfloat16


def dot_nn(left, right):
    return lax.dot_general(left, right, (((1,), (0,)), ((), ())), preferred_element_type=f32)


def dot_nt(left, right):
    return lax.dot_general(left, right, (((1,), (1,)), ((), ())), preferred_element_type=f32)


def dot_tn(left, right):
    return lax.dot_general(left, right, (((0,), (0,)), ((), ())), preferred_element_type=f32)


def layer_norm(values, scaling, offset):
    center = values - jnp.mean(values, axis=-1, keepdims=True)
    spread = jnp.mean(center * center, axis=-1, keepdims=True)
    return center * lax.rsqrt(spread + norm_epsilon) * scaling + offset


def block_plan(length, randoms, flip, query_blocks):
    blocks = randoms.shape[0]
    last = (length + BLOCK - 1) // BLOCK - 1
    places = jnp.arange(query_blocks, dtype=jnp.int32) ^ flip
    own_randoms = jnp.take_along_axis(randoms, places[:, None], axis=0)
    zero = jnp.zeros((query_blocks,), jnp.int32)
    candidates = jnp.concatenate(
        [
            jnp.stack([places - 1, places, places + 1, zero, zero + last], axis=1),
            own_randoms,
        ],
        axis=1,
    )
    usable = (candidates >= 0) & (candidates < blocks)
    same = candidates[:, :, None] == candidates[:, None, :]
    before = jnp.arange(SLOTS)[:, None] > jnp.arange(SLOTS)[None, :]
    usable = usable & ~jnp.any(same & before[None], axis=2)
    is_global = (places == 0) | (places == last)
    usable = usable & ~is_global[:, None]
    names = jnp.clip(candidates, 0, blocks - 1) ^ flip
    global_name = jnp.where((flip ^ last) < query_blocks, flip ^ last, flip)
    every = jnp.arange(blocks, dtype=jnp.int32).reshape(blocks // SLOTS, SLOTS)
    query_names = jnp.concatenate(
        [
            jnp.arange(query_blocks, dtype=jnp.int32),
            jnp.zeros((blocks // SLOTS,), jnp.int32) + global_name,
        ]
    )
    key_names = jnp.concatenate([names, every])
    bias_names = jnp.concatenate([jnp.where(usable, names, blocks), every])
    return query_names, key_names, bias_names, global_name.reshape(1)


GROUPS = ((0, 256), (256, 128))


def spread_heads(rows):
    lane = lax.broadcasted_iota(jnp.int32, rows.shape, 1)
    zero = jnp.zeros_like(rows)
    heads = rows.shape[1] // HEAD_DIM
    return jnp.concatenate([jnp.where(lane // HEAD_DIM == head, rows, zero) for head in range(heads)], axis=0)


def join_heads(stacked):
    width = stacked.shape[1]
    lane = lax.broadcasted_iota(jnp.int32, (BLOCK, width), 1)
    joined = stacked[:BLOCK]
    for head in range(1, width // HEAD_DIM):
        joined = jnp.where(lane // HEAD_DIM == head, stacked[head * BLOCK : (head + 1) * BLOCK], joined)
    return joined


def wide(bias, width):
    return jnp.concatenate([bias] * (width // bias.shape[1]), axis=1)


def lanes_spec(rows, first, width):
    return pl.BlockSpec((rows, width), lambda step, *_: (0, first // width))


def block_rows(name):
    return pl.ds(pl.multiple_of(name * BLOCK, BLOCK), BLOCK)


def gather_blocks(ref, names):
    return jnp.concatenate([ref[block_rows(name), :] for name in names], axis=0)


def fill_length_bias(bias_scratch, length, flip):
    rows = bias_scratch.shape[0] - BLOCK
    place = lax.broadcasted_iota(jnp.int32, bias_scratch.shape, 0)
    token = (((place // BLOCK) ^ flip) * BLOCK) + place % BLOCK
    live = (token < length) & (place < rows)
    bias_scratch[...] = jnp.where(live, 0.0, masked_score)


def forward_kernel(
    key_names, bias_names, global_name, lengths, flips,
    q_ref, k_ref, v_ref, context_ref, logsum_ref, bias_scratch, score_scratch, *, unroll, query_blocks,
):
    width = q_ref.shape[1]

    @pl.when(pl.program_id(0) == 0)
    def _():
        fill_length_bias(bias_scratch, lengths[0], flips[0])

    def put(block, context, largest, total):
        context_ref[block_rows(block), :] = join_heads(context).astype(bf16)
        logsum_ref[pl.ds(block, 1), :] = largest + jnp.log(total)

    def one(block):
        queries = spread_heads(q_ref[block_rows(block), :])
        names = [key_names[block, slot] for slot in range(SLOTS)]
        biases = [bias_names[block, slot] for slot in range(SLOTS)]
        scores = dot_nt(gather_blocks(k_ref, names), queries) + wide(gather_blocks(bias_scratch, biases), width)
        largest = jnp.max(scores, axis=0, keepdims=True)
        weights = jnp.exp(scores - largest)
        total = jnp.sum(weights, axis=0, keepdims=True)
        shares = (weights * (1.0 / total)).astype(bf16)
        put(block, dot_tn(shares, gather_blocks(v_ref, names)), largest, total)

    def body(step, carry):
        for within in range(unroll):
            one(step * unroll + within)
        return carry

    lax.fori_loop(0, query_blocks // unroll, body, 0)
    block = global_name[0]
    queries = spread_heads(q_ref[block_rows(block), :])
    tokens = k_ref.shape[0]
    chunk = SLOTS * BLOCK
    together = 4

    def score_chunk(step, largest):
        for within in range(together):
            rows = pl.ds(pl.multiple_of((step * together + within) * chunk, chunk), chunk)
            scores = dot_nt(k_ref[rows, :], queries) + wide(bias_scratch[rows, :], width)
            score_scratch[rows, :] = scores
            largest = jnp.maximum(largest, jnp.max(scores, axis=0, keepdims=True))
        return largest

    steps = tokens // chunk // together
    lanes = width
    largest = lax.fori_loop(0, steps, score_chunk, jnp.full((1, lanes), masked_score, f32))

    def value_chunk(step, carry):
        total, context = carry
        for within in range(together):
            rows = pl.ds(pl.multiple_of((step * together + within) * chunk, chunk), chunk)
            weights = jnp.exp(score_scratch[rows, :] - largest)
            total = total + jnp.sum(weights, axis=0, keepdims=True)
            context = context + dot_tn(weights.astype(bf16), v_ref[rows, :])
        return total, context

    total, context = lax.fori_loop(
        0, steps, value_chunk, (jnp.zeros((1, lanes), f32), jnp.zeros((lanes, lanes), f32))
    )
    context = context * jnp.transpose(jnp.broadcast_to(1.0 / total, (lanes, lanes)))
    put(block, context, largest, total)


def attend(plan, length, flip, q, k, v):
    query_names, key_names, bias_names, global_name = plan
    query_rows, lanes = q.shape
    tokens = k.shape[0]
    query_blocks = query_rows // BLOCK
    width = 128

    def lanes_of(rows):
        return pl.BlockSpec((rows, width), lambda step, *_: (0, step))

    return pl.pallas_call(
        partial(forward_kernel, unroll=query_blocks, query_blocks=query_blocks),
        grid_spec=pltpu.PrefetchScalarGridSpec(
            num_scalar_prefetch=5,
            grid=(lanes // width,),
            in_specs=[lanes_of(query_rows), lanes_of(tokens), lanes_of(tokens)],
            out_specs=[lanes_of(query_rows), lanes_of(query_blocks)],
            scratch_shapes=[
                pltpu.VMEM((tokens + BLOCK, 128), f32),
                pltpu.VMEM((tokens, width), f32),
            ],
        ),
        out_shape=[
            jax.ShapeDtypeStruct((query_rows, lanes), bf16),
            jax.ShapeDtypeStruct((query_blocks, lanes), f32),
        ],
        compiler_params=pltpu.CompilerParams(vmem_limit_bytes=60 << 20),
        cost_estimate=pl.CostEstimate(flops=10**9, bytes_accessed=10**6, transcendentals=10**5),
        name="attend_forward",
    )(key_names, bias_names, global_name, length, flip, q, k, v)


def backward_kernel(
    query_names, key_names, bias_names, lengths, flips,
    q_ref, k_ref, v_ref, back_ref, context_ref, logsum_ref,
    back_q_ref, back_k_ref, back_v_ref, bias_scratch, q_scratch, k_scratch, v_scratch, *, unroll, items,
):
    width = q_ref.shape[1]
    fill_length_bias(bias_scratch, lengths[0], flips[0])
    q_scratch[...] = jnp.zeros_like(q_scratch)
    k_scratch[...] = jnp.zeros_like(k_scratch)
    v_scratch[...] = jnp.zeros_like(v_scratch)
    ones = jnp.ones((16, width), bf16)

    def one(item):
        block = query_names[item]
        rows = block_rows(block)
        queries = spread_heads(q_ref[rows, :])
        back = back_ref[rows, :]
        backs = spread_heads(back)
        product = (back.astype(f32) * context_ref[rows, :].astype(f32)).astype(bf16)
        inner = dot_nt(ones, spread_heads(product))[0:1]
        logsum = logsum_ref[pl.ds(block, 1), :]
        names = [key_names[item, slot] for slot in range(SLOTS)]
        biases = [bias_names[item, slot] for slot in range(SLOTS)]
        keys = gather_blocks(k_ref, names)
        scores = dot_nt(keys, queries) + wide(gather_blocks(bias_scratch, biases), width)
        shares = jnp.exp(scores - logsum)
        back_shares = dot_nt(gather_blocks(v_ref, names), backs)
        back_values = dot_nn(shares.astype(bf16), backs)
        back_scores = (shares * (back_shares - inner)).astype(bf16)
        back_keys = dot_nn(back_scores, queries)
        q_scratch[rows, :] += join_heads(dot_tn(back_scores, keys))
        for slot in range(SLOTS):
            part = slice(slot * BLOCK, (slot + 1) * BLOCK)
            v_scratch[block_rows(names[slot]), :] += back_values[part]
            k_scratch[block_rows(names[slot]), :] += back_keys[part]

    def body(step, carry):
        for within in range(unroll):
            one(step * unroll + within)
        return carry

    lax.fori_loop(0, items // unroll, body, 0)
    back_q_ref[...] = (q_scratch[...] * HEAD_DIM ** (-0.5)).astype(bf16)
    back_k_ref[...] = k_scratch[...].astype(bf16)
    back_v_ref[...] = v_scratch[...].astype(bf16)


def attend_back(plan, length, flip, group, q, k, v, back, context, logsum):
    first, width = group
    query_names, key_names, bias_names, _ = plan
    query_rows = q.shape[0]
    tokens = k.shape[0]
    query_blocks = query_rows // BLOCK
    q_in, k_in = lanes_spec(query_rows, first, width), lanes_spec(tokens, first, width)
    q_out, k_out = lanes_spec(query_rows, 0, width), lanes_spec(tokens, 0, width)
    return pl.pallas_call(
        partial(backward_kernel, unroll=20, items=query_names.shape[0]),
        grid_spec=pltpu.PrefetchScalarGridSpec(
            num_scalar_prefetch=5,
            grid=(1,),
            in_specs=[q_in, k_in, k_in, q_in, q_in, lanes_spec(query_blocks, first, width)],
            out_specs=[q_out, k_out, k_out],
            scratch_shapes=[
                pltpu.VMEM((tokens + BLOCK, 128), f32),
                pltpu.VMEM((query_rows, width), f32),
                pltpu.VMEM((tokens, width), f32),
                pltpu.VMEM((tokens, width), f32),
            ],
        ),
        out_shape=[
            jax.ShapeDtypeStruct((query_rows, width), bf16),
            jax.ShapeDtypeStruct((tokens, width), bf16),
            jax.ShapeDtypeStruct((tokens, width), bf16),
        ],
        compiler_params=pltpu.CompilerParams(vmem_limit_bytes=60 << 20),
        cost_estimate=pl.CostEstimate(flops=10**9, bytes_accessed=10**6, transcendentals=10**5),
        name="attend_backward",
    )(query_names, key_names, bias_names, length, flip, q, k, v, back, context, logsum)


def project_kernel(core, x_ref, x_near_ref, w_q, w_k, w_v, b_q, b_v, q_ref, k_ref, v_ref):
    step = pl.program_id(0)

    def project(tile):
        q = (dot_nn(tile, w_q[...]) + b_q[...]).astype(bf16)
        q_ref[...] = q * jnp.asarray(HEAD_DIM ** (-0.5), bf16)
        k_ref[...] = dot_nn(tile, w_k[...]).astype(bf16)
        v_ref[...] = (dot_nn(tile, w_v[...]) + b_v[...]).astype(bf16)

    @pl.when(step < pl.num_programs(0) // 2)
    def _():
        project(x_ref[...])

    @pl.when(step >= pl.num_programs(0) // 2)
    def _():
        project(x_near_ref[...])


def project_far_kernel(core, x_ref, x_near_ref, w_k, w_v, b_v, k_old, v_old, k_ref, v_ref):
    step = pl.program_id(0)

    def project(tile):
        k_ref[...] = dot_nn(tile, w_k[...]).astype(bf16)
        v_ref[...] = (dot_nn(tile, w_v[...]) + b_v[...]).astype(bf16)

    @pl.when(step < pl.num_programs(0) // 2)
    def _():
        project(x_ref[...])

    @pl.when(step >= pl.num_programs(0) // 2)
    def _():
        project(x_near_ref[...])


TILE = 512


def piece_spec(piece, per, width, tile=TILE):
    return pl.BlockSpec((tile, width), lambda step, *_: (jnp.clip(step - piece * per, 0, per - 1), 0))


def own_weight(which):
    return pl.BlockSpec((D, D // 2), lambda step, core, *_: (0, 2 * which + core[0]))


def own_bias():
    return pl.BlockSpec((1, D // 2), lambda step, core, *_: (0, core[0]))


def project_chip(core, x, x_near, qkv_weight, query_bias, value_bias):
    rows = x.shape[0]
    half = D // 2
    per = rows // TILE
    out = pl.BlockSpec((TILE, half), lambda step, *_: (step, 0))
    return pl.pallas_call(
        project_kernel,
        grid_spec=pltpu.PrefetchScalarGridSpec(
            num_scalar_prefetch=1,
            grid=(2 * per,),
            in_specs=[piece_spec(0, per, D), piece_spec(1, per, D)]
            + [own_weight(0), own_weight(1), own_weight(2), own_bias(), own_bias()],
            out_specs=[out, out, out],
        ),
        out_shape=[
            jax.ShapeDtypeStruct((2 * rows, half), bf16),
            jax.ShapeDtypeStruct((4 * rows, half), bf16),
            jax.ShapeDtypeStruct((4 * rows, half), bf16),
        ],
        compiler_params=pltpu.CompilerParams(vmem_limit_bytes=60 << 20),
        cost_estimate=pl.CostEstimate(flops=4 * 10**9, bytes_accessed=10**7, transcendentals=0),
        name="project_chip",
    )(core, x, x_near, qkv_weight, qkv_weight, qkv_weight, query_bias, value_bias)


def project_far(core, x_far, x_far_near, qkv_weight, value_bias, k, v):
    rows = x_far.shape[0]
    half = D // 2
    per = rows // TILE
    out = pl.BlockSpec((TILE, half), lambda step, *_: (2 * per + step, 0))
    kept = pl.BlockSpec(memory_space=pl.ANY)
    return pl.pallas_call(
        project_far_kernel,
        grid_spec=pltpu.PrefetchScalarGridSpec(
            num_scalar_prefetch=1,
            grid=(2 * per,),
            in_specs=[piece_spec(0, per, D), piece_spec(1, per, D)]
            + [own_weight(1), own_weight(2), own_bias(), kept, kept],
            out_specs=[out, out],
        ),
        out_shape=[jax.ShapeDtypeStruct(k.shape, bf16), jax.ShapeDtypeStruct(v.shape, bf16)],
        input_output_aliases={6: 0, 7: 1},
        compiler_params=pltpu.CompilerParams(vmem_limit_bytes=60 << 20),
        cost_estimate=pl.CostEstimate(flops=3 * 10**9, bytes_accessed=10**7, transcendentals=0),
        name="project_far",
    )(core, x_far, x_far_near, qkv_weight, qkv_weight, value_bias, k, v)


def gelu_pair(x):
    t = 1.0 / (1.0 + (0.3275911 * 0.5**0.5) * jnp.abs(x))
    bell = jnp.exp(-0.5 * x * x)
    poly = 0.7107068705 + t * (-0.7265760135 + t * 0.5307027145)
    tail = t * (0.127414796 + t * (-0.142248368 + t * poly)) * bell
    cdf = jnp.where(x < 0, tail, 1.0 - tail)
    return x * cdf, cdf + x * bell * 0.3989422804014327


def norm_parts(value):
    center = value - jnp.mean(value, axis=-1, keepdims=True)
    spread = jnp.mean(center * center, axis=-1, keepdims=True)
    scale = lax.rsqrt(spread + norm_epsilon)
    return center * scale, scale


def norm_back(slope, normed, scale):
    along = jnp.mean(slope * normed, axis=-1, keepdims=True)
    return scale * (slope - jnp.mean(slope, axis=-1, keepdims=True) - normed * along)


def column_sum(value):
    return jnp.sum(value, axis=0, keepdims=True)


PIECES = 16
VECTOR_ROWS = 128


def row_spec(tile, width):
    return pl.BlockSpec((tile, width), lambda step, *_: (step, 0))


def stack_spec(count, tile, width):
    return pl.BlockSpec((count, tile, width), lambda step, *_: (0, step, 0))


def whole_spec(shape):
    return pl.BlockSpec(shape, lambda step, *_: (0,) * len(shape))


def middle_kernel(
    core,
    own_ref, other_ref, x_ref, cot_ref, vector_ref, expand_bias_ref, proj_hbm, expand_hbm, shrink_hbm,
    output_ref, back_one_ref, back_own_ref, back_other_ref, wide_keep, wide_send, lows_ref, sums_ref,
    proj_w, expand_w, shrink_w, slope_s, wide_s, weight_sems, wide_sems, *, chunk,
):
    step = pl.program_id(0)
    half = D // 2
    ff = expand_w.shape[1]
    chunks = ff // chunk
    hc = core[0]
    loads = [
        pltpu.make_async_copy(proj_hbm.at[pl.ds(hc * half, half)], proj_w.at[pl.ds(0, half)], weight_sems.at[0]),
        pltpu.make_async_copy(
            proj_hbm.at[pl.ds((1 - hc) * half, half)], proj_w.at[pl.ds(half, half)], weight_sems.at[1]
        ),
        pltpu.make_async_copy(expand_hbm, expand_w, weight_sems.at[2]),
        pltpu.make_async_copy(shrink_hbm, shrink_w, weight_sems.at[3]),
    ]

    @pl.when(step == 0)
    def _():
        for load in loads:
            load.start()
        sums_ref[...] = jnp.zeros_like(sums_ref)
        for load in loads:
            load.wait()

    def vector(row):
        return vector_ref[pl.ds(row, 1), :]

    slot = lax.rem(step, 2)
    tile = x_ref.shape[0]

    def wide_copies(slot, first_row):
        copies = []
        for which in range(2):
            for side, out in enumerate((wide_keep, wide_send)):
                first = pl.multiple_of((hc if side == 0 else 1 - hc) * (ff // 2), ff // 2)
                copies.append(
                    pltpu.make_async_copy(
                        wide_s.at[slot, which, :, pl.ds(first, ff // 2)],
                        out.at[which, pl.ds(pl.multiple_of(first_row, tile), tile)],
                        wide_sems.at[slot, 2 * which + side],
                    )
                )
        return copies

    @pl.when(step >= 2)
    def _():
        for copy in wide_copies(slot, 0):
            copy.wait()

    context = jnp.concatenate([own_ref[...], other_ref[...]], axis=1)
    resid = x_ref[...].astype(f32) + dot_nn(context, proj_w[...]) + vector(0)
    normed_one, scale_one = norm_parts(resid)
    hidden = normed_one * vector(1) + vector(2)
    low = hidden.astype(bf16)
    lows_ref[0] = low
    resid_two = hidden + vector(3)

    for part in range(chunks):
        cols = slice(part * chunk, (part + 1) * chunk)
        inner = dot_nn(low, expand_w[:, cols]) + expand_bias_ref[:, cols]
        active, slope = gelu_pair(inner)
        active = active.astype(bf16)
        wide_s[slot, 0, :, cols] = active
        slope_s[:, cols] = slope.astype(bf16)
        resid_two = resid_two + dot_nn(active, shrink_w[cols, :])
    normed_two, scale_two = norm_parts(resid_two)
    output_ref[...] = (normed_two * vector(4) + vector(5)).astype(bf16)
    cot = cot_ref[...].astype(f32)
    back_two = norm_back(vector(4) * cot, normed_two, scale_two)
    low_two = back_two.astype(bf16)
    lows_ref[1] = low_two
    sums_ref[3:4, :] += column_sum(low_two.astype(f32))
    sums_ref[4:5, :] += column_sum(cot * normed_two)
    sums_ref[5:6, :] += column_sum(cot)
    back = back_two
    for part in range(chunks):
        cols = slice(part * chunk, (part + 1) * chunk)
        back_inner = (dot_nt(low_two, shrink_w[cols, :]) * slope_s[:, cols].astype(f32)).astype(bf16)
        wide_s[slot, 1, :, cols] = back_inner
        sums_ref[8 + part : 9 + part, :] += column_sum(back_inner.astype(f32))
        back = back + dot_nt(back_inner, expand_w[:, cols])
    sums_ref[1:2, :] += column_sum(back * normed_one)
    sums_ref[2:3, :] += column_sum(back)
    back_one = norm_back(vector(1) * back, normed_one, scale_one)
    back_one_ref[...] = back_one
    low_one = back_one.astype(bf16)
    lows_ref[2] = low_one
    sums_ref[0:1, :] += column_sum(low_one.astype(f32))
    back_context = dot_nt(low_one, proj_w[...]).astype(bf16)
    back_own_ref[...] = back_context[:, :half]
    back_other_ref[...] = back_context[:, half:]
    for copy in wide_copies(slot, step * tile):
        copy.start()

    @pl.when(step == pl.num_programs(0) - 1)
    def _():
        for other in range(2):
            for copy in wide_copies(other, 0):
                copy.wait()


def middle(core, own, other, x, cot, vectors, expand_bias, proj_weight, expand_weight, shrink_weight):
    rows = x.shape[0]
    ff = expand_weight.shape[1]
    half = D // 2
    tile = 256
    kept = pl.BlockSpec(memory_space=pl.ANY)
    assert ff // D == 4
    return pl.pallas_call(
        partial(middle_kernel, chunk=D),
        grid_spec=pltpu.PrefetchScalarGridSpec(
            num_scalar_prefetch=1,
            grid=(rows // tile,),
            in_specs=[row_spec(tile, half)] * 2
            + [row_spec(tile, D)] * 2
            + [whole_spec(vectors.shape), whole_spec(expand_bias.shape), kept, kept, kept],
            out_specs=[row_spec(tile, D)] * 2
            + [row_spec(tile, half)] * 2
            + [kept] * 2
            + [stack_spec(3, tile, D), whole_spec((16, D))],
            scratch_shapes=[
                pltpu.VMEM((D, D), bf16),
                pltpu.VMEM((D, ff), bf16),
                pltpu.VMEM((ff, D), bf16),
                pltpu.VMEM((tile, ff), bf16),
                pltpu.VMEM((2, 2, tile, ff), bf16),
                pltpu.SemaphoreType.DMA((4,)),
                pltpu.SemaphoreType.DMA((2, 4)),
            ],
        ),
        out_shape=[
            jax.ShapeDtypeStruct((rows, D), bf16),
            jax.ShapeDtypeStruct((rows, D), f32),
            jax.ShapeDtypeStruct((rows, half), bf16),
            jax.ShapeDtypeStruct((rows, half), bf16),
            jax.ShapeDtypeStruct((2, rows, ff // 2), bf16),
            jax.ShapeDtypeStruct((2, rows, ff // 2), bf16),
            jax.ShapeDtypeStruct((3, rows, D), bf16),
            jax.ShapeDtypeStruct((16, D), f32),
        ],
        compiler_params=pltpu.CompilerParams(vmem_limit_bytes=60 << 20),
        cost_estimate=pl.CostEstimate(flops=10**9, bytes_accessed=10**7, transcendentals=10**6),
        name="middle",
    )(core, own, other, x, cot, vectors, expand_bias, proj_weight, expand_weight, shrink_weight)


def weights_kernel(
    places, wide_own, wide_other, lows_own, lows_other, context_ref, sums_own, sums_other, *refs
):
    packed = refs[:4]
    shrink_g, expand_g, proj_g = refs[4:]
    step = pl.program_id(0)
    half = D // 2

    @pl.when(step == 0)
    def _():
        shrink_g[...] = jnp.zeros_like(shrink_g)
        expand_g[...] = jnp.zeros_like(expand_g)
        proj_g[...] = jnp.zeros_like(proj_g)
        proj_g[half : half + 16, :] = sums_own[...] + sums_other[...]

    def add(wide, lows):
        shrink_g[...] += dot_tn(wide[0], lows[1])
        expand_g[...] += dot_tn(lows[0], wide[1])
        proj_g[:half, :] += dot_tn(context_ref[...], lows[2])

    @pl.when(step < pl.num_programs(0) // 2)
    def _():
        add(wide_own, lows_own)

    @pl.when(step >= pl.num_programs(0) // 2)
    def _():
        add(wide_other, lows_other)

    @pl.when(step == pl.num_programs(0) - 1)
    def _():
        rows = shrink_g.shape[0] // PIECES
        extra = proj_g.shape[0] // (2 * PIECES)
        wide = expand_g.shape[1] // D
        for piece in range(PIECES):
            place = piece % (PIECES // 2)
            first = piece ^ places[0]
            second = piece ^ places[1]
            out = packed[piece // (PIECES // 2)]
            out[place, :rows, :] = shrink_g[pl.ds(pl.multiple_of(first * rows, rows), rows), :].astype(bf16)
            out[place, rows:, :] = proj_g[pl.ds(pl.multiple_of(first * extra, extra), extra), :].astype(bf16)
            out = packed[2 + piece // (PIECES // 2)]
            down = pl.ds(pl.multiple_of((second // wide) * rows, rows), rows)
            across = pl.ds(pl.multiple_of(lax.rem(second, wide) * D, D), D)
            out[place, :rows, :] = expand_g[down, across].astype(bf16)
            part = pl.ds(pl.multiple_of((PIECES + second) * extra, extra), extra)
            out[place, rows:, :] = proj_g[part, :].astype(bf16)


def weight_grads(places, wide_own, wide_other, lows_own, lows_other, context, sums_own, sums_other):
    _, rows, wide = wide_own.shape
    half = D // 2
    per = rows // TILE
    piece_rows = wide // PIECES + (half + VECTOR_ROWS) // (2 * PIECES)

    def own(count, width):
        return pl.BlockSpec((count, TILE, width), lambda step, *_: (0, jnp.minimum(step, per - 1), 0))

    def other(count, width):
        return pl.BlockSpec((count, TILE, width), lambda step, *_: (0, jnp.maximum(step - per, 0), 0))

    packed_shape = (PIECES // 2, piece_rows, D)
    return pl.pallas_call(
        weights_kernel,
        grid_spec=pltpu.PrefetchScalarGridSpec(
            num_scalar_prefetch=1,
            grid=(2 * per,),
            in_specs=[own(2, wide), other(2, wide), own(3, D), other(3, D), row_spec(TILE, half)]
            + [whole_spec((16, D))] * 2,
            out_specs=[whole_spec(packed_shape)] * 4,
            scratch_shapes=[
                pltpu.VMEM((wide, D), f32),
                pltpu.VMEM((D, wide), f32),
                pltpu.VMEM((half + VECTOR_ROWS, D), f32),
            ],
        ),
        out_shape=[jax.ShapeDtypeStruct(packed_shape, bf16)] * 4,
        compiler_params=pltpu.CompilerParams(vmem_limit_bytes=60 << 20),
        cost_estimate=pl.CostEstimate(flops=10**9, bytes_accessed=10**7, transcendentals=0),
        name="weight_grads",
    )(places, wide_own, wide_other, lows_own, lows_other, context, sums_own, sums_other)


def quarters_spec(place, per):
    return pl.BlockSpec((TILE, D), lambda step, *_: (jnp.clip(step - place * per, 0, per - 1), 0))


def input_kernel(core, *refs, per):
    weights, arrays, outs = refs[:3], refs[3:-4], refs[-4:]
    pairs = len(arrays) // 3
    step = pl.program_id(0)

    def through(which):
        back = jnp.concatenate([ref[...] for ref in arrays[which * pairs : (which + 1) * pairs]], axis=1)
        return dot_nt(back, weights[which][...])

    for place in range(4):

        @pl.when((step >= place * per) & (step < (place + 1) * per))
        def _():
            total = through(1) + through(2)
            if place >= 2:
                total = total + through(0)
            outs[place][...] = total.astype(bf16)


def input_parts(core, qkv_weight, back_qs, back_ks, back_vs, rows):
    per = rows // TILE
    tokens = [
        pl.BlockSpec((TILE, array.shape[1]), lambda step, *_: (lax.rem(step + 2 * per, 4 * per), 0)) for array in back_ks
    ]
    queries = [
        pl.BlockSpec((TILE, array.shape[1]), lambda step, *_: (jnp.maximum(step - 2 * per, 0), 0)) for array in back_qs
    ]
    return pl.pallas_call(
        partial(input_kernel, per=per),
        grid_spec=pltpu.PrefetchScalarGridSpec(
            num_scalar_prefetch=1,
            grid=(4 * per,),
            in_specs=[own_weight(which) for which in range(3)] + queries + 2 * tokens,
            out_specs=[quarters_spec(place, per) for place in range(4)],
        ),
        out_shape=[jax.ShapeDtypeStruct((rows, D), bf16)] * 4,
        compiler_params=pltpu.CompilerParams(vmem_limit_bytes=60 << 20),
        cost_estimate=pl.CostEstimate(flops=10**9, bytes_accessed=10**7, transcendentals=0),
        name="input_parts",
    )(core, *[qkv_weight] * 3, *back_qs, *back_ks, *back_vs)


QKV_PIECES = 16
JOINED_TILE = 1024


def joined_kernel(places, core, *refs, tiles, pairs):
    x_refs = refs[:4]
    arrays = refs[4 : 4 + 3 * pairs]
    packed = refs[4 + 3 * pairs : 8 + 3 * pairs]
    total, sums = refs[8 + 3 * pairs :]
    step = pl.program_id(0)
    half = D // 2
    per = tiles // 4

    @pl.when(step == 0)
    def _():
        total[...] = jnp.zeros_like(total)
        sums[...] = jnp.zeros_like(sums)

    def joined(first, last):
        return jnp.concatenate([ref[...] for ref in arrays[first * pairs : last * pairs]], axis=1)

    for piece in range(4):

        @pl.when((step >= piece * per) & (step < (piece + 1) * per))
        def _():
            first = 0 if piece < 2 else 1
            back = joined(first, 3)
            total[:, first * half : 3 * half] += dot_tn(x_refs[piece][...], back)
            sums[0:1, first * half :] += column_sum(back.astype(f32))

    @pl.when(step == tiles - 1)
    def _():
        rows = D // QKV_PIECES
        q_sums = jnp.transpose(jnp.broadcast_to(sums[0:1, :half], (128, half)))
        v_sums = jnp.transpose(jnp.broadcast_to(sums[0:1, 2 * half :], (128, half)))
        total[:half, 3 * half :] = q_sums
        total[half:, 3 * half :] = v_sums
        width = packed[0].shape[2]
        for color in range(2):
            cols = slice(color * width, (color + 1) * width)
            for piece in range(QKV_PIECES):
                part = pl.ds(pl.multiple_of((piece ^ places[color]) * rows, rows), rows)
                out = packed[2 * color + piece // (QKV_PIECES // 2)]
                out[piece % (QKV_PIECES // 2)] = total[part, cols].astype(bf16)


def joined_grads(places, core, xs, back_qs, back_ks, back_vs):
    rows = xs[0].shape[0]
    pairs = len(back_qs)
    per = rows // JOINED_TILE
    tiles = 4 * per
    width = D // 2 + 256
    tokens = [row_spec(JOINED_TILE, array.shape[1]) for array in back_ks]
    queries = [
        pl.BlockSpec((JOINED_TILE, array.shape[1]), lambda step, *_: (jnp.minimum(step, 2 * per - 1), 0)) for array in back_qs
    ]
    packed = pl.BlockSpec((QKV_PIECES // 2, D // QKV_PIECES, width), lambda step, *_: (0, 0, 0))
    packed_shape = jax.ShapeDtypeStruct((QKV_PIECES // 2, D // QKV_PIECES, width), bf16)
    return pl.pallas_call(
        partial(joined_kernel, tiles=tiles, pairs=pairs),
        grid_spec=pltpu.PrefetchScalarGridSpec(
            num_scalar_prefetch=2,
            grid=(tiles,),
            in_specs=[piece_spec(piece, per, D, JOINED_TILE) for piece in range(4)] + queries + 2 * tokens,
            out_specs=[packed] * 4,
            scratch_shapes=[pltpu.VMEM((D, 2 * width), f32), pltpu.VMEM((8, 3 * D // 2), f32)],
        ),
        out_shape=[packed_shape] * 4,
        compiler_params=pltpu.CompilerParams(vmem_limit_bytes=60 << 20),
        cost_estimate=pl.CostEstimate(flops=10**9, bytes_accessed=10**7, transcendentals=0),
        name="joined_grads",
    )(places, core, *xs, *back_qs, *back_ks, *back_vs)


def input_near_kernel(core, *refs):
    w_q, w_k, w_v, out = refs[0], refs[1], refs[2], refs[-1]
    arrays = refs[3:-1]
    pairs = len(arrays) // 3

    def joined(which):
        return jnp.concatenate([ref[...] for ref in arrays[which * pairs : (which + 1) * pairs]], axis=1)

    out[...] = (dot_nt(joined(0), w_q[...]) + dot_nt(joined(1), w_k[...]) + dot_nt(joined(2), w_v[...])).astype(bf16)


def input_near(core, qkv_weight, back_qs, back_ks, back_vs):
    rows = back_qs[0].shape[0]
    token = pl.BlockSpec((JOINED_TILE, 128), lambda step, *_: (step, 0))
    arrays = list(back_qs) + list(back_ks) + list(back_vs)
    return pl.pallas_call(
        input_near_kernel,
        grid_spec=pltpu.PrefetchScalarGridSpec(
            num_scalar_prefetch=1,
            grid=(rows // JOINED_TILE,),
            in_specs=[own_weight(0), own_weight(1), own_weight(2)] + [token] * len(arrays),
            out_specs=pl.BlockSpec((JOINED_TILE, D), lambda step, *_: (step, 0)),
        ),
        out_shape=jax.ShapeDtypeStruct((rows, D), bf16),
        compiler_params=pltpu.CompilerParams(vmem_limit_bytes=60 << 20),
        cost_estimate=pl.CostEstimate(flops=10**9, bytes_accessed=10**7, transcendentals=0),
        name="input_near",
    )(core, qkv_weight, qkv_weight, qkv_weight, *arrays)


GROUP = 8


def unpack_kernel(numbers, *refs, parts, outs, held):
    sources = refs[:4]
    targets = refs[4 + held : 4 + held + outs]
    stages = refs[4 + held + outs : -1]
    sems = refs[-1]
    step = pl.program_id(0)

    def copy(color, which, slot, number, elsewhere=False):
        part = parts[color][which]
        out, place = part["instead"][1:] if elsewhere else (part["out"], part["place"])
        row, col = place(number)
        rows, cols = part["rows"][1] - part["rows"][0], part["cols"][1] - part["cols"][0]
        target = targets[out].at[pl.ds(pl.multiple_of(row, rows), rows), pl.ds(pl.multiple_of(col, 128), cols)]
        at = part["at"]
        source = stages[color].at[slot, pl.ds(at[0], rows), pl.ds(at[1], cols)]
        return pltpu.make_async_copy(source, target, sems.at[color, which, slot])

    for place, source in enumerate(sources):
        color, side = place // 2, place % 2

        @pl.when(step == place)
        def _():
            for within in range(GROUP):
                slot = side * GROUP + within
                number = numbers[place * GROUP + within]
                stages[color][slot] = source[within].astype(f32)
                for which, part in enumerate(parts[color]):
                    if part["instead"] is None:
                        copy(color, which, slot, number).start()
                        continue
                    elsewhere = part["instead"][0](number)

                    @pl.when(elsewhere)
                    def _():
                        copy(color, which, slot, number, True).start()

                    @pl.when(jnp.logical_not(elsewhere))
                    def _():
                        copy(color, which, slot, number).start()

    @pl.when(step == pl.num_programs(0) - 1)
    def _():
        for color in range(2):
            for slot in range(2 * GROUP):
                for which in range(len(parts[color])):
                    copy(color, which, slot, 0).wait()


def unpack(numbers, sources, parts, out_shapes, held, name):
    count, rows, width = sources[0].shape
    assert count == GROUP and len(sources) == 4
    most = max(len(part) for part in parts)
    kept = pl.BlockSpec(memory_space=pl.ANY)
    return pl.pallas_call(
        partial(unpack_kernel, parts=parts, outs=len(out_shapes), held=len(held)),
        grid_spec=pltpu.PrefetchScalarGridSpec(
            num_scalar_prefetch=1,
            grid=(len(sources),),
            in_specs=[pl.BlockSpec((GROUP, rows, width), lambda step, *_: (0, 0, 0))] * len(sources) + [kept] * len(held),
            out_specs=[kept] * len(out_shapes),
            scratch_shapes=[pltpu.VMEM((2 * GROUP, rows, width), f32)] * 2
            + [pltpu.SemaphoreType.DMA((2, most, 2 * GROUP))],
        ),
        out_shape=[jax.ShapeDtypeStruct(shape, f32) for shape in out_shapes],
        input_output_aliases={1 + len(sources) + place: place for place in range(len(held))},
        compiler_params=pltpu.CompilerParams(vmem_limit_bytes=60 << 20),
        cost_estimate=pl.CostEstimate(flops=10**6, bytes_accessed=10**6, transcendentals=0),
        name=name,
    )(numbers, *sources, *held)


def part_of(rows, cols, out, place, instead=None):
    return {"rows": rows, "cols": cols, "at": (rows[0], cols[0]), "out": out, "place": place, "instead": instead}


def swap(value, axis, bit=1):
    size = lax.axis_size(axis)
    return lax.ppermute(value, axis, [(place, place ^ bit) for place in range(size)])


def place_of(order):
    number = jnp.zeros((), jnp.int32)
    for axis, bit in order:
        number = 2 * number + ((lax.axis_index(axis) & bit) // bit).astype(jnp.int32)
    return number


def add_low(left, right):
    return (left.astype(f32) + right.astype(f32)).astype(bf16)


class Chain:
    def __init__(self, scatter_order, gather_order, keep, first):
        self.orders = list(scatter_order) + list(gather_order)
        self.steps = len(scatter_order)
        self.keep, self.first, self.arrived = keep, first, None
        self.at = 0
        self.gathered = None
        self.other_gathered = None
        self.other_arrived = None

    def left(self):
        return len(self.orders) + 1 - self.at

    def send(self):
        if self.at < self.steps:
            if self.at == 0:
                return self.first
            half = self.keep.shape[0] // 2
            high = add_low(self.keep[half:], self.arrived[half:])
            self.keep = add_low(self.keep[:half], self.arrived[:half])
            return high
        if self.at == self.steps:
            total = add_low(self.keep, self.arrived)
            bit = 8
            while bit < lax.axis_size("dp"):
                total = add_low(total, swap(total, "dp", bit))
                bit *= 2
            self.gathered = total
        elif self.at < len(self.orders):
            self.gathered = jnp.concatenate([self.gathered, self.arrived], axis=0)
        else:
            return self.arrived
        return self.gathered

    def move(self, value):
        if self.at == len(self.orders):
            self.arrived, self.other_arrived = value, swap(value, "hc")
            self.at += 1
            return
        if self.at >= self.steps:
            self.gathered = value
        axis, bit = self.orders[self.at]
        self.arrived = swap(value, axis, bit)
        self.at += 1
        if self.at == len(self.orders):
            self.other_gathered = swap(value, "hc")


def gathered_numbers(number, scatter_order, gather_order):
    count = 1 << len(scatter_order)
    places = jnp.arange(count, dtype=jnp.int32)
    turned = jnp.zeros((count,), jnp.int32)
    for at, name in enumerate(gather_order):
        turned = turned + (((places >> at) & 1) << (len(scatter_order) - 1 - scatter_order.index(name)))
    return turned ^ number


def ready(*values):
    return lax.optimization_barrier(values)


def per_device(
    inputs, doc_lengths, random_blocks, qkv_weight, query_bias, value_bias, proj_weight, proj_bias,
    first_gain, first_shift, expand_weight, expand_bias, shrink_weight, shrink_bias,
    second_gain, second_shift, cotangent,
):
    hx = lax.axis_index("hx")
    hc = lax.axis_index("hc")
    docs, rows, _ = inputs.shape
    assert docs == 1 and lax.axis_size("hx") == 2 and lax.axis_size("hc") == 2
    half = D // 2
    ff = expand_weight.shape[1]
    x = inputs.reshape(rows, D)
    x_far = swap(x, "hx")
    x_near = swap(x, "hc")
    row_blocks = rows // BLOCK
    flip = (hx * 2 + hc).astype(jnp.int32) * row_blocks
    plan = block_plan(doc_lengths[0], random_blocks[0], flip, 2 * row_blocks)
    flip = flip.reshape(1)
    core = hc.astype(jnp.int32).reshape(1)
    chip_steps = {"x": ("hx", 1), "y": ("dp", 1), "n": ("dp", 2), "f": ("dp", 4)}
    orders = {
        name: tuple([chip_steps[step] for step in part] for part in text.split())
        for name, text in ORDERS.items()
    }

    def places_of(letter):
        return jnp.stack([place_of(orders[f"{letter}{color}"][0]) for color in range(2)])

    def numbers_of(letter, places):
        own = [gathered_numbers(places[color], *orders[f"{letter}{color}"]) for color in range(2)]
        parts = [slice(0, GROUP), slice(GROUP, 2 * GROUP)]
        return tuple(
            jnp.concatenate([own[color][part] + PIECES * side for color in range(2) for side in (core, 1 - core)])
            for part in parts
        )

    middle_places, joined_places = places_of("M"), places_of("Q")
    numbers = numbers_of("M", middle_places) + numbers_of("Q", joined_places)
    vectors = jnp.concatenate(
        [proj_bias, first_gain, first_shift, shrink_bias, second_gain, second_shift, query_bias, value_bias]
    ).reshape(8, D)
    vectors = vectors.astype(f32)
    bias_q, bias_v = vectors[6:7], vectors[7:8]
    expand_row = expand_bias.astype(f32).reshape(1, ff)

    q, k, v = project_chip(core, x, x_near, qkv_weight, bias_q, bias_v)
    x_far, q, expand_row, vectors, middle_places, joined_places, *rest = ready(
        x_far, q, expand_row, vectors, middle_places, joined_places, *numbers, *plan
    )
    numbers, plan = rest[:4], rest[4:]
    x_far_near = swap(x_far, "hc")
    k, v = project_far(core, x_far, x_far_near, qkv_weight, bias_v, k, v)
    context, logsum = attend(plan, doc_lengths, flip, q, k, v)
    other_context = swap(context[rows:], "hc")
    output, back_one, back_own, back_other, wide_keep, wide_send, lows, sums = middle(
        core, context, other_context, x, cotangent.reshape(rows, D), vectors,
        expand_row, proj_weight, expand_weight, shrink_weight,
    )
    from_other = swap(back_other, "hc")
    wide_send, lows_send, sums_send, from_other = ready(wide_send, lows, sums, from_other)
    back = jnp.concatenate([back_own, from_other], axis=0)
    wide_other, lows_other, sums_other = swap(wide_send, "hc"), swap(lows_send, "hc"), swap(sums_send, "hc")

    held = {"last": back}
    chains = {}

    def tie(value):
        value, held["last"] = ready(value, held["last"])
        return value

    def pairs_of(which):
        return [held["grads", pair][which] for pair in range(len(GROUPS))]

    rows_each, extra, wide_blocks = ff // 2 // PIECES, (D // 2 + VECTOR_ROWS) // (2 * PIECES), ff // 2 // D
    proj_pieces = half // extra

    def split(number):
        return number // PIECES, lax.rem(number, PIECES)

    def expand_place(number):
        side, piece = split(number)
        return piece // wide_blocks * rows_each, (side * wide_blocks + lax.rem(piece, wide_blocks)) * D

    def proj_place(color):
        def place(number):
            side, piece = split(number)
            return side * half + (color * PIECES + piece) * extra, number * 0

        return place

    def vector_place(number):
        side, piece = split(number)
        return (side * (2 * PIECES - proj_pieces) + PIECES + piece - proj_pieces) * extra, number * 0

    def joined_place(which, offset):
        def place(number):
            side, piece = split(number)
            return piece * (D // QKV_PIECES), which * D + side * half + offset

        return place

    def bias_place(number):
        side, piece = split(number)
        return (side * QKV_PIECES + piece) * (D // QKV_PIECES), number * 0

    each = D // QKV_PIECES
    middle_parts = [
        [
            part_of((0, rows_each), (0, D), 0, lambda n: (n * rows_each, n * 0)),
            part_of((rows_each, rows_each + extra), (0, D), 2, proj_place(0)),
        ],
        [
            part_of((0, rows_each), (0, D), 1, expand_place),
            part_of(
                (rows_each, rows_each + extra), (0, D), 2, proj_place(1),
                (lambda n: lax.rem(n, PIECES) >= proj_pieces - PIECES, 3, vector_place),
            ),
        ],
    ]
    joined_parts = [
        [
            part_of((0, each), (0, half), 0, joined_place(0, 0)),
            part_of((0, each), (half, half + 256), 0, joined_place(1, 0)),
        ],
        [
            part_of((0, each), (0, 128), 0, joined_place(1, 256)),
            part_of((0, each), (128, 128 + half), 0, joined_place(2, 0)),
            part_of((0, each), (128 + half, 256 + half), 1, bias_place),
        ],
    ]
    layouts = {
        "M": (middle_parts, [(ff, D), (D, ff), (D, D), (2 * VECTOR_ROWS, D)], numbers[:2]),
        "Q": (joined_parts, [(D, 3 * D), (2 * D, 128)], numbers[2:]),
    }

    def run(name):
        if name.startswith("attend"):
            pair = int(name[-1])
            held["grads", pair] = attend_back(
                plan, doc_lengths, flip, GROUPS[pair], q, k, v, tie(back), context, logsum
            )
            held["last"] = held["grads", pair][0]
        elif name == "weights":
            packed = weight_grads(
                middle_places, tie(wide_keep), wide_other, lows, lows_other, context, sums, sums_other
            )
            held["last"] = packed[0]
            for color in range(2):
                chains[f"M{color}"] = Chain(*orders[f"M{color}"], packed[2 * color], packed[2 * color + 1])
        elif name == "joined":
            back_qs = pairs_of(0)
            back_qs[0] = tie(back_qs[0])
            packed = joined_grads(
                joined_places, core, (x, x_near, x_far, x_far_near), back_qs, pairs_of(1), pairs_of(2)
            )
            held["last"] = packed[0]
            for color in range(2):
                chains[f"Q{color}"] = Chain(*orders[f"Q{color}"], packed[2 * color], packed[2 * color + 1])
        elif name == "inputs":
            back_ks = pairs_of(1)
            back_ks[0] = tie(back_ks[0])
            far, far_others, near, near_others = input_parts(core, qkv_weight, pairs_of(0), back_ks, pairs_of(2), rows)
            held["last"] = far
            held["far"] = far, swap(far_others, "hc")
            held["near"] = near, swap(near_others, "hc")
        elif name == "dx":
            value = tie(add_low(*held["far"]))
            held["last"] = value
            held["from_far"] = swap(value, "hx")
        elif name == "input":
            near, from_near = held["near"]
            near = tie(near)
            value = back_one + near.astype(f32) + from_near.astype(f32) + held["from_far"].astype(f32)
            held["last"] = held["input"] = value
        elif name.startswith("early") or name.startswith("late"):
            letter = name[-1]
            parts, shapes, places = layouts[letter]
            early = name.startswith("early")
            sides = ("gathered", "other_gathered") if early else ("arrived", "other_arrived")
            sources = [getattr(chains[f"{letter}{color}"], side) for color in range(2) for side in sides]
            sources[0] = tie(sources[0])
            held["out", letter] = unpack(
                places[0 if early else 1], sources, parts, shapes, () if early else held["out", letter],
                f"unpack_{letter}",
            )
            held["last"] = held["out", letter][0]
        else:
            chain = chains[name]
            value = tie(chain.send())
            chain.move(value)
            held["last"] = value

    for names in SEQUENCE:
        for name in names.split():
            run(name)
    assert all(chain.left() == 0 for chain in chains.values())
    grad_shrink, grad_expand, grad_proj, vector = held["out", "M"]
    grad_qkv, bias = held["out", "Q"]
    grad_query_bias = jnp.concatenate([bias[:half, 0], bias[D : D + half, 0]])
    grad_value_bias = jnp.concatenate([bias[half:D, 0], bias[D + half :, 0]])
    grad_expand_bias = vector[8 : 8 + ff // D].reshape(ff)
    return (
        output.reshape(docs, rows, D),
        held["input"].reshape(docs, rows, D),
        grad_qkv, grad_query_bias, grad_value_bias, grad_proj, vector[0], vector[1], vector[2],
        grad_expand, grad_expand_bias, grad_shrink, vector[3], vector[4], vector[5],
    )


ORDERS = {"M0": "xnyf fnxy", "M1": "nxfy fxyn", "Q0": "nyxf yfnx", "Q1": "yxnf fnyx"}
SEQUENCE = (
    "attend0 weights M1 M0",
    "attend1 inputs M1 M0",
    "dx joined M1 M0",
    "Q1 Q0 M0 M1",
    "Q0 Q1 M1 M0",
    "input Q0 Q1 M1",
    "Q0 Q1 M0 Q0",
    "M1 Q1 Q0 M0",
    "Q1 Q0 Q1 M1",
    "Q0 M0 Q1 earlyQ",
    "earlyM Q1 Q0 lateQ",
    "M1 M0 lateM",
)


def solution(mesh):
    dp = mesh.shape["dp"]
    heads = mesh.shape["heads"]
    split = Mesh(mesh.devices.reshape(dp, heads // 2, 2), ("dp", "hx", "hc"))
    rows = P("dp", ("hx", "hc"), None)
    in_specs = (rows, P("dp"), P("dp", None, None)) + (P(),) * 13 + (rows,)
    out_specs = (rows, rows) + (P(),) * 13
    return jax.shard_map(
        per_device, mesh=split, in_specs=in_specs, out_specs=out_specs, check_vma=False
    )
```
